32 devices in a mesh: span: 16 (over z, y, x), width: 2 (over core).
Axes of the slice: x: 2, y: 2, z: 4, core: 2. Of those that a mesh axis runs over, the one named last changes fastest.
Arguments:
- state: float32 [4, 128, 64, 128], P(None, 'span', 'width'), may hold values from 0.2 to 2
- source: float32 [4, 128, 64, 128], P(None, 'span', 'width'), may hold values from -6 to 8
- conductance: float32 [128, 64, 128], P('span', 'width'), may hold values from 0.5 to 2
- rebar_cover: int32 [128, 64, 128], P('span', 'width'), may hold values 0 or 1
- colour: int32 [16, 2], P('span', 'width'), may hold values from 0 to 1
- diffusivity: float32 [4], replicated, may hold values from 0.5 to 2
- binding: float32 [4], replicated, may hold values from 0.1 to 1
Outputs:
- updated: float32 [4, 128, 64, 128], P(None, 'span', 'width')
- residual: float32 [4, 128, 64, 128], P(None, 'span', 'width')
The draws below stay inside these ranges and needn't reach their ends.
All inputs are finite; a program needn't handle non-finite values. No bound on the sum of `rebar_cover` on one device may be relied on, other than what follows from the above.
Results may differ from the reference program's by a relative error of at most 0.002.
Values sent between devices are 32-bit elements; how exact they have to be, the bound alone decides.
A program may use at most 64 MiB of HBM per device.

```python
import math
import jax
import jax.numpy as jnp
from jax import lax

IONS = 4
COARSEN = 8
SWEEPS = 4
COARSE_ITERS = 20
CX = 8
CY = 32
NX = 128
NY = 64
NZ = 128
N_SPAN = 16
N_WIDTH = 2


def draw_source(key, part):
    key_noise = jax.random.fold_in(key, 11)
    key_amp = jax.random.fold_in(key, 12)
    key_phase = jax.random.fold_in(key, 13)
    xs = jnp.arange(NX, dtype=jnp.float32)[None, :, None, None] / NX
    zs = jnp.arange(NZ, dtype=jnp.float32)[None, None, None, :] / NZ
    phase = jax.random.uniform(key_phase, (IONS, 1, 1, 1), jnp.float32, 0.0, 6.2831853)
    profile = 1.0 + 0.5 * jnp.sin(6.2831853 * xs + phase) * jnp.cos(3.1415927 * zs)
    amp = jax.random.uniform(key_amp, (IONS, 1, 1, 1), jnp.float32, 0.6, 1.4)
    noise = jax.random.normal(key_noise, (IONS, NX, NY, NZ), jnp.float32)
    return jnp.clip(amp * profile + noise, -6.0, 8.0)


def set_ends(entries, own_key, smallest, top_value):
    shape = entries.shape
    index_at = [jax.random.randint(jax.random.fold_in(own_key, axis), (), 0, shape[axis]) for axis in range(len(shape))]
    entries = entries.at[tuple(index_at)].set(smallest)
    longest = shape.index(max(shape))
    index_at[longest] = (index_at[longest] + 1) % shape[longest]
    return entries.at[tuple(index_at)].set(top_value)


def level_of(stream_key, extent, pieces, least, largest):
    factor_of, own = 1.0, jax.random.fold_in(stream_key, 6)
    for axis_at, blocks in pieces:
        steps = jnp.exp(jax.random.uniform(jax.random.fold_in(own, axis_at), (blocks,), jnp.float32, least / len(pieces), largest / len(pieces)))
        factor_of = factor_of * jnp.repeat(steps, extent[axis_at] // blocks).reshape([-1 if axis == axis_at else 1 for axis in range(len(extent))])
    return factor_of


def setup_inputs(seed: int = 0) -> dict:
    arg_keys = jax.random.split(jax.random.key(seed), 8)
    return {
        "state": jnp.clip(0.2 + 1.8 * jax.random.uniform(arg_keys[0], (IONS, NX, NY, NZ), jnp.float32) ** level_of(arg_keys[0], (IONS, NX, NY, NZ), ((1, 16), (2, 2)), -0.2, 0.2), 0.2, 2.0),
        "source": draw_source(jax.random.fold_in(arg_keys[7], 71), 0),
        "conductance": jnp.clip(jnp.exp(math.log(2.0) - 1.3862944 * jax.random.uniform(arg_keys[2], (NX, NY, NZ), jnp.float32) ** level_of(arg_keys[2], (NX, NY, NZ), ((0, 16), (1, 2)), -0.2, 0.2)), 0.5, 2.0),
        "rebar_cover": set_ends((jax.random.randint(arg_keys[3], (NX, NY, NZ), 0, 2) < 1).astype(jnp.int32), jax.random.fold_in(arg_keys[3], 1), 0, 1),
        "colour": set_ends(jax.random.randint(arg_keys[4], (N_SPAN, N_WIDTH), 0, 2), jax.random.fold_in(arg_keys[4], 1), 0, 1).astype(jnp.int32),
        "diffusivity": jnp.clip(jnp.exp(jax.random.uniform(arg_keys[5], (IONS,), jnp.float32, math.log(0.5), math.log(2.0))), 0.5, 2.0),
        "binding": jnp.clip(jnp.exp(jax.random.uniform(arg_keys[6], (IONS,), jnp.float32, math.log(0.1), math.log(1.0))), 0.1, 1.0),
    }


INV_STEP = 0.05
EPSILON = 1e-6


def later(value, axis):
    size = value.shape[axis]
    padded = jnp.pad(value, [(0, 1) if k == axis else (0, 0) for k in range(value.ndim)])
    return lax.slice_in_dim(padded, 1, size + 1, axis=axis)


def earlier(value, axis):
    size = value.shape[axis]
    padded = jnp.pad(value, [(1, 0) if k == axis else (0, 0) for k in range(value.ndim)])
    return lax.slice_in_dim(padded, 0, size, axis=axis)


def plain_sum(value):
    total = later(value, 0) + earlier(value, 0)
    total = total + later(value, 1)
    total = total + earlier(value, 1)
    total = total + later(value, 2)
    total = total + earlier(value, 2)
    return total


def split_sum(current, frozen, upper_x, lower_x, upper_y, lower_y):
    total = jnp.where(upper_x, later(frozen, 0), later(current, 0)) + jnp.where(lower_x, earlier(frozen, 0), earlier(current, 0))
    total = total + jnp.where(upper_y, later(frozen, 1), later(current, 1))
    total = total + jnp.where(lower_y, earlier(frozen, 1), earlier(current, 1))
    total = total + later(current, 2)
    total = total + earlier(current, 2)
    return total


def block_sum(value):
    n_one, n_two, n_three = value.shape
    shaped = value.reshape(n_one // COARSEN, COARSEN, n_two // COARSEN, COARSEN, n_three // COARSEN, COARSEN)
    return shaped.sum(axis=(1, 3, 5))


def reference(state, source, conductance, rebar_cover, colour, diffusivity, binding):
    xs = jnp.arange(NX, dtype=jnp.int32)
    ys = jnp.arange(NY, dtype=jnp.int32)
    zs = jnp.arange(NZ, dtype=jnp.int32)
    upper_x = (xs % CX == CX - 1)[:, None, None]
    lower_x = (xs % CX == 0)[:, None, None]
    upper_y = (ys % CY == CY - 1)[None, :, None]
    lower_y = (ys % CY == 0)[None, :, None]
    parity = (xs[:, None, None] + ys[None, :, None] + zs[None, None, :]) % 2
    owner = jnp.repeat(jnp.repeat(colour, CX, axis=0), CY, axis=1)[:, :, None]
    cover = rebar_cover.astype(jnp.float32)
    cond_sum = block_sum(conductance)

    def one_ion(items):
        conc, supply, spread, strength = items
        coef = spread * conductance
        bound_term = cover * strength * conc / (1.0 + conc)
        mass = INV_STEP + cover * strength / ((1.0 + conc) * (1.0 + conc))
        diag = mass + 6.0 * coef
        rhs = supply - (coef * (6.0 * conc - plain_sum(conc)) + bound_term)
        delta = jnp.zeros_like(conc)
        for phase in range(2):
            frozen = delta
            active = owner == phase
            for sweep in range(SWEEPS):
                for side in range(2):
                    total = split_sum(delta, frozen, upper_x, lower_x, upper_y, lower_y)
                    fresh = (rhs + coef * total) / diag
                    delta = jnp.where(active & (parity == side), fresh, delta)
        fine = rhs - (diag * delta - coef * plain_sum(delta))
        coarse_rhs = block_sum(fine)
        coarse_off = spread * cond_sum / COARSEN
        coarse_diag = block_sum(mass) + 6.0 * coarse_off

        def jacobi(step, value):
            return (coarse_rhs + coarse_off * plain_sum(value)) / coarse_diag

        coarse = lax.fori_loop(0, COARSE_ITERS, jacobi, jnp.zeros_like(coarse_rhs))
        lift = jnp.repeat(jnp.repeat(jnp.repeat(coarse, COARSEN, axis=0), COARSEN, axis=1), COARSEN, axis=2)
        image = diag * lift - coef * plain_sum(lift)
        weight = jnp.sum(fine * image) / (jnp.sum(image * image) + EPSILON)
        delta = delta + weight * lift
        final = rhs - (diag * delta - coef * plain_sum(delta))
        return conc + delta, final

    updated, residual = lax.map(one_ion, (state, source, diffusivity, binding))
    return updated, residual
```

```python
import functools

import jax
import jax.numpy as jnp
from jax import lax
from jax.experimental import pallas as pl
from jax.experimental.pallas import tpu as pltpu
from jax.sharding import PartitionSpec as P

COARSEN = 8
SWEEPS = 4
COARSE_ITERS = 20
INV_STEP = 0.05
EPSILON = 1e-06
MESH = pl.DeviceIdType.MESH
GROUPS = 2
UNROLL = 2
F32 = jnp.float32


def kernel(
    n_span, n_width, ions, cx, cy, cz,
    state_hbm, source_hbm, cond_hbm, cover_hbm, colour_ref, spread_ref, strength_ref,
    up_ref, res_ref,
    state_ref, source_ref, cond_ref, cover_ref, xs, xh, ys, yh, ysc, xhc, yhc, ops, gath, part, condp, coverp, rhs, diag, c, a, d, image,
    mx, fx, py, aj, cj, ej, sp, wv,
    send_sem, recv_sem, csend, crecv, osend, orecv, gsend, grecv, psend, precv, in_sem, met,
):
    s = lax.axis_index("span")
    w = lax.axis_index("width")
    kp = cx // 2
    rows = cy // COARSEN
    row = lax.broadcasted_iota(jnp.int32, (cy, cz), 0)
    lane = lax.broadcasted_iota(jnp.int32, (cy, cz), 1)
    p = (row + lane) % 2 == 1
    first_y, last_y = row == 0, row == cy - 1
    first_z, last_z = lane == 0, lane == cz - 1

    loads = [
        pltpu.make_async_copy(src, dst, in_sem.at[k])
        for k, (src, dst) in enumerate((
            (state_hbm, state_ref), (cond_hbm, cond_ref),
            (cover_hbm, cover_ref), (source_hbm, source_ref)))
    ]
    for load in loads:
        load.start()

    barrier = pltpu.get_barrier_semaphore()

    has = (s < n_span - 1, s > 0, w < n_width - 1, w > 0)
    gets = (s > 0, s < n_span - 1, w > 0, w < n_width - 1)
    to = ((s + 1, w), (s - 1, w), (s, w + 1), (s, w - 1))

    def flip(v, bit):
        return v + bit - 2 * bit * (v // bit % 2)

    quad = 4
    high = [1 << k for k in range(2, (n_span - 1).bit_length())]
    partners = [lax.rem(w + k, n_width) for k in range(1, n_width)]
    quads = [s - s % quad + (s + k) % quad for k in range(1, quad)]
    greet = [(s, v) for v in partners] + [(t, w) for t in quads] + [(flip(s, b), w) for b in high]
    up_far = (s % quad == quad - 1) & (s < n_span - 1)
    down_far = (s % quad == 0) & (s > 0)
    rounds = [
        [(s, v) for v in partners] + [(t, w) for t in quads],
        [(flip(s, high[0]), w)] + [(flip(s, b), v) for b in high[:2] for v in partners],
    ] + [[(flip(s, b), w)] for b in high[2:]]
    for other in greet:
        pl.semaphore_signal(barrier, inc=1, device_id=other, device_id_type=MESH)
    for ok, other in ((up_far, (s + 1, w)), (down_far, (s - 1, w))):
        @pl.when(ok)
        def _():
            pl.semaphore_signal(barrier, inc=1, device_id=other, device_id_type=MESH)
    greeted = len(greet) + up_far.astype(jnp.int32) + down_far.astype(jnp.int32)

    def meet(k):
        for other in rounds[k]:
            pl.semaphore_signal(met.at[k], inc=1, device_id=other, device_id_type=MESH)

    def met_by(k):
        pl.semaphore_wait(met.at[k], len(rounds[k]))

    everyone = n_span * n_width
    me = s * n_width + w

    def to_all(buf, ssem, rsem):
        @pl.loop(1, everyone)
        def _(off):
            other = lax.rem(me + off, everyone)
            pltpu.make_async_remote_copy(
                src_ref=buf.at[me], dst_ref=buf.at[me], send_sem=ssem, recv_sem=rsem,
                device_id=(other // n_width, other % n_width), device_id_type=MESH,
            ).start()

    def all_of(buf, sem):
        others = buf.at[pl.ds(0, everyone - 1)]
        pltpu.make_async_copy(others, others, sem).wait()

    def split(x):
        pairs = x.reshape(kp, 2, cy, cz)
        even, odd = pairs[:, 0], pairs[:, 1]
        return jnp.where(p, odd, even), jnp.where(p, even, odd)

    def yz_sum(v):
        out = jnp.where(last_y, 0.0, pltpu.roll(v, cy - 1, v.ndim - 2))
        out += jnp.where(first_y, 0.0, pltpu.roll(v, 1, v.ndim - 2))
        out += jnp.where(last_z, 0.0, pltpu.roll(v, cz - 1, v.ndim - 1))
        out += jnp.where(first_z, 0.0, pltpu.roll(v, 1, v.ndim - 1))
        return out

    zero_face = jnp.zeros((1, cy, cz), F32)

    def nb_red(black):
        above = jnp.concatenate([black[1:], zero_face], axis=0)
        below = jnp.concatenate([zero_face, black[:-1]], axis=0)
        return black + jnp.where(p, above, below) + yz_sum(black)

    def nb_black(red):
        above = jnp.concatenate([red[1:], zero_face], axis=0)
        below = jnp.concatenate([zero_face, red[:-1]], axis=0)
        return red + jnp.where(p, below, above) + yz_sum(red)

    def rim(e, i):
        lo, hi = xh[e, 0, i], xh[e, 1, i]
        ylo, yhi = yh[e, 0, i], yh[e, 1, i]
        mid = jnp.zeros((kp - 2, cy, cz), F32)

        def faces(k0, k1, half):
            x_part = jnp.concatenate([k0[None], mid, k1[None]], axis=0)
            low = ylo[half * kp:(half + 1) * kp][:, None, :]
            high = yhi[half * kp:(half + 1) * kp][:, None, :]
            return x_part + jnp.where(first_y, low, 0.0) + jnp.where(last_y, high, 0.0)

        red = faces(jnp.where(p, 0.0, lo), jnp.where(p, hi, 0.0), 1)
        black = faces(jnp.where(p, lo, 0.0), jnp.where(p, 0.0, hi), 0)
        return red, black

    def put_y(e, i, red, black):
        ys[e, 0, i] = jnp.concatenate([red[:, cy - 1, :], black[:, cy - 1, :]], axis=0)
        ys[e, 1, i] = jnp.concatenate([red[:, 0, :], black[:, 0, :]], axis=0)

    def put_x(e, i, red, black):
        xs[e - 1, 0, i] = jnp.where(p, red[kp - 1], black[kp - 1])
        xs[e - 1, 1, i] = jnp.where(p, black[0], red[0])

    pair_of = ions // GROUPS

    def copy(e, k, g):
        own = pl.ds(g * pair_of, pair_of)
        if k >= 2:
            src, dst = ys.at[e, k - 2, own], yh.at[e, k - 2, own]
        else:
            dst = xh.at[e, k, own]
            if e == 0:
                src = state_ref.at[own, cx - 1] if k == 0 else state_ref.at[own, 0]
            else:
                src = xs.at[e - 1, k, own]
        return pltpu.make_async_remote_copy(
            src_ref=src, dst_ref=dst, send_sem=send_sem.at[e, k, g], recv_sem=recv_sem.at[e, k, g],
            device_id=to[k], device_id_type=MESH,
        )

    def cond_copy(k):
        if k >= 2:
            src, dst = ysc.at[k - 2], yhc.at[k - 2]
        else:
            src, dst = cond_ref.at[cx - 1 if k == 0 else 0], xhc.at[k]
        return pltpu.make_async_remote_copy(
            src_ref=src, dst_ref=dst, send_sem=csend.at[k], recv_sem=crecv.at[k],
            device_id=to[k], device_id_type=MESH,
        )

    def send(e, g):
        for k in range(4):
            @pl.when(has[k])
            def _():
                copy(e, k, g).start()

    def receive(e, g):
        for k in range(4):
            @pl.when(gets[k])
            def _():
                copy(e, k, g).wait_recv()

    for k in range(4):
        @pl.when(jnp.logical_not(gets[k]))
        def _():
            for e in range(3):
                if k >= 2:
                    yh[e, k - 2] = jnp.zeros(yh.shape[2:], F32)
                else:
                    xh[e, k] = jnp.zeros(xh.shape[2:], F32)
            if k >= 2:
                yhc[k - 2] = jnp.zeros(yhc.shape[1:], F32)
            else:
                xhc[k] = jnp.zeros(xhc.shape[1:], F32)

    def pack_state(i, _):
        put_y(0, i, *split(state_ref[i]))
        return 0

    loads[0].wait()
    lax.fori_loop(0, ions, pack_state, 0)
    pl.semaphore_wait(barrier, greeted)
    for g in range(GROUPS):
        send(0, g)
    meet(0)

    loads[1].wait()
    condp[0], condp[1] = split(cond_ref[...])
    ysc[0] = jnp.concatenate([condp[0, :, cy - 1, :], condp[1, :, cy - 1, :]], axis=0)
    ysc[1] = jnp.concatenate([condp[0, :, 0, :], condp[1, :, 0, :]], axis=0)
    for k in range(4):
        @pl.when(has[k])
        def _():
            cond_copy(k).start()
    for load in loads[2:]:
        load.wait()
    coverp[0], coverp[1] = split(cover_ref[...].astype(F32))

    eighth = lane % COARSEN

    def pack(fields):
        step = 1
        while len(fields) > 1:
            low = lane[:1] // step % 2 == 0
            fields = [
                jnp.where(low, u + pltpu.roll(u, cz - step, 1), v + pltpu.roll(v, step, 1))
                for u, v in zip(fields[::2], fields[1::2])
            ]
            step *= 2
        v = fields[0]
        return jnp.concatenate(
            [jnp.sum(v[j * COARSEN:(j + 1) * COARSEN], axis=0, keepdims=True)
             for j in range(v.shape[0] // COARSEN)], axis=0)

    def local_terms(i, _):
        spread, strength = spread_ref[i], strength_ref[i]
        st = split(state_ref[i])
        src = split(source_ref[i])
        near = (nb_red(st[1]), nb_black(st[0]))
        mass_sum = jnp.zeros((cy, cz), F32)
        for h in range(2):
            coef = spread * condp[h]
            inv = 1.0 / (1.0 + st[h])
            bound = coverp[h] * strength * inv
            mass = INV_STEP + bound * inv
            dg = mass + 6.0 * coef
            diag[h, i] = dg
            c[h, i] = coef / dg
            rhs[h, i] = src[h] - (coef * (6.0 * st[h] - near[h]) + bound * st[h])
            mass_sum += jnp.sum(mass, axis=0)
        mx[i] = mass_sum
        return 0

    lax.fori_loop(0, ions, local_terms, 0)
    cond_sum = jnp.sum(cond_ref[...], axis=0)
    sums = pack([mx[i] for i in range(ions)] + [spread_ref[i] * cond_sum for i in range(ions)])
    low_slot = eighth[:rows] < ions
    coarse_off = pltpu.roll(sums, cz - ions, 1) / COARSEN
    coarse_inv = 1.0 / jnp.where(low_slot, sums + 6.0 * coarse_off, 1.0)
    ops[me] = jnp.where(low_slot, coarse_off * coarse_inv, pltpu.roll(coarse_inv, ions, 1))

    mine = colour_ref[0, 0].astype(F32)

    def sweeps(ar, ab, cr, cb):
        red = ar
        black = ab + cb * nb_black(red)
        for _ in range(SWEEPS - 1):
            red = ar + cr * nb_red(black)
            black = ab + cb * nb_black(red)
        return red, black

    def phase_zero(i, _):
        near = rim(0, i)
        for h in range(2):
            right = rhs[h, i] + spread_ref[i] * condp[h] * near[h]
            rhs[h, i] = right
            a[h, i] = right / diag[h, i]
        red, black = sweeps(
            (1.0 - mine) * a[0, i], (1.0 - mine) * a[1, i], c[0, i], c[1, i]
        )
        d[0, i], d[1, i] = red, black
        put_y(1, i, red, black)
        put_x(1, i, red, black)
        return 0

    for g in range(GROUPS):
        receive(0, g)
        lax.fori_loop(g * pair_of, (g + 1) * pair_of, phase_zero, 0, unroll=UNROLL)
        send(1, g)
    met_by(0)
    meet(1)
    for k in range(4):
        @pl.when(gets[k])
        def _():
            cond_copy(k).wait_recv()

    def phase_one(i, _):
        near = rim(1, i)
        red, black = sweeps(
            mine * (a[0, i] + c[0, i] * near[0]), mine * (a[1, i] + c[1, i] * near[1]),
            c[0, i], c[1, i],
        )
        red, black = red + d[0, i], black + d[1, i]
        d[0, i], d[1, i] = red, black
        put_y(2, i, red, black)
        put_x(2, i, red, black)
        near = (nb_red(black), nb_black(red))
        total = jnp.zeros((cy, cz), F32)
        for h, v in ((0, red), (1, black)):
            fine = rhs[h, i] - (diag[h, i] * v - spread_ref[i] * condp[h] * near[h])
            rhs[h, i] = fine
            total += jnp.sum(fine, axis=0)
        fx[0, i] = total
        fx[1, i] = spread_ref[i] * (xhc[1] * xs[1, 0, i])
        fx[2, i] = spread_ref[i] * (xhc[0] * xs[1, 1, i])
        for k in range(2):
            face = ys[2, k, i]
            other = jnp.concatenate([face[kp:], face[:kp]], axis=0)
            py[k, i] = spread_ref[i] * jnp.sum(yhc[1 - k] * other, axis=0, keepdims=True)
        return 0

    for g in range(GROUPS):
        receive(1, g)
        lax.fori_loop(g * pair_of, (g + 1) * pair_of, phase_one, 0, unroll=UNROLL)
        if g == GROUPS - 2:
            met_by(1)
            for k in range(2, len(rounds)):
                meet(k)
                met_by(k)
            to_all(ops, osend, orecv)

    def column(i):
        y_part = jnp.where(first_y, py[1, i], jnp.where(last_y, py[0, i], 0.0))
        return (jnp.concatenate([fx[0, i], fx[2, i]], axis=0),
                jnp.concatenate([fx[1, i], y_part], axis=0))

    columns = [column(i) for i in range(ions)]
    gath[me] = pack([u for u, _ in columns] + [v for _, v in columns])
    to_all(gath, gsend, grecv)
    for g in range(GROUPS):
        send(2, g)

    wide = n_width * rows
    half = n_span // 2
    all_of(ops, orecv)
    all_of(gath, grecv)

    crow = lax.broadcasted_iota(jnp.int32, (wide, cz), 0)
    slot_low = lax.broadcasted_iota(jnp.int32, (wide, cz), 1) % COARSEN < ions

    def wide_of(v):
        return jnp.concatenate([v[:, k] for k in range(n_width)], axis=1)

    def down(v):
        return pltpu.roll(v, cz - ions, 2)

    def up(v):
        return pltpu.roll(v, ions, 2)

    def fold(low_part, high_part):
        return jnp.where(slot_low, low_part, high_part)

    plane = jnp.zeros((1, wide, cz), F32)
    o = wide_of(ops[...].reshape(n_span, n_width, rows, cz))
    g = gath[...].reshape(n_span, n_width, 2 * rows, cz)
    plus, minus = wide_of(g[:, :, :rows]), wide_of(g[:, :, rows:])
    y_sum = jnp.where(crow % rows == 0, pltpu.roll(minus, 1, 1), 0.0)
    y_sum = jnp.where(crow % rows == rows - 1, pltpu.roll(minus, wide - 1, 1), y_sum)
    crhs = fold(plus[:half], up(plus[half:]))
    crhs += fold(jnp.concatenate([plane, down(plus[:half - 1])], axis=0), plus[half - 1:-1])
    crhs += fold(minus[1:half + 1], jnp.concatenate([up(minus[half + 1:]), plane], axis=0))
    crhs += fold(down(y_sum[:half]), y_sum[half:])
    aj[...] = crhs * fold(down(o[:half]), o[half:])
    cj[...] = fold(o[:half], up(o[half:]))
    crow = lax.broadcasted_iota(jnp.int32, (wide, cz), 0)
    clane = lax.broadcasted_iota(jnp.int32, (wide, cz), 1)

    def jacobi(_, e):
        above = jnp.where(slot_low, up_one(e[:1], -1), 0.0)
        below = jnp.where(slot_low, 0.0, up_one(e[half - 1:], 1))
        total = jnp.concatenate([e[1:], above], axis=0)
        total += jnp.concatenate([below, e[:-1]], axis=0)
        total += jnp.where(crow == wide - 1, 0.0, pltpu.roll(e, wide - 1, 1))
        total += jnp.where(crow == 0, 0.0, pltpu.roll(e, 1, 1))
        total += jnp.where(clane >= cz - COARSEN, 0.0, pltpu.roll(e, cz - COARSEN, 2))
        total += jnp.where(clane < COARSEN, 0.0, pltpu.roll(e, COARSEN, 2))
        return aj[...] + cj[...] * total

    def up_one(v, sign):
        return pltpu.roll(v, ions if sign > 0 else cz - ions, 2)

    e = lax.fori_loop(0, COARSE_ITERS - 1, jacobi, aj[...])
    ej[0] = plane[0]
    ej[n_span + 1] = plane[0]
    ej[1:half + 1] = e
    ej[half + 1:n_span + 1] = down(e)
    before, here, after = ej[s], ej[s + 1], ej[s + 2]

    def own_rows(v):
        out = v[:rows]
        for k in range(1, n_width):
            out = jnp.where(w == k, v[k * rows:(k + 1) * rows], out)
        return out

    y_low = jnp.zeros((1, cz), F32)
    y_high = jnp.zeros((1, cz), F32)
    for k in range(n_width):
        if k > 0:
            y_low = jnp.where(w == k, here[k * rows - 1:k * rows], y_low)
        if k < n_width - 1:
            y_high = jnp.where(w == k, here[(k + 1) * rows:(k + 1) * rows + 1], y_high)
    packed = jnp.concatenate(
        [own_rows(here), own_rows(before), own_rows(after), y_low, y_high,
         jnp.zeros((16 - 3 * rows - 2, cz), F32)], axis=0)
    for i in range(ions):
        v = jnp.where(eighth[:16] == i, packed, 0.0)
        if i:
            v = pltpu.roll(v, cz - i, 1)
        for step in (1, 2, 4):
            v = v + pltpu.roll(v, step, 1)
        sp[i] = v

    def tall(v):
        return jnp.concatenate(
            [jnp.broadcast_to(v[j:j + 1], (COARSEN, cz)) for j in range(rows)], axis=0)

    for g in range(GROUPS):
        receive(2, g)
    sums = []
    for i in range(ions):
        near = rim(2, i)
        for h in range(2):
            rhs[h, i] += spread_ref[i] * condp[h] * near[h]
        v = sp[i]
        lift = tall(v[:rows])
        lo, hi = tall(v[rows:2 * rows]), tall(v[2 * rows:3 * rows])
        base = yz_sum(lift) + lift
        base += jnp.where(first_y, v[3 * rows:3 * rows + 1], 0.0)
        base += jnp.where(last_y, v[3 * rows + 1:3 * rows + 2], 0.0)
        numer = jnp.zeros((cy, cz), F32)
        denom = jnp.zeros((cy, cz), F32)
        for h in range(2):
            for k in range(kp):
                side = lift
                low_side = p if h else jnp.logical_not(p)
                high_side = jnp.logical_not(p) if h else p
                if k == 0:
                    side = jnp.where(low_side, lo, side)
                if k == kp - 1:
                    side = jnp.where(high_side, hi, side)
                im = diag[h, i, k] * lift - spread_ref[i] * condp[h, k] * (base + side)
                image[h, i, k] = im
                numer += rhs[h, i, k] * im
                denom += im * im
        sums.append((jnp.sum(numer, axis=0, keepdims=True), jnp.sum(denom, axis=0, keepdims=True)))
    moments = jnp.concatenate([n for n, _ in sums] + [m for _, m in sums], axis=0)
    moments = jnp.sum(moments, axis=1, keepdims=True)
    share = cz // (2 * ions)
    prow = lax.broadcasted_iota(jnp.int32, (2 * ions, cz), 0)
    plane_of = lax.broadcasted_iota(jnp.int32, (2 * ions, cz), 1) // share
    part[me] = jnp.sum(jnp.where(prow == plane_of, moments, 0.0), axis=0, keepdims=True)
    to_all(part, psend, precv)
    all_of(part, precv)
    whole = jnp.sum(part[...], axis=0)
    weight = whole / (pltpu.roll(whole, ions * share, 1) + EPSILON)
    for i in range(ions):
        wv[i:i + 1] = jnp.broadcast_to(weight[:, i * share:i * share + 1], (1, cz))

    for i in range(ions):
        wt = wv[i:i + 1]
        lifted = wt * tall(sp[i, :rows])
        for k in range(kp):
            red, black = d[0, i, k], d[1, i, k]
            up_ref[i, 2 * k] = state_ref[i, 2 * k] + (jnp.where(p, black, red) + lifted)
            up_ref[i, 2 * k + 1] = state_ref[i, 2 * k + 1] + (jnp.where(p, red, black) + lifted)
            red = rhs[0, i, k] - wt * image[0, i, k]
            black = rhs[1, i, k] - wt * image[1, i, k]
            res_ref[i, 2 * k] = jnp.where(p, black, red)
            res_ref[i, 2 * k + 1] = jnp.where(p, red, black)

    for e in range(3):
        for k in range(4):
            @pl.when(has[k])
            def _():
                for g in range(GROUPS):
                    copy(e, k, g).wait_send()
    for k in range(4):
        @pl.when(has[k])
        def _():
            cond_copy(k).wait_send()
    all_of(ops, osend)
    all_of(gath, gsend)
    all_of(part, psend)


def drain(up_ref, res_ref, up_out, res_out, sem):
    copies = [pltpu.make_async_copy(up_ref, up_out, sem.at[0]),
              pltpu.make_async_copy(res_ref, res_out, sem.at[1])]
    for one in copies:
        one.start()
    for one in copies:
        one.wait()


def on_device(n_span, n_width, state, source, conductance, rebar_cover, colour, diffusivity, binding):
    ions, cx, cy, cz = state.shape
    kp = cx // 2
    rows = cy // COARSEN
    half = pltpu.VMEM((2, ions, kp, cy, cz), F32)
    pair = pltpu.VMEM((2, kp, cy, cz), F32)
    vmem = pl.BlockSpec(memory_space=pltpu.VMEM)
    smem = pl.BlockSpec(memory_space=pltpu.SMEM)
    dma = pltpu.SemaphoreType.DMA
    anywhere = pl.BlockSpec(memory_space=pl.ANY)
    hbm = pl.BlockSpec(memory_space=pltpu.HBM)
    face_x = pltpu.VMEM((3, 2, ions, cy, cz), F32)
    face_y = pltpu.VMEM((3, 2, ions, 2 * kp, cz), F32)
    everyone = n_span * n_width
    rounds = (n_span - 1).bit_length()
    up, res = pl.pallas_call(
        functools.partial(kernel, n_span, n_width, ions, cx, cy, cz),
        out_shape=(pltpu.VMEM(state.shape, F32),) * 2,
        in_specs=[pl.BlockSpec(memory_space=pltpu.HBM)] * 4 + [smem] * 3,
        out_specs=(vmem, vmem),
        scratch_shapes=[
            pltpu.VMEM(state.shape, F32), pltpu.VMEM(state.shape, F32),
            pltpu.VMEM(conductance.shape, F32), pltpu.VMEM(conductance.shape, jnp.int32),
            pltpu.VMEM((2, 2, ions, cy, cz), F32), face_x, face_y, face_y,
            pltpu.VMEM((2, 2 * kp, cz), F32),
            pltpu.VMEM((2, cy, cz), F32),
            pltpu.VMEM((2, 2 * kp, cz), F32),
            pltpu.VMEM((everyone, rows, cz), F32),
            pltpu.VMEM((everyone, 2 * rows, cz), F32),
            pltpu.VMEM((everyone, 1, cz), F32),
            pair, pair, half, half, half, half, half, half,
            pltpu.VMEM((ions, cy, cz), F32),
            pltpu.VMEM((3, ions, cy, cz), F32),
            pltpu.VMEM((2, ions, 1, cz), F32),
            pltpu.VMEM((n_span // 2, n_width * rows, cz), F32),
            pltpu.VMEM((n_span // 2, n_width * rows, cz), F32),
            pltpu.VMEM((n_span + 2, n_width * rows, cz), F32),
            pltpu.VMEM((ions, 16, cz), F32),
            pltpu.VMEM((ions, cz), F32),
            dma((3, 4, GROUPS)), dma((3, 4, GROUPS)), dma((4,)), dma((4,)),
            dma, dma, dma, dma, dma, dma, dma((4,)), pltpu.SemaphoreType.REGULAR((rounds,)),
        ],
        compiler_params=pltpu.CompilerParams(
            collective_id=0, has_side_effects=True, vmem_limit_bytes=48 * 1024 * 1024
        ),
    )(state, source, conductance, rebar_cover, colour, diffusivity, binding)
    return pl.pallas_call(
        drain,
        out_shape=(jax.ShapeDtypeStruct(state.shape, F32),) * 2,
        in_specs=[anywhere] * 2,
        out_specs=(hbm, hbm),
        scratch_shapes=[dma((2,))],
        compiler_params=pltpu.CompilerParams(vmem_limit_bytes=1024 * 1024),
    )(up, res)


def solution(mesh):
    in_specs = (
        P(None, "span", "width", None),
        P(None, "span", "width", None),
        P("span", "width", None),
        P("span", "width", None),
        P("span", "width"),
        P(),
        P(),
    )
    out_specs = (P(None, "span", "width", None), P(None, "span", "width", None))
    return jax.shard_map(
        functools.partial(on_device, mesh.shape["span"], mesh.shape["width"]),
        mesh=mesh, in_specs=in_specs, out_specs=out_specs, check_vma=False,
    )
```

```python
import functools

import jax
import jax.numpy as jnp
from jax import lax
from jax.experimental import pallas as pl
from jax.experimental.pallas import tpu as pltpu
from jax.sharding import PartitionSpec as P

COARSEN = 8
SWEEPS = 4
COARSE_ITERS = 20
INV_STEP = 0.05
EPSILON = 1e-06
MESH = pl.DeviceIdType.MESH
GROUPS = 2
UNROLL = 2
F32 = jnp.float32


def kernel(
    n_span, n_width, ions, cx, cy, cz,
    state_hbm, source_hbm, cond_hbm, cover_hbm, colour_ref, spread_ref, strength_ref,
    up_ref, res_ref,
    state_ref, source_ref, cond_ref, cover_ref, xs, xh, ys, yh, ysc, xhc, yhc, ops, gath, part, condp, coverp, rhs, diag, c, a, d, image,
    mx, fx, py, aj, cj, ej, sp, wv,
    send_sem, recv_sem, csend, crecv, osend, orecv, gsend, grecv, psend, precv, in_sem, met,
):
    s = lax.axis_index("span")
    w = lax.axis_index("width")
    kp = cx // 2
    rows = cy // COARSEN
    row = lax.broadcasted_iota(jnp.int32, (cy, cz), 0)
    lane = lax.broadcasted_iota(jnp.int32, (cy, cz), 1)
    p = (row + lane) % 2 == 1
    first_y, last_y = row == 0, row == cy - 1
    first_z, last_z = lane == 0, lane == cz - 1

    loads = [
        pltpu.make_async_copy(src, dst, in_sem.at[k])
        for k, (src, dst) in enumerate((
            (state_hbm, state_ref), (cond_hbm, cond_ref),
            (cover_hbm, cover_ref), (source_hbm, source_ref)))
    ]
    for load in loads:
        load.start()

    barrier = pltpu.get_barrier_semaphore()

    has = (s < n_span - 1, s > 0, w < n_width - 1, w > 0)
    gets = (s > 0, s < n_span - 1, w > 0, w < n_width - 1)
    to = ((s + 1, w), (s - 1, w), (s, w + 1), (s, w - 1))

    def flip(v, bit):
        return v + bit - 2 * bit * (v // bit % 2)

    quad = 4
    high = [1 << k for k in range(2, (n_span - 1).bit_length())]
    partners = [lax.rem(w + k, n_width) for k in range(1, n_width)]
    quads = [s - s % quad + (s + k) % quad for k in range(1, quad)]
    greet = [(s, v) for v in partners] + [(t, w) for t in quads] + [(flip(s, b), w) for b in high]
    up_far = (s % quad == quad - 1) & (s < n_span - 1)
    down_far = (s % quad == 0) & (s > 0)
    rounds = [
        [(s, v) for v in partners] + [(t, w) for t in quads],
        [(flip(s, high[0]), w)] + [(flip(s, b), v) for b in high[:2] for v in partners],
    ] + [[(flip(s, b), w)] for b in high[2:]]
    for other in greet:
        pl.semaphore_signal(barrier, inc=1, device_id=other, device_id_type=MESH)
    for ok, other in ((up_far, (s + 1, w)), (down_far, (s - 1, w))):
        @pl.when(ok)
        def _():
            pl.semaphore_signal(barrier, inc=1, device_id=other, device_id_type=MESH)
    greeted = len(greet) + up_far.astype(jnp.int32) + down_far.astype(jnp.int32)

    def meet(k):
        for other in rounds[k]:
            pl.semaphore_signal(met.at[k], inc=1, device_id=other, device_id_type=MESH)

    def met_by(k):
        pl.semaphore_wait(met.at[k], len(rounds[k]))

    everyone = n_span * n_width
    me = s * n_width + w

    def to_all(buf, ssem, rsem):
        @pl.loop(1, everyone)
        def _(off):
            other = lax.rem(me + off, everyone)
            pltpu.make_async_remote_copy(
                src_ref=buf.at[me], dst_ref=buf.at[me], send_sem=ssem, recv_sem=rsem,
                device_id=(other // n_width, other % n_width), device_id_type=MESH,
            ).start()

    def all_of(buf, sem):
        others = buf.at[pl.ds(0, everyone - 1)]
        pltpu.make_async_copy(others, others, sem).wait()

    def split(x):
        pairs = x.reshape(kp, 2, cy, cz)
        even, odd = pairs[:, 0], pairs[:, 1]
        return jnp.where(p, odd, even), jnp.where(p, even, odd)

    def yz_sum(v):
        out = jnp.where(last_y, 0.0, pltpu.roll(v, cy - 1, v.ndim - 2))
        out += jnp.where(first_y, 0.0, pltpu.roll(v, 1, v.ndim - 2))
        out += jnp.where(last_z, 0.0, pltpu.roll(v, cz - 1, v.ndim - 1))
        out += jnp.where(first_z, 0.0, pltpu.roll(v, 1, v.ndim - 1))
        return out

    zero_face = jnp.zeros((1, cy, cz), F32)

    def nb_red(black):
        above = jnp.concatenate([black[1:], zero_face], axis=0)
        below = jnp.concatenate([zero_face, black[:-1]], axis=0)
        return black + jnp.where(p, above, below) + yz_sum(black)

    def nb_black(red):
        above = jnp.concatenate([red[1:], zero_face], axis=0)
        below = jnp.concatenate([zero_face, red[:-1]], axis=0)
        return red + jnp.where(p, below, above) + yz_sum(red)

    def rim(e, i):
        lo, hi = xh[e, 0, i], xh[e, 1, i]
        ylo, yhi = yh[e, 0, i], yh[e, 1, i]
        mid = jnp.zeros((kp - 2, cy, cz), F32)

        def faces(k0, k1, half):
            x_part = jnp.concatenate([k0[None], mid, k1[None]], axis=0)
            low = ylo[half * kp:(half + 1) * kp][:, None, :]
            high = yhi[half * kp:(half + 1) * kp][:, None, :]
            return x_part + jnp.where(first_y, low, 0.0) + jnp.where(last_y, high, 0.0)

        red = faces(jnp.where(p, 0.0, lo), jnp.where(p, hi, 0.0), 1)
        black = faces(jnp.where(p, lo, 0.0), jnp.where(p, 0.0, hi), 0)
        return red, black

    def put_y(e, i, red, black):
        ys[e, 0, i] = jnp.concatenate([red[:, cy - 1, :], black[:, cy - 1, :]], axis=0)
        ys[e, 1, i] = jnp.concatenate([red[:, 0, :], black[:, 0, :]], axis=0)

    def put_x(e, i, red, black):
        xs[e - 1, 0, i] = jnp.where(p, red[kp - 1], black[kp - 1])
        xs[e - 1, 1, i] = jnp.where(p, black[0], red[0])

    pair_of = ions // GROUPS

    def copy(e, k, g):
        own = pl.ds(g * pair_of, pair_of)
        if k >= 2:
            src, dst = ys.at[e, k - 2, own], yh.at[e, k - 2, own]
        else:
            dst = xh.at[e, k, own]
            if e == 0:
                src = state_ref.at[own, cx - 1] if k == 0 else state_ref.at[own, 0]
            else:
                src = xs.at[e - 1, k, own]
        return pltpu.make_async_remote_copy(
            src_ref=src, dst_ref=dst, send_sem=send_sem.at[e, k, g], recv_sem=recv_sem.at[e, k, g],
            device_id=to[k], device_id_type=MESH,
        )

    def cond_copy(k):
        if k >= 2:
            src, dst = ysc.at[k - 2], yhc.at[k - 2]
        else:
            src, dst = cond_ref.at[cx - 1 if k == 0 else 0], xhc.at[k]
        return pltpu.make_async_remote_copy(
            src_ref=src, dst_ref=dst, send_sem=csend.at[k], recv_sem=crecv.at[k],
            device_id=to[k], device_id_type=MESH,
        )

    def send(e, g):
        for k in range(4):
            @pl.when(has[k])
            def _():
                copy(e, k, g).start()

    def receive(e, g):
        for k in range(4):
            @pl.when(gets[k])
            def _():
                copy(e, k, g).wait_recv()

    for k in range(4):
        @pl.when(jnp.logical_not(gets[k]))
        def _():
            for e in range(3):
                if k >= 2:
                    yh[e, k - 2] = jnp.zeros(yh.shape[2:], F32)
                else:
                    xh[e, k] = jnp.zeros(xh.shape[2:], F32)
            if k >= 2:
                yhc[k - 2] = jnp.zeros(yhc.shape[1:], F32)
            else:
                xhc[k] = jnp.zeros(xhc.shape[1:], F32)

    def pack_state(i, _):
        put_y(0, i, *split(state_ref[i]))
        return 0

    loads[0].wait()
    lax.fori_loop(0, ions, pack_state, 0)
    pl.semaphore_wait(barrier, greeted)
    for g in range(GROUPS):
        send(0, g)
    meet(0)

    loads[1].wait()
    condp[0], condp[1] = split(cond_ref[...])
    ysc[0] = jnp.concatenate([condp[0, :, cy - 1, :], condp[1, :, cy - 1, :]], axis=0)
    ysc[1] = jnp.concatenate([condp[0, :, 0, :], condp[1, :, 0, :]], axis=0)
    for k in range(4):
        @pl.when(has[k])
        def _():
            cond_copy(k).start()
    for load in loads[2:]:
        load.wait()
    coverp[0], coverp[1] = split(cover_ref[...].astype(F32))

    eighth = lane % COARSEN

    def pack(fields):
        step = 1
        while len(fields) > 1:
            low = lane[:1] // step % 2 == 0
            fields = [
                jnp.where(low, u + pltpu.roll(u, cz - step, 1), v + pltpu.roll(v, step, 1))
                for u, v in zip(fields[::2], fields[1::2])
            ]
            step *= 2
        v = fields[0]
        return jnp.concatenate(
            [jnp.sum(v[j * COARSEN:(j + 1) * COARSEN], axis=0, keepdims=True)
             for j in range(v.shape[0] // COARSEN)], axis=0)

    def local_terms(i, _):
        spread, strength = spread_ref[i], strength_ref[i]
        st = split(state_ref[i])
        src = split(source_ref[i])
        near = (nb_red(st[1]), nb_black(st[0]))
        mass_sum = jnp.zeros((cy, cz), F32)
        for h in range(2):
            coef = spread * condp[h]
            inv = 1.0 / (1.0 + st[h])
            bound = coverp[h] * strength * inv
            mass = INV_STEP + bound * inv
            dg = mass + 6.0 * coef
            diag[h, i] = dg
            c[h, i] = coef / dg
            rhs[h, i] = src[h] - (coef * (6.0 * st[h] - near[h]) + bound * st[h])
            mass_sum += jnp.sum(mass, axis=0)
        mx[i] = mass_sum
        return 0

    lax.fori_loop(0, ions, local_terms, 0)
    cond_sum = jnp.sum(cond_ref[...], axis=0)
    sums = pack([mx[i] for i in range(ions)] + [spread_ref[i] * cond_sum for i in range(ions)])
    low_slot = eighth[:rows] < ions
    coarse_off = pltpu.roll(sums, cz - ions, 1) / COARSEN
    coarse_inv = 1.0 / jnp.where(low_slot, sums + 6.0 * coarse_off, 1.0)
    ops[me] = jnp.where(low_slot, coarse_off * coarse_inv, pltpu.roll(coarse_inv, ions, 1))

    mine = colour_ref[0, 0].astype(F32)

    def sweeps(ar, ab, cr, cb):
        red = ar
        black = ab + cb * nb_black(red)
        for _ in range(SWEEPS - 1):
            red = ar + cr * nb_red(black)
            black = ab + cb * nb_black(red)
        return red, black

    def phase_zero(i, _):
        near = rim(0, i)
        for h in range(2):
            right = rhs[h, i] + spread_ref[i] * condp[h] * near[h]
            rhs[h, i] = right
            a[h, i] = right / diag[h, i]
        red, black = sweeps(
            (1.0 - mine) * a[0, i], (1.0 - mine) * a[1, i], c[0, i], c[1, i]
        )
        d[0, i], d[1, i] = red, black
        put_y(1, i, red, black)
        put_x(1, i, red, black)
        return 0

    for g in range(GROUPS):
        receive(0, g)
        lax.fori_loop(g * pair_of, (g + 1) * pair_of, phase_zero, 0, unroll=UNROLL)
        send(1, g)
    met_by(0)
    meet(1)
    for k in range(4):
        @pl.when(gets[k])
        def _():
            cond_copy(k).wait_recv()

    def phase_one(i, _):
        near = rim(1, i)
        red, black = sweeps(
            mine * (a[0, i] + c[0, i] * near[0]), mine * (a[1, i] + c[1, i] * near[1]),
            c[0, i], c[1, i],
        )
        red, black = red + d[0, i], black + d[1, i]
        d[0, i], d[1, i] = red, black
        put_y(2, i, red, black)
        put_x(2, i, red, black)
        near = (nb_red(black), nb_black(red))
        total = jnp.zeros((cy, cz), F32)
        for h, v in ((0, red), (1, black)):
            fine = rhs[h, i] - (diag[h, i] * v - spread_ref[i] * condp[h] * near[h])
            rhs[h, i] = fine
            total += jnp.sum(fine, axis=0)
        fx[0, i] = total
        fx[1, i] = spread_ref[i] * (xhc[1] * xs[1, 0, i])
        fx[2, i] = spread_ref[i] * (xhc[0] * xs[1, 1, i])
        for k in range(2):
            face = ys[2, k, i]
            other = jnp.concatenate([face[kp:], face[:kp]], axis=0)
            py[k, i] = spread_ref[i] * jnp.sum(yhc[1 - k] * other, axis=0, keepdims=True)
        return 0

    for g in range(GROUPS):
        receive(1, g)
        lax.fori_loop(g * pair_of, (g + 1) * pair_of, phase_one, 0, unroll=UNROLL)
        if g == GROUPS - 2:
            met_by(1)
            for k in range(2, len(rounds)):
                meet(k)
                met_by(k)
            to_all(ops, osend, orecv)

    def column(i):
        y_part = jnp.where(first_y, py[1, i], jnp.where(last_y, py[0, i], 0.0))
        return (jnp.concatenate([fx[0, i], fx[2, i]], axis=0),
                jnp.concatenate([fx[1, i], y_part], axis=0))

    columns = [column(i) for i in range(ions)]
    gath[me] = pack([u for u, _ in columns] + [v for _, v in columns])
    to_all(gath, gsend, grecv)
    for g in range(GROUPS):
        send(2, g)

    wide = n_width * rows
    half = n_span // 2
    all_of(ops, orecv)
    all_of(gath, grecv)

    crow = lax.broadcasted_iota(jnp.int32, (wide, cz), 0)
    slot_low = lax.broadcasted_iota(jnp.int32, (wide, cz), 1) % COARSEN < ions

    def wide_of(v):
        return jnp.concatenate([v[:, k] for k in range(n_width)], axis=1)

    def down(v):
        return pltpu.roll(v, cz - ions, 2)

    def up(v):
        return pltpu.roll(v, ions, 2)

    def fold(low_part, high_part):
        return jnp.where(slot_low, low_part, high_part)

    plane = jnp.zeros((1, wide, cz), F32)
    o = wide_of(ops[...].reshape(n_span, n_width, rows, cz))
    g = gath[...].reshape(n_span, n_width, 2 * rows, cz)
    plus, minus = wide_of(g[:, :, :rows]), wide_of(g[:, :, rows:])
    y_sum = jnp.where(crow % rows == 0, pltpu.roll(minus, 1, 1), 0.0)
    y_sum = jnp.where(crow % rows == rows - 1, pltpu.roll(minus, wide - 1, 1), y_sum)
    crhs = fold(plus[:half], up(plus[half:]))
    crhs += fold(jnp.concatenate([plane, down(plus[:half - 1])], axis=0), plus[half - 1:-1])
    crhs += fold(minus[1:half + 1], jnp.concatenate([up(minus[half + 1:]), plane], axis=0))
    crhs += fold(down(y_sum[:half]), y_sum[half:])
    aj[...] = crhs * fold(down(o[:half]), o[half:])
    cj[...] = fold(o[:half], up(o[half:]))
    crow = lax.broadcasted_iota(jnp.int32, (wide, cz), 0)
    clane = lax.broadcasted_iota(jnp.int32, (wide, cz), 1)

    def jacobi(_, e):
        above = jnp.where(slot_low, up_one(e[:1], -1), 0.0)
        below = jnp.where(slot_low, 0.0, up_one(e[half - 1:], 1))
        total = jnp.concatenate([e[1:], above], axis=0)
        total += jnp.concatenate([below, e[:-1]], axis=0)
        total += jnp.where(crow == wide - 1, 0.0, pltpu.roll(e, wide - 1, 1))
        total += jnp.where(crow == 0, 0.0, pltpu.roll(e, 1, 1))
        total += jnp.where(clane >= cz - COARSEN, 0.0, pltpu.roll(e, cz - COARSEN, 2))
        total += jnp.where(clane < COARSEN, 0.0, pltpu.roll(e, COARSEN, 2))
        return aj[...] + cj[...] * total

    def up_one(v, sign):
        return pltpu.roll(v, ions if sign > 0 else cz - ions, 2)

    e = lax.fori_loop(0, COARSE_ITERS - 1, jacobi, aj[...])
    ej[0] = plane[0]
    ej[n_span + 1] = plane[0]
    ej[1:half + 1] = e
    ej[half + 1:n_span + 1] = down(e)
    before, here, after = ej[s], ej[s + 1], ej[s + 2]

    def own_rows(v):
        out = v[:rows]
        for k in range(1, n_width):
            out = jnp.where(w == k, v[k * rows:(k + 1) * rows], out)
        return out

    y_low = jnp.zeros((1, cz), F32)
    y_high = jnp.zeros((1, cz), F32)
    for k in range(n_width):
        if k > 0:
            y_low = jnp.where(w == k, here[k * rows - 1:k * rows], y_low)
        if k < n_width - 1:
            y_high = jnp.where(w == k, here[(k + 1) * rows:(k + 1) * rows + 1], y_high)
    packed = jnp.concatenate(
        [own_rows(here), own_rows(before), own_rows(after), y_low, y_high,
         jnp.zeros((16 - 3 * rows - 2, cz), F32)], axis=0)
    for i in range(ions):
        v = jnp.where(eighth[:16] == i, packed, 0.0)
        if i:
            v = pltpu.roll(v, cz - i, 1)
        for step in (1, 2, 4):
            v = v + pltpu.roll(v, step, 1)
        sp[i] = v

    def tall(v):
        return jnp.concatenate(
            [jnp.broadcast_to(v[j:j + 1], (COARSEN, cz)) for j in range(rows)], axis=0)

    for g in range(GROUPS):
        receive(2, g)
    sums = []
    for i in range(ions):
        near = rim(2, i)
        for h in range(2):
            rhs[h, i] += spread_ref[i] * condp[h] * near[h]
        v = sp[i]
        lift = tall(v[:rows])
        lo, hi = tall(v[rows:2 * rows]), tall(v[2 * rows:3 * rows])
        base = yz_sum(lift) + lift
        base += jnp.where(first_y, v[3 * rows:3 * rows + 1], 0.0)
        base += jnp.where(last_y, v[3 * rows + 1:3 * rows + 2], 0.0)
        numer = jnp.zeros((cy, cz), F32)
        denom = jnp.zeros((cy, cz), F32)
        for h in range(2):
            for k in range(kp):
                side = lift
                low_side = p if h else jnp.logical_not(p)
                high_side = jnp.logical_not(p) if h else p
                if k == 0:
                    side = jnp.where(low_side, lo, side)
                if k == kp - 1:
                    side = jnp.where(high_side, hi, side)
                im = diag[h, i, k] * lift - spread_ref[i] * condp[h, k] * (base + side)
                image[h, i, k] = im
                numer += rhs[h, i, k] * im
                denom += im * im
        sums.append((jnp.sum(numer, axis=0, keepdims=True), jnp.sum(denom, axis=0, keepdims=True)))
    moments = jnp.concatenate([n for n, _ in sums] + [m for _, m in sums], axis=0)
    moments = jnp.sum(moments, axis=1, keepdims=True)
    share = cz // (2 * ions)
    prow = lax.broadcasted_iota(jnp.int32, (2 * ions, cz), 0)
    plane_of = lax.broadcasted_iota(jnp.int32, (2 * ions, cz), 1) // share
    part[me] = jnp.sum(jnp.where(prow == plane_of, moments, 0.0), axis=0, keepdims=True)
    to_all(part, psend, precv)
    all_of(part, precv)
    whole = jnp.sum(part[...], axis=0)
    weight = whole / (pltpu.roll(whole, ions * share, 1) + EPSILON)
    for i in range(ions):
        wv[i:i + 1] = jnp.broadcast_to(weight[:, i * share:i * share + 1], (1, cz))

    for i in range(ions):
        wt = wv[i:i + 1]
        lifted = wt * tall(sp[i, :rows])
        for k in range(kp):
            red, black = d[0, i, k], d[1, i, k]
            up_ref[i, 2 * k] = state_ref[i, 2 * k] + (jnp.where(p, black, red) + lifted)
            up_ref[i, 2 * k + 1] = state_ref[i, 2 * k + 1] + (jnp.where(p, red, black) + lifted)
            red = rhs[0, i, k] - wt * image[0, i, k]
            black = rhs[1, i, k] - wt * image[1, i, k]
            res_ref[i, 2 * k] = jnp.where(p, black, red)
            res_ref[i, 2 * k + 1] = jnp.where(p, red, black)

    for e in range(3):
        for k in range(4):
            @pl.when(has[k])
            def _():
                for g in range(GROUPS):
                    copy(e, k, g).wait_send()
    for k in range(4):
        @pl.when(has[k])
        def _():
            cond_copy(k).wait_send()
    all_of(ops, osend)
    all_of(gath, gsend)
    all_of(part, psend)


def drain(up_ref, res_ref, up_out, res_out, sem):
    copies = [pltpu.make_async_copy(up_ref, up_out, sem.at[0]),
              pltpu.make_async_copy(res_ref, res_out, sem.at[1])]
    for one in copies:
        one.start()
    for one in copies:
        one.wait()


def on_device(n_span, n_width, state, source, conductance, rebar_cover, colour, diffusivity, binding):
    ions, cx, cy, cz = state.shape
    kp = cx // 2
    rows = cy // COARSEN
    half = pltpu.VMEM((2, ions, kp, cy, cz), F32)
    pair = pltpu.VMEM((2, kp, cy, cz), F32)
    vmem = pl.BlockSpec(memory_space=pltpu.VMEM)
    smem = pl.BlockSpec(memory_space=pltpu.SMEM)
    dma = pltpu.SemaphoreType.DMA
    anywhere = pl.BlockSpec(memory_space=pl.ANY)
    hbm = pl.BlockSpec(memory_space=pltpu.HBM)
    face_x = pltpu.VMEM((3, 2, ions, cy, cz), F32)
    face_y = pltpu.VMEM((3, 2, ions, 2 * kp, cz), F32)
    everyone = n_span * n_width
    rounds = (n_span - 1).bit_length()
    up, res = pl.pallas_call(
        functools.partial(kernel, n_span, n_width, ions, cx, cy, cz),
        out_shape=(pltpu.VMEM(state.shape, F32),) * 2,
        in_specs=[pl.BlockSpec(memory_space=pltpu.HBM)] * 4 + [smem] * 3,
        out_specs=(vmem, vmem),
        scratch_shapes=[
            pltpu.VMEM(state.shape, F32), pltpu.VMEM(state.shape, F32),
            pltpu.VMEM(conductance.shape, F32), pltpu.VMEM(conductance.shape, jnp.int32),
            pltpu.VMEM((2, 2, ions, cy, cz), F32), face_x, face_y, face_y,
            pltpu.VMEM((2, 2 * kp, cz), F32),
            pltpu.VMEM((2, cy, cz), F32),
            pltpu.VMEM((2, 2 * kp, cz), F32),
            pltpu.VMEM((everyone, rows, cz), F32),
            pltpu.VMEM((everyone, 2 * rows, cz), F32),
            pltpu.VMEM((everyone, 1, cz), F32),
            pair, pair, half, half, half, half, half, half,
            pltpu.VMEM((ions, cy, cz), F32),
            pltpu.VMEM((3, ions, cy, cz), F32),
            pltpu.VMEM((2, ions, 1, cz), F32),
            pltpu.VMEM((n_span // 2, n_width * rows, cz), F32),
            pltpu.VMEM((n_span // 2, n_width * rows, cz), F32),
            pltpu.VMEM((n_span + 2, n_width * rows, cz), F32),
            pltpu.VMEM((ions, 16, cz), F32),
            pltpu.VMEM((ions, cz), F32),
            dma((3, 4, GROUPS)), dma((3, 4, GROUPS)), dma((4,)), dma((4,)),
            dma, dma, dma, dma, dma, dma, dma((4,)), pltpu.SemaphoreType.REGULAR((rounds,)),
        ],
        compiler_params=pltpu.CompilerParams(
            collective_id=0, has_side_effects=True, vmem_limit_bytes=60 * 1024 * 1024
        ),
    )(state, source, conductance, rebar_cover, colour, diffusivity, binding)
    return pl.pallas_call(
        drain,
        out_shape=(jax.ShapeDtypeStruct(state.shape, F32),) * 2,
        in_specs=[anywhere] * 2,
        out_specs=(hbm, hbm),
        scratch_shapes=[dma((2,))],
        compiler_params=pltpu.CompilerParams(vmem_limit_bytes=1024 * 1024),
    )(up, res)


def solution(mesh):
    in_specs = (
        P(None, "span", "width", None),
        P(None, "span", "width", None),
        P("span", "width", None),
        P("span", "width", None),
        P("span", "width"),
        P(),
        P(),
    )
    out_specs = (P(None, "span", "width", None), P(None, "span", "width", None))
    return jax.shard_map(
        functools.partial(on_device, mesh.shape["span"], mesh.shape["width"]),
        mesh=mesh, in_specs=in_specs, out_specs=out_specs, check_vma=False,
    )
```

```python
import functools

import jax
import jax.numpy as jnp
from jax import lax
from jax.experimental import pallas as pl
from jax.experimental.pallas import tpu as pltpu
from jax.sharding import PartitionSpec as P

COARSEN = 8
SWEEPS = 4
COARSE_ITERS = 20
INV_STEP = 0.05
EPSILON = 1e-06
MESH = pl.DeviceIdType.MESH
GROUPS = 2
UNROLL = 2
F32 = jnp.float32


def kernel(
    n_span, n_width, ions, cx, cy, cz,
    state_hbm, source_hbm, cond_hbm, cover_hbm, colour_hbm, spread_hbm, strength_hbm,
    up_ref, res_ref,
    colour_ref, spread_ref, strength_ref, state_ref, source_ref, cond_ref, cover_ref, xs, xh, ys, yh, ysc, xhc, yhc, ops, gath, part, condp, coverp, rhs, diag, c, a, d, image,
    mx, fx, aj, cj, ej, sp, wv,
    send_sem, recv_sem, csend, crecv, osend, orecv, gsend, grecv, psend, precv, in_sem, met,
):
    s = lax.axis_index("span")
    w = lax.axis_index("width")
    kp = cx // 2
    rows = cy // COARSEN
    row = lax.broadcasted_iota(jnp.int32, (cy, cz), 0)
    lane = lax.broadcasted_iota(jnp.int32, (cy, cz), 1)
    p = (row + lane) % 2 == 1
    first_y, last_y = row == 0, row == cy - 1
    first_z, last_z = lane == 0, lane == cz - 1

    loads = [
        pltpu.make_async_copy(src, dst, in_sem.at[k])
        for k, (src, dst) in enumerate((
            (state_hbm, state_ref), (cond_hbm, cond_ref),
            (cover_hbm, cover_ref), (source_hbm, source_ref),
            (colour_hbm, colour_ref), (spread_hbm, spread_ref), (strength_hbm, strength_ref)))
    ]
    for load in loads:
        load.start()

    barrier = pltpu.get_barrier_semaphore()

    has = (s < n_span - 1, s > 0, w < n_width - 1, w > 0)
    gets = (s > 0, s < n_span - 1, w > 0, w < n_width - 1)
    to = ((s + 1, w), (s - 1, w), (s, w + 1), (s, w - 1))

    def flip(v, bit):
        return v + bit - 2 * bit * (v // bit % 2)

    def signal(sem, moves):
        count = 0
        for ok, t, v in moves:
            @pl.when(ok)
            def _():
                pl.semaphore_signal(sem, inc=1, device_id=(t, v), device_id_type=MESH)
            count = count + ok.astype(jnp.int32)
        return count

    quad = 4
    planes = n_span // quad
    everyone = n_span * n_width
    me = s * n_width + w
    staged = n_width == 2 and 2 <= planes <= 4
    if staged:
        z = s // quad

        def shifted(by):
            return (z + by >= 0) & (z + by < planes), s + by * quad

        def pairs(*moves):
            return [shifted(by) + (v,) for by, v in moves]

        always = s >= 0
        greet = [(always, s, 1 - w), (always, flip(s, 1), w), (always, flip(s, 2), w)]
        greet += pairs((1, w), (-1, w))
        greet += [((s % 2 == 1) & (s < n_span - 1), s + 1, w), ((s % 2 == 0) & (s > 0), s - 1, w)]
        rounds = [
            [(always, s, 1 - w), (always, flip(s, 1), w)],
            [(always, flip(s, 2), w)] + pairs((1, w), (-1, w)),
            [(always, flip(s, 2), w)] + pairs((2, w), (-2, w), (2, 1 - w), (-2, 1 - w)),
        ]
        greeted = signal(barrier, greet)
    else:
        rounds = [[], [], []]
        greeted = everyone - 1

        @pl.loop(1, everyone)
        def _(off):
            other = lax.rem(me + off, everyone)
            pl.semaphore_signal(
                barrier, inc=1, device_id=(other // n_width, other % n_width), device_id_type=MESH)

    def meet(k):
        return signal(met.at[k], rounds[k]) if rounds[k] else 0

    def met_by(k, count):
        if rounds[k]:
            pl.semaphore_wait(met.at[k], count)

    def to_all(buf, ssem, rsem):
        @pl.loop(1, everyone)
        def _(off):
            other = lax.rem(me + off, everyone)
            pltpu.make_async_remote_copy(
                src_ref=buf.at[me], dst_ref=buf.at[me], send_sem=ssem, recv_sem=rsem,
                device_id=(other // n_width, other % n_width), device_id_type=MESH,
            ).start()

    def all_of(buf, sem):
        others = buf.at[pl.ds(0, everyone - 1)]
        pltpu.make_async_copy(others, others, sem).wait()

    def split(x):
        pairs = x.reshape(kp, 2, cy, cz)
        even, odd = pairs[:, 0], pairs[:, 1]
        return jnp.where(p, odd, even), jnp.where(p, even, odd)

    def yz_sum(v):
        out = jnp.where(last_y, 0.0, pltpu.roll(v, cy - 1, v.ndim - 2))
        out += jnp.where(first_y, 0.0, pltpu.roll(v, 1, v.ndim - 2))
        out += jnp.where(last_z, 0.0, pltpu.roll(v, cz - 1, v.ndim - 1))
        out += jnp.where(first_z, 0.0, pltpu.roll(v, 1, v.ndim - 1))
        return out

    zero_face = jnp.zeros((1, cy, cz), F32)

    def nb_red(black):
        above = jnp.concatenate([black[1:], zero_face], axis=0)
        below = jnp.concatenate([zero_face, black[:-1]], axis=0)
        return black + jnp.where(p, above, below) + yz_sum(black)

    def nb_black(red):
        above = jnp.concatenate([red[1:], zero_face], axis=0)
        below = jnp.concatenate([zero_face, red[:-1]], axis=0)
        return red + jnp.where(p, below, above) + yz_sum(red)

    def rim(e, i):
        lo, hi = xh[e, 0, i], xh[e, 1, i]
        ylo, yhi = yh[e, 0, i], yh[e, 1, i]
        mid = jnp.zeros((kp - 2, cy, cz), F32)

        def faces(k0, k1, half):
            x_part = jnp.concatenate([k0[None], mid, k1[None]], axis=0)
            low = ylo[half * kp:(half + 1) * kp][:, None, :]
            high = yhi[half * kp:(half + 1) * kp][:, None, :]
            return x_part + jnp.where(first_y, low, 0.0) + jnp.where(last_y, high, 0.0)

        red = faces(jnp.where(p, 0.0, lo), jnp.where(p, hi, 0.0), 1)
        black = faces(jnp.where(p, lo, 0.0), jnp.where(p, 0.0, hi), 0)
        return red, black

    def put_y(e, i, red, black):
        ys[e, 0, i] = jnp.concatenate([red[:, cy - 1, :], black[:, cy - 1, :]], axis=0)
        ys[e, 1, i] = jnp.concatenate([red[:, 0, :], black[:, 0, :]], axis=0)

    def put_x(e, i, red, black):
        xs[e - 1, 0, i] = jnp.where(p, red[kp - 1], black[kp - 1])
        xs[e - 1, 1, i] = jnp.where(p, black[0], red[0])

    pair_of = ions // GROUPS

    def copy(e, k, g):
        own = pl.ds(g * pair_of, pair_of)
        if k >= 2:
            src, dst = ys.at[e, k - 2, own], yh.at[e, k - 2, own]
        else:
            dst = xh.at[e, k, own]
            if e == 0:
                src = state_ref.at[own, cx - 1] if k == 0 else state_ref.at[own, 0]
            else:
                src = xs.at[e - 1, k, own]
        return pltpu.make_async_remote_copy(
            src_ref=src, dst_ref=dst, send_sem=send_sem.at[e, k, g], recv_sem=recv_sem.at[e, k, g],
            device_id=to[k], device_id_type=MESH,
        )

    def cond_copy(k):
        if k >= 2:
            src, dst = ysc.at[k - 2], yhc.at[k - 2]
        else:
            src, dst = cond_ref.at[cx - 1 if k == 0 else 0], xhc.at[k]
        return pltpu.make_async_remote_copy(
            src_ref=src, dst_ref=dst, send_sem=csend.at[k], recv_sem=crecv.at[k],
            device_id=to[k], device_id_type=MESH,
        )

    def send(e, g):
        for k in range(4):
            @pl.when(has[k])
            def _():
                copy(e, k, g).start()

    def receive(e, g):
        for k in range(4):
            @pl.when(gets[k])
            def _():
                copy(e, k, g).wait_recv()

    for k in range(4):
        @pl.when(jnp.logical_not(gets[k]))
        def _():
            for e in range(3):
                if k >= 2:
                    yh[e, k - 2] = jnp.zeros(yh.shape[2:], F32)
                else:
                    xh[e, k] = jnp.zeros(xh.shape[2:], F32)
            if k >= 2:
                yhc[k - 2] = jnp.zeros(yhc.shape[1:], F32)
            else:
                xhc[k] = jnp.zeros(xhc.shape[1:], F32)

    def pack_state(i, _):
        put_y(0, i, *split(state_ref[i]))
        return 0

    loads[0].wait()
    lax.fori_loop(0, ions, pack_state, 0)
    pl.semaphore_wait(barrier, greeted)
    for g in range(GROUPS):
        send(0, g)
    expected = meet(0)

    loads[1].wait()
    condp[0], condp[1] = split(cond_ref[...])
    ysc[0] = jnp.concatenate([condp[0, :, cy - 1, :], condp[1, :, cy - 1, :]], axis=0)
    ysc[1] = jnp.concatenate([condp[0, :, 0, :], condp[1, :, 0, :]], axis=0)
    for load in loads[2:]:
        load.wait()
    coverp[0], coverp[1] = split(cover_ref[...].astype(F32))

    eighth = lane % COARSEN

    def pack(fields):
        total = None
        for j, v in enumerate(fields):
            v = jnp.concatenate(
                [jnp.sum(v[b * COARSEN:(b + 1) * COARSEN], axis=0, keepdims=True)
                 for b in range(v.shape[0] // COARSEN)], axis=0)
            turned = [v if l == j else pltpu.roll(v, (j - l) % cz, 1) for l in range(COARSEN)]
            while len(turned) > 1:
                turned = [u + t for u, t in zip(turned[::2], turned[1::2])]
            here = eighth[:v.shape[0]] == j
            total = turned[0] if total is None else jnp.where(here, turned[0], total)
        return total

    def local_terms(i, _):
        spread, strength = spread_ref[i], strength_ref[i]
        st = split(state_ref[i])
        src = split(source_ref[i])
        near = (nb_red(st[1]), nb_black(st[0]))
        mass_sum = jnp.zeros((cy, cz), F32)
        for h in range(2):
            coef = spread * condp[h]
            inv = 1.0 / (1.0 + st[h])
            bound = coverp[h] * strength * inv
            mass = INV_STEP + bound * inv
            dg = mass + 6.0 * coef
            diag[h, i] = dg
            c[h, i] = coef / dg
            rhs[h, i] = src[h] - (coef * (6.0 * st[h] - near[h]) + bound * st[h])
            mass_sum += jnp.sum(mass, axis=0)
        mx[i] = mass_sum
        return 0

    lax.fori_loop(0, ions, local_terms, 0)
    cond_sum = jnp.sum(cond_ref[...], axis=0)
    sums = pack([mx[i] for i in range(ions)] + [spread_ref[i] * cond_sum for i in range(ions)])
    low_slot = eighth[:rows] < ions
    coarse_off = pltpu.roll(sums, cz - ions, 1) / COARSEN
    coarse_inv = 1.0 / jnp.where(low_slot, sums + 6.0 * coarse_off, 1.0)
    ops[me] = jnp.where(low_slot, coarse_off * coarse_inv, pltpu.roll(coarse_inv, ions, 1))

    mine = colour_ref[0, 0].astype(F32)

    def sweeps(ar, ab, cr, cb):
        red = ar
        black = ab + cb * nb_black(red)
        for _ in range(SWEEPS - 1):
            red = ar + cr * nb_red(black)
            black = ab + cb * nb_black(red)
        return red, black

    def phase_zero(i, _):
        near = rim(0, i)
        for h in range(2):
            right = rhs[h, i] + spread_ref[i] * condp[h] * near[h]
            rhs[h, i] = right
            a[h, i] = right / diag[h, i]
        red, black = sweeps(
            (1.0 - mine) * a[0, i], (1.0 - mine) * a[1, i], c[0, i], c[1, i]
        )
        d[0, i], d[1, i] = red, black
        put_y(1, i, red, black)
        put_x(1, i, red, black)
        return 0

    met_by(0, expected)
    expected = meet(1)
    for g in range(GROUPS):
        receive(0, g)
        lax.fori_loop(g * pair_of, (g + 1) * pair_of, phase_zero, 0, unroll=UNROLL)
        send(1, g)
    met_by(1, expected)
    expected = meet(2)
    for k in range(4):
        @pl.when(has[k])
        def _():
            cond_copy(k).start()
    def phase_one(i, _):
        near = rim(1, i)
        red, black = sweeps(
            mine * (a[0, i] + c[0, i] * near[0]), mine * (a[1, i] + c[1, i] * near[1]),
            c[0, i], c[1, i],
        )
        red, black = red + d[0, i], black + d[1, i]
        d[0, i], d[1, i] = red, black
        put_y(2, i, red, black)
        put_x(2, i, red, black)
        near = (nb_red(black), nb_black(red))
        total = jnp.zeros((cy, cz), F32)
        for h, v in ((0, red), (1, black)):
            fine = rhs[h, i] - (diag[h, i] * v - spread_ref[i] * condp[h] * near[h])
            rhs[h, i] = fine
            total += jnp.sum(fine, axis=0)
        fx[i] = total
        return 0

    for g in range(GROUPS):
        receive(1, g)
        if g == GROUPS - 1:
            met_by(2, expected)
            to_all(ops, osend, orecv)
        lax.fori_loop(g * pair_of, (g + 1) * pair_of, phase_one, 0, unroll=UNROLL)

    for k in range(4):
        @pl.when(gets[k])
        def _():
            cond_copy(k).wait_recv()

    def across(k, i):
        face = ys[2, k, i]
        other = jnp.concatenate([face[kp:], face[:kp]], axis=0)
        return spread_ref[i] * jnp.sum(yhc[1 - k] * other, axis=0, keepdims=True)

    def column(i):
        spread = spread_ref[i]
        y_part = jnp.where(first_y, across(1, i), jnp.where(last_y, across(0, i), 0.0))
        return (jnp.concatenate([fx[i], spread * (xhc[0] * xs[1, 1, i])], axis=0),
                jnp.concatenate([spread * (xhc[1] * xs[1, 0, i]), y_part], axis=0))

    columns = [column(i) for i in range(ions)]
    gath[me] = pack([u for u, _ in columns] + [v for _, v in columns])
    to_all(gath, gsend, grecv)
    for g in range(GROUPS):
        send(2, g)

    wide = n_width * rows
    half = n_span // 2
    all_of(ops, orecv)
    all_of(gath, grecv)

    crow = lax.broadcasted_iota(jnp.int32, (wide, cz), 0)
    slot_low = lax.broadcasted_iota(jnp.int32, (wide, cz), 1) % COARSEN < ions

    def wide_of(v):
        return jnp.concatenate([v[:, k] for k in range(n_width)], axis=1)

    def down(v):
        return pltpu.roll(v, cz - ions, 2)

    def up(v):
        return pltpu.roll(v, ions, 2)

    def fold(low_part, high_part):
        return jnp.where(slot_low, low_part, high_part)

    plane = jnp.zeros((1, wide, cz), F32)
    o = wide_of(ops[...].reshape(n_span, n_width, rows, cz))
    g = gath[...].reshape(n_span, n_width, 2 * rows, cz)
    plus, minus = wide_of(g[:, :, :rows]), wide_of(g[:, :, rows:])
    y_sum = jnp.where(crow % rows == 0, pltpu.roll(minus, 1, 1), 0.0)
    y_sum = jnp.where(crow % rows == rows - 1, pltpu.roll(minus, wide - 1, 1), y_sum)
    crhs = fold(plus[:half], up(plus[half:]))
    crhs += fold(jnp.concatenate([plane, down(plus[:half - 1])], axis=0), plus[half - 1:-1])
    crhs += fold(minus[1:half + 1], jnp.concatenate([up(minus[half + 1:]), plane], axis=0))
    crhs += fold(down(y_sum[:half]), y_sum[half:])
    aj[...] = crhs * fold(down(o[:half]), o[half:])
    cj[...] = fold(o[:half], up(o[half:]))
    crow = lax.broadcasted_iota(jnp.int32, (wide, cz), 0)
    clane = lax.broadcasted_iota(jnp.int32, (wide, cz), 1)

    def jacobi(_, e):
        above = jnp.where(slot_low, up_one(e[:1], -1), 0.0)
        below = jnp.where(slot_low, 0.0, up_one(e[half - 1:], 1))
        total = jnp.concatenate([e[1:], above], axis=0)
        total += jnp.concatenate([below, e[:-1]], axis=0)
        total += jnp.where(crow == wide - 1, 0.0, pltpu.roll(e, wide - 1, 1))
        total += jnp.where(crow == 0, 0.0, pltpu.roll(e, 1, 1))
        total += jnp.where(clane >= cz - COARSEN, 0.0, pltpu.roll(e, cz - COARSEN, 2))
        total += jnp.where(clane < COARSEN, 0.0, pltpu.roll(e, COARSEN, 2))
        return aj[...] + cj[...] * total

    def up_one(v, sign):
        return pltpu.roll(v, ions if sign > 0 else cz - ions, 2)

    e = lax.fori_loop(0, COARSE_ITERS - 1, jacobi, aj[...])
    ej[0] = plane[0]
    ej[n_span + 1] = plane[0]
    ej[1:half + 1] = e
    ej[half + 1:n_span + 1] = down(e)
    before, here, after = ej[s], ej[s + 1], ej[s + 2]

    def own_rows(v):
        out = v[:rows]
        for k in range(1, n_width):
            out = jnp.where(w == k, v[k * rows:(k + 1) * rows], out)
        return out

    y_low = jnp.zeros((1, cz), F32)
    y_high = jnp.zeros((1, cz), F32)
    for k in range(n_width):
        if k > 0:
            y_low = jnp.where(w == k, here[k * rows - 1:k * rows], y_low)
        if k < n_width - 1:
            y_high = jnp.where(w == k, here[(k + 1) * rows:(k + 1) * rows + 1], y_high)
    packed = jnp.concatenate(
        [own_rows(here), own_rows(before), own_rows(after), y_low, y_high,
         jnp.zeros((16 - 3 * rows - 2, cz), F32)], axis=0)
    for i in range(ions):
        v = jnp.where(eighth[:16] == i, packed, 0.0)
        turned = [v if l == i else pltpu.roll(v, (l - i) % cz, 1) for l in range(COARSEN)]
        while len(turned) > 1:
            turned = [u + t for u, t in zip(turned[::2], turned[1::2])]
        sp[i] = turned[0]

    def tall(v):
        return jnp.concatenate(
            [jnp.broadcast_to(v[j:j + 1], (COARSEN, cz)) for j in range(rows)], axis=0)

    for g in range(GROUPS):
        receive(2, g)
    sums = []
    for i in range(ions):
        near = rim(2, i)
        for h in range(2):
            rhs[h, i] += spread_ref[i] * condp[h] * near[h]
        v = sp[i]
        lift = tall(v[:rows])
        lo, hi = tall(v[rows:2 * rows]), tall(v[2 * rows:3 * rows])
        base = yz_sum(lift) + lift
        base += jnp.where(first_y, v[3 * rows:3 * rows + 1], 0.0)
        base += jnp.where(last_y, v[3 * rows + 1:3 * rows + 2], 0.0)
        numer = jnp.zeros((cy, cz), F32)
        denom = jnp.zeros((cy, cz), F32)
        for h in range(2):
            for k in range(kp):
                side = lift
                low_side = p if h else jnp.logical_not(p)
                high_side = jnp.logical_not(p) if h else p
                if k == 0:
                    side = jnp.where(low_side, lo, side)
                if k == kp - 1:
                    side = jnp.where(high_side, hi, side)
                im = diag[h, i, k] * lift - spread_ref[i] * condp[h, k] * (base + side)
                image[h, i, k] = im
                numer += rhs[h, i, k] * im
                denom += im * im
        sums.append((jnp.sum(numer, axis=0, keepdims=True), jnp.sum(denom, axis=0, keepdims=True)))
    moments = jnp.concatenate([n for n, _ in sums] + [m for _, m in sums], axis=0)
    moments = jnp.sum(moments, axis=1, keepdims=True)
    share = cz // ions
    prow = lax.broadcasted_iota(jnp.int32, (ions, cz), 0)
    mine_of = prow == lax.broadcasted_iota(jnp.int32, (ions, cz), 1) // share
    part[me] = jnp.concatenate(
        [jnp.sum(jnp.where(mine_of, v, 0.0), axis=0, keepdims=True)
         for v in (moments[:ions], moments[ions:])], axis=0)
    to_all(part, psend, precv)
    all_of(part, precv)
    whole = jnp.sum(part[...], axis=0)
    weight = whole[:1] / (whole[1:] + EPSILON)
    for i in range(ions):
        wv[i:i + 1] = jnp.broadcast_to(weight[:, i * share:i * share + 1], (1, cz))

    for i in range(ions):
        wt = wv[i:i + 1]
        lifted = wt * tall(sp[i, :rows])
        for k in range(kp):
            red, black = d[0, i, k], d[1, i, k]
            up_ref[i, 2 * k] = state_ref[i, 2 * k] + (jnp.where(p, black, red) + lifted)
            up_ref[i, 2 * k + 1] = state_ref[i, 2 * k + 1] + (jnp.where(p, red, black) + lifted)
            red = rhs[0, i, k] - wt * image[0, i, k]
            black = rhs[1, i, k] - wt * image[1, i, k]
            res_ref[i, 2 * k] = jnp.where(p, black, red)
            res_ref[i, 2 * k + 1] = jnp.where(p, red, black)

    for e in range(3):
        for k in range(4):
            @pl.when(has[k])
            def _():
                for g in range(GROUPS):
                    copy(e, k, g).wait_send()
    for k in range(4):
        @pl.when(has[k])
        def _():
            cond_copy(k).wait_send()
    all_of(ops, osend)
    all_of(gath, gsend)
    all_of(part, psend)


def drain(up_ref, res_ref, up_out, res_out, sem):
    copies = [pltpu.make_async_copy(up_ref, up_out, sem.at[0]),
              pltpu.make_async_copy(res_ref, res_out, sem.at[1])]
    for one in copies:
        one.start()
    for one in copies:
        one.wait()


def on_device(n_span, n_width, state, source, conductance, rebar_cover, colour, diffusivity, binding):
    ions, cx, cy, cz = state.shape
    kp = cx // 2
    rows = cy // COARSEN
    half = pltpu.VMEM((2, ions, kp, cy, cz), F32)
    pair = pltpu.VMEM((2, kp, cy, cz), F32)
    vmem = pl.BlockSpec(memory_space=pltpu.VMEM)
    dma = pltpu.SemaphoreType.DMA
    anywhere = pl.BlockSpec(memory_space=pl.ANY)
    hbm = pl.BlockSpec(memory_space=pltpu.HBM)
    face_x = pltpu.VMEM((3, 2, ions, cy, cz), F32)
    face_y = pltpu.VMEM((3, 2, ions, 2 * kp, cz), F32)
    everyone = n_span * n_width
    up, res = pl.pallas_call(
        functools.partial(kernel, n_span, n_width, ions, cx, cy, cz),
        out_shape=(pltpu.VMEM(state.shape, F32),) * 2,
        in_specs=[pl.BlockSpec(memory_space=pltpu.HBM)] * 7,
        out_specs=(vmem, vmem),
        scratch_shapes=[
            pltpu.SMEM((1, 1), jnp.int32), pltpu.SMEM((ions,), F32), pltpu.SMEM((ions,), F32),
            pltpu.VMEM(state.shape, F32), pltpu.VMEM(state.shape, F32),
            pltpu.VMEM(conductance.shape, F32), pltpu.VMEM(conductance.shape, jnp.int32),
            pltpu.VMEM((2, 2, ions, cy, cz), F32), face_x, face_y, face_y,
            pltpu.VMEM((2, 2 * kp, cz), F32),
            pltpu.VMEM((2, cy, cz), F32),
            pltpu.VMEM((2, 2 * kp, cz), F32),
            pltpu.VMEM((everyone, rows, cz), F32),
            pltpu.VMEM((everyone, 2 * rows, cz), F32),
            pltpu.VMEM((everyone, 2, cz), F32),
            pair, pair, half, half, half, half, half, half,
            pltpu.VMEM((ions, cy, cz), F32),
            pltpu.VMEM((ions, cy, cz), F32),
            pltpu.VMEM((n_span // 2, n_width * rows, cz), F32),
            pltpu.VMEM((n_span // 2, n_width * rows, cz), F32),
            pltpu.VMEM((n_span + 2, n_width * rows, cz), F32),
            pltpu.VMEM((ions, 16, cz), F32),
            pltpu.VMEM((ions, cz), F32),
            dma((3, 4, GROUPS)), dma((3, 4, GROUPS)), dma((4,)), dma((4,)),
            dma, dma, dma, dma, dma, dma, dma((7,)), pltpu.SemaphoreType.REGULAR((3,)),
        ],
        compiler_params=pltpu.CompilerParams(
            collective_id=0, has_side_effects=True, vmem_limit_bytes=60 * 1024 * 1024
        ),
    )(state, source, conductance, rebar_cover, colour, diffusivity, binding)
    return pl.pallas_call(
        drain,
        out_shape=(jax.ShapeDtypeStruct(state.shape, F32),) * 2,
        in_specs=[anywhere] * 2,
        out_specs=(hbm, hbm),
        scratch_shapes=[dma((2,))],
        compiler_params=pltpu.CompilerParams(vmem_limit_bytes=1024 * 1024),
    )(up, res)


def solution(mesh):
    in_specs = (
        P(None, "span", "width", None),
        P(None, "span", "width", None),
        P("span", "width", None),
        P("span", "width", None),
        P("span", "width"),
        P(),
        P(),
    )
    out_specs = (P(None, "span", "width", None), P(None, "span", "width", None))
    return jax.shard_map(
        functools.partial(on_device, mesh.shape["span"], mesh.shape["width"]),
        mesh=mesh, in_specs=in_specs, out_specs=out_specs, check_vma=False,
    )
```

```python
import functools

import jax
import jax.numpy as jnp
from jax import lax
from jax.experimental import pallas as pl
from jax.experimental.pallas import tpu as pltpu
from jax.sharding import PartitionSpec as P

COARSEN = 8
SUB = 8
SWEEPS = 4
COARSE_ITERS = 20
INV_STEP = 0.05
EPSILON = 1e-06
MESH = pl.DeviceIdType.MESH
GROUPS = 2
UNROLL_J = 19
F32 = jnp.float32


def kernel(
    n_span, n_width, ions, cx, cy, cz,
    state_hbm, source_hbm, cond_hbm, cover_hbm, colour_hbm, spread_hbm, strength_hbm,
    up_ref, res_ref,
    colour_ref, spread_ref, strength_ref, state_ref, source_ref, cond_ref, cover_ref, xs, xh, ys, yh, ysc, xhc, yhc, ops, gath, part, condp, coverp, rhs, diag, c, a, d, image,
    mx, fx, aj, cj, ej, sp, wv,
    send_sem, recv_sem, csend, crecv, osend, orecv, gsend, grecv, psend, precv, in_sem, met,
):
    s = lax.axis_index("span")
    w = lax.axis_index("width")
    kp = cx // 2
    rows = cy // COARSEN
    nv = cy // SUB
    spread_of = SUB // rows
    slot = lax.broadcasted_iota(jnp.int32, (cy, cz), 0)
    row = slot % SUB * nv + slot // SUB
    lane = lax.broadcasted_iota(jnp.int32, (cy, cz), 1)
    p = (row + lane) % 2 == 1
    first_y, last_y = row == 0, row == cy - 1
    first_z, last_z = lane == 0, lane == cz - 1

    loads = [
        pltpu.make_async_copy(src, dst, in_sem.at[k])
        for k, (src, dst) in enumerate((
            (state_hbm, state_ref), (cond_hbm, cond_ref),
            (cover_hbm, cover_ref), (source_hbm, source_ref),
            (colour_hbm, colour_ref), (spread_hbm, spread_ref), (strength_hbm, strength_ref)))
    ]
    for load in loads:
        load.start()

    barrier = pltpu.get_barrier_semaphore()

    has = (s < n_span - 1, s > 0, w < n_width - 1, w > 0)
    gets = (s > 0, s < n_span - 1, w > 0, w < n_width - 1)
    to = ((s + 1, w), (s - 1, w), (s, w + 1), (s, w - 1))

    def flip(v, bit):
        return v + bit - 2 * bit * (v // bit % 2)

    def signal(sem, moves):
        count = 0
        for ok, t, v in moves:
            @pl.when(ok)
            def _():
                pl.semaphore_signal(sem, inc=1, device_id=(t, v), device_id_type=MESH)
            count = count + ok.astype(jnp.int32)
        return count

    quad = 4
    planes = n_span // quad
    everyone = n_span * n_width
    me = s * n_width + w
    staged = n_width == 2 and 2 <= planes <= 4
    if staged:
        z = s // quad

        def shifted(by):
            return (z + by >= 0) & (z + by < planes), s + by * quad

        def pairs(*moves):
            return [shifted(by) + (v,) for by, v in moves]

        always = s >= 0
        greet = [(always, s, 1 - w), (always, flip(s, 1), w), (always, flip(s, 2), w)]
        greet += pairs((1, w), (-1, w))
        greet += [((s % 2 == 1) & (s < n_span - 1), s + 1, w), ((s % 2 == 0) & (s > 0), s - 1, w)]
        rounds = [
            [(always, s, 1 - w), (always, flip(s, 1), w)],
            [(always, flip(s, 2), w)] + pairs((1, w), (-1, w)),
            [(always, flip(s, 2), w)] + pairs((2, w), (-2, w), (2, 1 - w), (-2, 1 - w)),
        ]
        greeted = signal(barrier, greet)
    else:
        rounds = [[], [], []]
        greeted = everyone - 1

        @pl.loop(1, everyone)
        def _(off):
            other = lax.rem(me + off, everyone)
            pl.semaphore_signal(
                barrier, inc=1, device_id=(other // n_width, other % n_width), device_id_type=MESH)

    def meet(k):
        return signal(met.at[k], rounds[k]) if rounds[k] else 0

    def met_by(k, count):
        if rounds[k]:
            pl.semaphore_wait(met.at[k], count)

    def to_all(buf, ssem, rsem):
        @pl.loop(1, everyone)
        def _(off):
            other = lax.rem(me + off, everyone)
            pltpu.make_async_remote_copy(
                src_ref=buf.at[me], dst_ref=buf.at[me], send_sem=ssem, recv_sem=rsem,
                device_id=(other // n_width, other % n_width), device_id_type=MESH,
            ).start()

    def all_of(buf, sem):
        others = buf.at[pl.ds(0, everyone - 1)]
        pltpu.make_async_copy(others, others, sem).wait()

    def rows_of(ref, *at):
        return jnp.concatenate(
            [ref[at + (pl.ds(v, SUB, stride=nv), slice(None))] for v in range(nv)], axis=-2)

    def split(ref, *at):
        pairs = rows_of(ref, *at, slice(None)).reshape(kp, 2, cy, cz)
        even, odd = pairs[:, 0], pairs[:, 1]
        return jnp.where(p, odd, even), jnp.where(p, even, odd)

    def y_up(v):
        edge = jnp.where(last_y[cy - SUB:], 0.0, pltpu.roll(v[..., :SUB, :], SUB - 1, v.ndim - 2))
        return jnp.concatenate([v[..., SUB:, :], edge], axis=-2)

    def y_down(v):
        edge = jnp.where(first_y[:SUB], 0.0, pltpu.roll(v[..., cy - SUB:, :], 1, v.ndim - 2))
        return jnp.concatenate([edge, v[..., :cy - SUB, :]], axis=-2)

    def yz_sum(v):
        out = y_up(v) + y_down(v)
        out += jnp.where(last_z, 0.0, pltpu.roll(v, cz - 1, v.ndim - 1))
        out += jnp.where(first_z, 0.0, pltpu.roll(v, 1, v.ndim - 1))
        return out

    zero_face = jnp.zeros((1, cy, cz), F32)

    def nb_red(black):
        above = jnp.concatenate([black[1:], zero_face], axis=0)
        below = jnp.concatenate([zero_face, black[:-1]], axis=0)
        return black + jnp.where(p, above, below) + yz_sum(black)

    def nb_black(red):
        above = jnp.concatenate([red[1:], zero_face], axis=0)
        below = jnp.concatenate([zero_face, red[:-1]], axis=0)
        return red + jnp.where(p, below, above) + yz_sum(red)

    def rim(e, i):
        lo, hi = (rows_of(xh, e, k, i) if e == 0 else xh[e, k, i] for k in range(2))
        ylo, yhi = yh[e, 0, i], yh[e, 1, i]
        mid = jnp.zeros((kp - 2, cy, cz), F32)

        def faces(k0, k1, half):
            x_part = jnp.concatenate([k0[None], mid, k1[None]], axis=0)
            low = ylo[half * kp:(half + 1) * kp][:, None, :]
            high = yhi[half * kp:(half + 1) * kp][:, None, :]
            return x_part + jnp.where(first_y, low, 0.0) + jnp.where(last_y, high, 0.0)

        red = faces(jnp.where(p, 0.0, lo), jnp.where(p, hi, 0.0), 1)
        black = faces(jnp.where(p, lo, 0.0), jnp.where(p, 0.0, hi), 0)
        return red, black

    def put_y(e, i, red, black):
        ys[e, 0, i] = jnp.concatenate([red[:, cy - 1, :], black[:, cy - 1, :]], axis=0)
        ys[e, 1, i] = jnp.concatenate([red[:, 0, :], black[:, 0, :]], axis=0)

    def put_x(e, i, red, black):
        xs[e - 1, 0, i] = jnp.where(p, red[kp - 1], black[kp - 1])
        xs[e - 1, 1, i] = jnp.where(p, black[0], red[0])

    pair_of = ions // GROUPS

    def copy(e, k, g):
        own = pl.ds(g * pair_of, pair_of)
        if k >= 2:
            src, dst = ys.at[e, k - 2, own], yh.at[e, k - 2, own]
        else:
            dst = xh.at[e, k, own]
            if e == 0:
                src = state_ref.at[own, cx - 1] if k == 0 else state_ref.at[own, 0]
            else:
                src = xs.at[e - 1, k, own]
        return pltpu.make_async_remote_copy(
            src_ref=src, dst_ref=dst, send_sem=send_sem.at[e, k, g], recv_sem=recv_sem.at[e, k, g],
            device_id=to[k], device_id_type=MESH,
        )

    def cond_copy(k):
        if k >= 2:
            src, dst = ysc.at[k - 2], yhc.at[k - 2]
        else:
            src, dst = cond_ref.at[cx - 1 if k == 0 else 0], xhc.at[k]
        return pltpu.make_async_remote_copy(
            src_ref=src, dst_ref=dst, send_sem=csend.at[k], recv_sem=crecv.at[k],
            device_id=to[k], device_id_type=MESH,
        )

    def send(e, g):
        for k in range(4):
            @pl.when(has[k])
            def _():
                copy(e, k, g).start()

    def receive(e, g):
        for k in range(4):
            @pl.when(gets[k])
            def _():
                copy(e, k, g).wait_recv()

    for k in range(4):
        @pl.when(jnp.logical_not(gets[k]))
        def _():
            for e in range(3):
                if k >= 2:
                    yh[e, k - 2] = jnp.zeros(yh.shape[2:], F32)
                else:
                    xh[e, k] = jnp.zeros(xh.shape[2:], F32)
            if k >= 2:
                yhc[k - 2] = jnp.zeros(yhc.shape[1:], F32)
            else:
                xhc[k] = jnp.zeros(xhc.shape[1:], F32)

    def pack_state(i, _):
        put_y(0, i, *split(state_ref, i))
        return 0

    loads[0].wait()
    lax.fori_loop(0, ions, pack_state, 0)
    pl.semaphore_wait(barrier, greeted)
    for g in range(GROUPS):
        send(0, g)
    expected = meet(0)

    loads[1].wait()
    condp[0], condp[1] = split(cond_ref)
    ysc[0] = jnp.concatenate([condp[0, :, cy - 1, :], condp[1, :, cy - 1, :]], axis=0)
    ysc[1] = jnp.concatenate([condp[0, :, 0, :], condp[1, :, 0, :]], axis=0)
    for load in loads[2:]:
        load.wait()
    coverp[0], coverp[1] = (v.astype(F32) for v in split(cover_ref))

    eighth = lane % COARSEN

    def pack(fields):
        total = None
        for j, v in enumerate(fields):
            pieces = []
            for b in range(0, v.shape[0], cy):
                u = sum(v[b + k * SUB:b + (k + 1) * SUB] for k in range(nv))
                pieces += [jnp.sum(u[r:r + spread_of], axis=0, keepdims=True)
                           for r in range(0, SUB, spread_of)]
            v = jnp.concatenate(pieces, axis=0)
            turned = [v if l == j else pltpu.roll(v, (j - l) % cz, 1) for l in range(COARSEN)]
            while len(turned) > 1:
                turned = [u + t for u, t in zip(turned[::2], turned[1::2])]
            here = eighth[:v.shape[0]] == j
            total = turned[0] if total is None else jnp.where(here, turned[0], total)
        return total

    def local_terms(i, _):
        spread, strength = spread_ref[i], strength_ref[i]
        st = split(state_ref, i)
        src = split(source_ref, i)
        near = (nb_red(st[1]), nb_black(st[0]))
        mass_sum = jnp.zeros((cy, cz), F32)
        for h in range(2):
            coef = spread * condp[h]
            inv = 1.0 / (1.0 + st[h])
            bound = coverp[h] * strength * inv
            mass = INV_STEP + bound * inv
            dg = mass + 6.0 * coef
            diag[h, i] = dg
            c[h, i] = coef / dg
            rhs[h, i] = src[h] - (coef * (6.0 * st[h] - near[h]) + bound * st[h])
            mass_sum += jnp.sum(mass, axis=0)
        mx[i] = mass_sum
        return 0

    lax.fori_loop(0, ions, local_terms, 0)
    cond_sum = jnp.sum(condp[0] + condp[1], axis=0)
    sums = pack([mx[i] for i in range(ions)] + [spread_ref[i] * cond_sum for i in range(ions)])
    low_slot = eighth[:rows] < ions
    coarse_off = pltpu.roll(sums, cz - ions, 1) / COARSEN
    coarse_inv = 1.0 / jnp.where(low_slot, sums + 6.0 * coarse_off, 1.0)
    ops[me] = jnp.where(low_slot, coarse_off * coarse_inv, pltpu.roll(coarse_inv, ions, 1))

    mine = colour_ref[0, 0].astype(F32)

    def sweeps(mask, right, ids):
        coefs = [(c[0, i], c[1, i]) for i in ids]
        red = [mask * ar for ar, _ in right]
        ab = [mask * v for _, v in right]
        ar = list(red)
        black = [v + cc[1] * nb_black(r) for v, cc, r in zip(ab, coefs, red)]
        for _ in range(SWEEPS - 1):
            red = [v + cc[0] * nb_red(u) for v, cc, u in zip(ar, coefs, black)]
            black = [v + cc[1] * nb_black(r) for v, cc, r in zip(ab, coefs, red)]
        return red, black

    def phase_zero(ids):
        for i in ids:
            near = rim(0, i)
            for h in range(2):
                right = rhs[h, i] + spread_ref[i] * condp[h] * near[h]
                rhs[h, i] = right
                a[h, i] = right / diag[h, i]
        reds, blacks = sweeps(1.0 - mine, [(a[0, i], a[1, i]) for i in ids], ids)
        for i, red, black in zip(ids, reds, blacks):
            d[0, i], d[1, i] = red, black
            put_y(1, i, red, black)
            put_x(1, i, red, black)

    met_by(0, expected)
    expected = meet(1)
    for g in range(GROUPS):
        receive(0, g)
        phase_zero(range(g * pair_of, (g + 1) * pair_of))
        send(1, g)
    met_by(1, expected)
    expected = meet(2)
    for k in range(4):
        @pl.when(has[k])
        def _():
            cond_copy(k).start()
    def phase_one(ids):
        right = []
        for i in ids:
            near = rim(1, i)
            right.append((a[0, i] + c[0, i] * near[0], a[1, i] + c[1, i] * near[1]))
        reds, blacks = sweeps(mine, right, ids)
        for i, red, black in zip(ids, reds, blacks):
            red, black = red + d[0, i], black + d[1, i]
            d[0, i], d[1, i] = red, black
            put_y(2, i, red, black)
            put_x(2, i, red, black)
            near = (nb_red(black), nb_black(red))
            total = jnp.zeros((cy, cz), F32)
            for h, v in ((0, red), (1, black)):
                fine = rhs[h, i] - (diag[h, i] * v - spread_ref[i] * condp[h] * near[h])
                rhs[h, i] = fine
                total += jnp.sum(fine, axis=0)
            fx[i] = total

    for g in range(GROUPS):
        receive(1, g)
        if g == GROUPS - 1:
            met_by(2, expected)
            to_all(ops, osend, orecv)
        phase_one(range(g * pair_of, (g + 1) * pair_of))
        send(2, g)

    for k in range(4):
        @pl.when(gets[k])
        def _():
            cond_copy(k).wait_recv()

    def across(k, i):
        face = ys[2, k, i]
        other = jnp.concatenate([face[kp:], face[:kp]], axis=0)
        return spread_ref[i] * jnp.sum(yhc[1 - k] * other, axis=0, keepdims=True)

    def column(i):
        spread = spread_ref[i]
        y_part = jnp.where(first_y, across(1, i), jnp.where(last_y, across(0, i), 0.0))
        return (jnp.concatenate([fx[i], spread * (rows_of(xhc, 0) * xs[1, 1, i])], axis=0),
                jnp.concatenate([spread * (rows_of(xhc, 1) * xs[1, 0, i]), y_part], axis=0))

    columns = [column(i) for i in range(ions)]
    gath[me] = pack([u for u, _ in columns] + [v for _, v in columns])
    to_all(gath, gsend, grecv)

    wide = n_width * rows
    half = n_span // 2

    crow = lax.broadcasted_iota(jnp.int32, (wide, cz), 0)
    slot_low = lax.broadcasted_iota(jnp.int32, (wide, cz), 1) % COARSEN < ions

    def wide_of(v):
        return jnp.concatenate([v[:, k] for k in range(n_width)], axis=1)

    def down(v):
        return pltpu.roll(v, cz - ions, 2)

    def up(v):
        return pltpu.roll(v, ions, 2)

    def fold(low_part, high_part):
        return jnp.where(slot_low, low_part, high_part)

    plane = jnp.zeros((1, wide, cz), F32)
    all_of(ops, orecv)
    o = wide_of(ops[...].reshape(n_span, n_width, rows, cz))
    aj[...] = fold(down(o[:half]), o[half:])
    cj[...] = fold(o[:half], up(o[half:]))
    def face_terms(i, _):
        near = rim(2, i)
        for h in range(2):
            rhs[h, i] += spread_ref[i] * condp[h] * near[h]
        return 0

    for g in range(GROUPS):
        receive(2, g)
    lax.fori_loop(0, ions, face_terms, 0)
    all_of(gath, grecv)
    g = gath[...].reshape(n_span, n_width, 2 * rows, cz)
    plus, minus = wide_of(g[:, :, :rows]), wide_of(g[:, :, rows:])
    y_sum = jnp.where(crow % rows == 0, pltpu.roll(minus, 1, 1), 0.0)
    y_sum = jnp.where(crow % rows == rows - 1, pltpu.roll(minus, wide - 1, 1), y_sum)
    crhs = fold(plus[:half], up(plus[half:]))
    crhs += fold(jnp.concatenate([plane, down(plus[:half - 1])], axis=0), plus[half - 1:-1])
    crhs += fold(minus[1:half + 1], jnp.concatenate([up(minus[half + 1:]), plane], axis=0))
    crhs += fold(down(y_sum[:half]), y_sum[half:])
    aj[...] = crhs * aj[...]
    crow = lax.broadcasted_iota(jnp.int32, (wide, cz), 0)
    clane = lax.broadcasted_iota(jnp.int32, (wide, cz), 1)

    y_plus = jnp.where(crow == wide - 1, 0.0, cj[...])
    y_minus = jnp.where(crow == 0, 0.0, cj[...])
    z_plus = jnp.where(clane >= cz - COARSEN, 0.0, cj[...])
    z_minus = jnp.where(clane < COARSEN, 0.0, cj[...])

    def jacobi(_, e):
        above = jnp.where(slot_low, up_one(e[:1], -1), 0.0)
        below = jnp.where(slot_low, 0.0, up_one(e[half - 1:], 1))
        near = jnp.concatenate([e[1:], above], axis=0) + jnp.concatenate([below, e[:-1]], axis=0)
        total = aj[...] + cj[...] * near
        total += y_plus * pltpu.roll(e, wide - 1, 1) + y_minus * pltpu.roll(e, 1, 1)
        return total + (z_plus * pltpu.roll(e, cz - COARSEN, 2) + z_minus * pltpu.roll(e, COARSEN, 2))

    def up_one(v, sign):
        return pltpu.roll(v, ions if sign > 0 else cz - ions, 2)

    e = lax.fori_loop(0, COARSE_ITERS - 1, jacobi, aj[...], unroll=UNROLL_J)
    ej[0] = plane[0]
    ej[n_span + 1] = plane[0]
    ej[1:half + 1] = e
    ej[half + 1:n_span + 1] = down(e)
    before, here, after = ej[s], ej[s + 1], ej[s + 2]

    def own_rows(v):
        out = v[:rows]
        for k in range(1, n_width):
            out = jnp.where(w == k, v[k * rows:(k + 1) * rows], out)
        return out

    y_low = jnp.zeros((1, cz), F32)
    y_high = jnp.zeros((1, cz), F32)
    for k in range(n_width):
        if k > 0:
            y_low = jnp.where(w == k, here[k * rows - 1:k * rows], y_low)
        if k < n_width - 1:
            y_high = jnp.where(w == k, here[(k + 1) * rows:(k + 1) * rows + 1], y_high)
    packed = jnp.concatenate(
        [own_rows(here), own_rows(before), own_rows(after), y_low, y_high,
         jnp.zeros((16 - 3 * rows - 2, cz), F32)], axis=0)
    for i in range(ions):
        v = jnp.where(eighth[:16] == i, packed, 0.0)
        turned = [v if l == i else pltpu.roll(v, (l - i) % cz, 1) for l in range(COARSEN)]
        while len(turned) > 1:
            turned = [u + t for u, t in zip(turned[::2], turned[1::2])]
        sp[i] = turned[0]

    def tall(v):
        return jnp.concatenate(
            [jnp.broadcast_to(v[j:j + 1], (spread_of, cz)) for j in range(rows)] * nv, axis=0)

    sums = []
    for i in range(ions):
        v = sp[i]
        lift = tall(v[:rows])
        lo, hi = tall(v[rows:2 * rows]), tall(v[2 * rows:3 * rows])
        base = yz_sum(lift) + lift
        base += jnp.where(first_y, v[3 * rows:3 * rows + 1], 0.0)
        base += jnp.where(last_y, v[3 * rows + 1:3 * rows + 2], 0.0)
        numer = jnp.zeros((cy, cz), F32)
        denom = jnp.zeros((cy, cz), F32)
        for h in range(2):
            for k in range(kp):
                side = lift
                low_side = p if h else jnp.logical_not(p)
                high_side = jnp.logical_not(p) if h else p
                if k == 0:
                    side = jnp.where(low_side, lo, side)
                if k == kp - 1:
                    side = jnp.where(high_side, hi, side)
                im = diag[h, i, k] * lift - spread_ref[i] * condp[h, k] * (base + side)
                image[h, i, k] = im
                numer += rhs[h, i, k] * im
                denom += im * im
        sums.append((jnp.sum(numer, axis=0, keepdims=True), jnp.sum(denom, axis=0, keepdims=True)))
    moments = jnp.concatenate([n for n, _ in sums] + [m for _, m in sums], axis=0)
    moments = jnp.sum(moments, axis=1, keepdims=True)
    share = cz // ions
    prow = lax.broadcasted_iota(jnp.int32, (ions, cz), 0)
    mine_of = prow == lax.broadcasted_iota(jnp.int32, (ions, cz), 1) // share
    part[me] = jnp.concatenate(
        [jnp.sum(jnp.where(mine_of, v, 0.0), axis=0, keepdims=True)
         for v in (moments[:ions], moments[ions:])], axis=0)
    to_all(part, psend, precv)

    def put(ref, i, x, value, add=None):
        for v in range(nv):
            at = (i, x, pl.ds(v, SUB, stride=nv), slice(None))
            piece = value[v * SUB:(v + 1) * SUB]
            ref[at] = piece if add is None else add[at] + piece

    def to_rows(i, _):
        for k in range(kp):
            for out, red, black, add in (
                    (up_ref, d[0, i, k], d[1, i, k], state_ref),
                    (res_ref, rhs[0, i, k], rhs[1, i, k], None),
                    (source_ref, image[0, i, k], image[1, i, k], None)):
                put(out, i, 2 * k, jnp.where(p, black, red), add)
                put(out, i, 2 * k + 1, jnp.where(p, red, black), add)
        return 0

    lax.fori_loop(0, ions, to_rows, 0)
    all_of(part, precv)
    whole = jnp.sum(part[...], axis=0)
    weight = whole[:1] / (whole[1:] + EPSILON)
    for i in range(ions):
        wv[i:i + 1] = jnp.broadcast_to(weight[:, i * share:i * share + 1], (1, cz))

    for i in range(ions):
        wt = wv[i:i + 1]
        lifted = wt * jnp.concatenate(
            [jnp.broadcast_to(sp[i, j:j + 1], (COARSEN, cz)) for j in range(rows)], axis=0)
        up_ref[i] = up_ref[i] + lifted
        res_ref[i] = res_ref[i] - wt * source_ref[i]

    for e in range(3):
        for k in range(4):
            @pl.when(has[k])
            def _():
                for g in range(GROUPS):
                    copy(e, k, g).wait_send()
    for k in range(4):
        @pl.when(has[k])
        def _():
            cond_copy(k).wait_send()
    all_of(ops, osend)
    all_of(gath, gsend)
    all_of(part, psend)


def drain(up_ref, res_ref, up_out, res_out, sem):
    copies = [pltpu.make_async_copy(up_ref, up_out, sem.at[0]),
              pltpu.make_async_copy(res_ref, res_out, sem.at[1])]
    for one in copies:
        one.start()
    for one in copies:
        one.wait()


def on_device(n_span, n_width, state, source, conductance, rebar_cover, colour, diffusivity, binding):
    ions, cx, cy, cz = state.shape
    kp = cx // 2
    rows = cy // COARSEN
    half = pltpu.VMEM((2, ions, kp, cy, cz), F32)
    pair = pltpu.VMEM((2, kp, cy, cz), F32)
    vmem = pl.BlockSpec(memory_space=pltpu.VMEM)
    dma = pltpu.SemaphoreType.DMA
    anywhere = pl.BlockSpec(memory_space=pl.ANY)
    hbm = pl.BlockSpec(memory_space=pltpu.HBM)
    face_x = pltpu.VMEM((3, 2, ions, cy, cz), F32)
    face_y = pltpu.VMEM((3, 2, ions, 2 * kp, cz), F32)
    everyone = n_span * n_width
    up, res = pl.pallas_call(
        functools.partial(kernel, n_span, n_width, ions, cx, cy, cz),
        out_shape=(pltpu.VMEM(state.shape, F32),) * 2,
        in_specs=[pl.BlockSpec(memory_space=pltpu.HBM)] * 7,
        out_specs=(vmem, vmem),
        scratch_shapes=[
            pltpu.SMEM((1, 1), jnp.int32), pltpu.SMEM((ions,), F32), pltpu.SMEM((ions,), F32),
            pltpu.VMEM(state.shape, F32), pltpu.VMEM(state.shape, F32),
            pltpu.VMEM(conductance.shape, F32), pltpu.VMEM(conductance.shape, jnp.int32),
            pltpu.VMEM((2, 2, ions, cy, cz), F32), face_x, face_y, face_y,
            pltpu.VMEM((2, 2 * kp, cz), F32),
            pltpu.VMEM((2, cy, cz), F32),
            pltpu.VMEM((2, 2 * kp, cz), F32),
            pltpu.VMEM((everyone, rows, cz), F32),
            pltpu.VMEM((everyone, 2 * rows, cz), F32),
            pltpu.VMEM((everyone, 2, cz), F32),
            pair, pair, half, half, half, half, half, half,
            pltpu.VMEM((ions, cy, cz), F32),
            pltpu.VMEM((ions, cy, cz), F32),
            pltpu.VMEM((n_span // 2, n_width * rows, cz), F32),
            pltpu.VMEM((n_span // 2, n_width * rows, cz), F32),
            pltpu.VMEM((n_span + 2, n_width * rows, cz), F32),
            pltpu.VMEM((ions, 16, cz), F32),
            pltpu.VMEM((ions, cz), F32),
            dma((3, 4, GROUPS)), dma((3, 4, GROUPS)), dma((4,)), dma((4,)),
            dma, dma, dma, dma, dma, dma, dma((7,)), pltpu.SemaphoreType.REGULAR((3,)),
        ],
        compiler_params=pltpu.CompilerParams(
            collective_id=0, has_side_effects=True, vmem_limit_bytes=60 * 1024 * 1024
        ),
    )(state, source, conductance, rebar_cover, colour, diffusivity, binding)
    return pl.pallas_call(
        drain,
        out_shape=(jax.ShapeDtypeStruct(state.shape, F32),) * 2,
        in_specs=[anywhere] * 2,
        out_specs=(hbm, hbm),
        scratch_shapes=[dma((2,))],
        compiler_params=pltpu.CompilerParams(vmem_limit_bytes=1024 * 1024),
    )(up, res)


def solution(mesh):
    in_specs = (
        P(None, "span", "width", None),
        P(None, "span", "width", None),
        P("span", "width", None),
        P("span", "width", None),
        P("span", "width"),
        P(),
        P(),
    )
    out_specs = (P(None, "span", "width", None), P(None, "span", "width", None))
    return jax.shard_map(
        functools.partial(on_device, mesh.shape["span"], mesh.shape["width"]),
        mesh=mesh, in_specs=in_specs, out_specs=out_specs, check_vma=False,
    )
```

```python
import functools

import jax
import jax.numpy as jnp
from jax import lax
from jax.experimental import pallas as pl
from jax.experimental.pallas import tpu as pltpu
from jax.sharding import PartitionSpec as P

COARSEN = 8
SUB = 8
SWEEPS = 4
COARSE_ITERS = 20
INV_STEP = 0.05
EPSILON = 1e-06
MESH = pl.DeviceIdType.MESH
GROUPS = 2
UNROLL_J = 19
F32 = jnp.float32


def kernel(
    n_span, n_width, ions, cx, cy, cz,
    state_hbm, source_hbm, cond_hbm, cover_hbm, colour_hbm, spread_hbm, strength_hbm,
    up_ref, res_ref,
    colour_ref, spread_ref, strength_ref, state_ref, source_ref, cond_ref, cover_ref, xs, xh, ys, yh, ysc, xhc, yhc, ops, gath, part, condp, coverp, rhs, diag, c, a, d, image,
    mx, fx, aj, cj, ej, sp, wv,
    send_sem, recv_sem, csend, crecv, osend, orecv, gsend, grecv, psend, precv, in_sem, met,
):
    s = lax.axis_index("span")
    w = lax.axis_index("width")
    kp = cx // 2
    rows = cy // COARSEN
    nv = cy // SUB
    spread_of = SUB // rows
    slot = lax.broadcasted_iota(jnp.int32, (cy, cz), 0)
    row = slot % SUB * nv + slot // SUB
    lane = lax.broadcasted_iota(jnp.int32, (cy, cz), 1)
    p = (row + lane) % 2 == 1
    first_y, last_y = row == 0, row == cy - 1
    first_z, last_z = lane == 0, lane == cz - 1

    loads = [
        pltpu.make_async_copy(src, dst, in_sem.at[k])
        for k, (src, dst) in enumerate((
            (state_hbm, state_ref), (cond_hbm, cond_ref),
            (cover_hbm, cover_ref), (source_hbm, source_ref),
            (colour_hbm, colour_ref), (spread_hbm, spread_ref), (strength_hbm, strength_ref)))
    ]
    for load in loads:
        load.start()

    barrier = pltpu.get_barrier_semaphore()

    has = (s < n_span - 1, s > 0, w < n_width - 1, w > 0)
    gets = (s > 0, s < n_span - 1, w > 0, w < n_width - 1)
    to = ((s + 1, w), (s - 1, w), (s, w + 1), (s, w - 1))

    def flip(v, bit):
        return v + bit - 2 * bit * (v // bit % 2)

    def signal(sem, moves):
        count = 0
        for ok, t, v in moves:
            @pl.when(ok)
            def _():
                pl.semaphore_signal(sem, inc=1, device_id=(t, v), device_id_type=MESH)
            count = count + ok.astype(jnp.int32)
        return count

    quad = 4
    planes = n_span // quad
    everyone = n_span * n_width
    me = s * n_width + w
    partners = [lax.rem(w + k, n_width) for k in range(1, n_width)]
    staged = n_width == 2 and 2 <= planes <= 4
    if staged:
        z = s // quad

        def shifted(by):
            return (z + by >= 0) & (z + by < planes), s + by * quad

        def pairs(*moves):
            return [shifted(by) + (v,) for by, v in moves]

        always = s >= 0
        greet = [(always, s, 1 - w), (always, flip(s, 1), w), (always, flip(s, 2), w)]
        greet += pairs((1, w), (-1, w))
        greet += [((s % 2 == 1) & (s < n_span - 1), s + 1, w), ((s % 2 == 0) & (s > 0), s - 1, w)]
        rounds = [
            [(always, s, 1 - w), (always, flip(s, 1), w)],
            [(always, flip(s, 2), w)] + pairs((1, w), (-1, w)),
            [(always, flip(s, 2), w)] + pairs((2, w), (-2, w), (2, 1 - w), (-2, 1 - w)),
        ]
        greeted = signal(barrier, greet)
    else:
        rounds = [[], [], []]
        greeted = everyone - 1

        @pl.loop(1, everyone)
        def _(off):
            other = lax.rem(me + off, everyone)
            pl.semaphore_signal(
                barrier, inc=1, device_id=(other // n_width, other % n_width), device_id_type=MESH)

    def meet(k):
        return signal(met.at[k], rounds[k]) if rounds[k] else 0

    def met_by(k, count):
        if rounds[k]:
            pl.semaphore_wait(met.at[k], count)

    def bits_of(v, count):
        return [((v // b % 2) * b, b - (v // b % 2) * b) for b in (1 << k for k in range(count))]

    def far(off):
        at = off // n_width
        return at // quad + at % quad // 2 + at % 2

    span_bits, width_bits = (n_span - 1).bit_length(), (n_width - 1).bit_length()
    listed = everyone == 1 << (span_bits + width_bits) and everyone <= 64
    span_of, width_of = bits_of(s, span_bits), bits_of(w, width_bits)

    def to_all(buf, ssem, rsem):
        def send_to(t, v):
            pltpu.make_async_remote_copy(
                src_ref=buf.at[me], dst_ref=buf.at[me], send_sem=ssem, recv_sem=rsem,
                device_id=(t, v), device_id_type=MESH,
            ).start()

        if listed:
            for off in sorted(range(1, everyone), key=far, reverse=True):
                at_s, at_w = off // n_width, off % n_width
                send_to(sum(pair[at_s >> k & 1] for k, pair in enumerate(span_of)),
                        sum(pair[at_w >> k & 1] for k, pair in enumerate(width_of)))
        else:
            @pl.loop(1, everyone)
            def _(off):
                other = lax.rem(me + off, everyone)
                send_to(other // n_width, other % n_width)

    def ops_along(first, last):
        for off in sorted(range(first, last), key=lambda k: far(k * n_width), reverse=True):
            t = sum(pair[off >> k & 1] for k, pair in enumerate(span_of)) if listed else lax.rem(s + off, n_span)
            pltpu.make_async_remote_copy(
                src_ref=ops.at[w, s], dst_ref=ops.at[w, s], send_sem=osend.at[0], recv_sem=orecv.at[0],
                device_id=(t, w), device_id_type=MESH,
            ).start()

    def ops_across(k):
        return pltpu.make_async_remote_copy(
            src_ref=ops.at[w], dst_ref=ops.at[w], send_sem=osend.at[k], recv_sem=orecv.at[k],
            device_id=(s, partners[k - 1]), device_id_type=MESH,
        )

    def ops_column(sem):
        others = ops.at[w, pl.ds(0, n_span - 1)]
        pltpu.make_async_copy(others, others, sem).wait()

    def all_of(buf, sem):
        others = buf.at[pl.ds(0, everyone - 1)]
        pltpu.make_async_copy(others, others, sem).wait()

    def rows_of(ref, *at):
        return jnp.concatenate(
            [ref[at + (pl.ds(v, SUB, stride=nv), slice(None))] for v in range(nv)], axis=-2)

    def split(ref, *at):
        pairs = rows_of(ref, *at, slice(None)).reshape(kp, 2, cy, cz)
        even, odd = pairs[:, 0], pairs[:, 1]
        return jnp.where(p, odd, even), jnp.where(p, even, odd)

    def y_up(v):
        edge = jnp.where(last_y[cy - SUB:], 0.0, pltpu.roll(v[..., :SUB, :], SUB - 1, v.ndim - 2))
        return jnp.concatenate([v[..., SUB:, :], edge], axis=-2)

    def y_down(v):
        edge = jnp.where(first_y[:SUB], 0.0, pltpu.roll(v[..., cy - SUB:, :], 1, v.ndim - 2))
        return jnp.concatenate([edge, v[..., :cy - SUB, :]], axis=-2)

    def yz_sum(v):
        out = y_up(v) + y_down(v)
        out += jnp.where(last_z, 0.0, pltpu.roll(v, cz - 1, v.ndim - 1))
        out += jnp.where(first_z, 0.0, pltpu.roll(v, 1, v.ndim - 1))
        return out

    zero_face = jnp.zeros((1, cy, cz), F32)

    def nb_red(black):
        above = jnp.concatenate([black[1:], zero_face], axis=0)
        below = jnp.concatenate([zero_face, black[:-1]], axis=0)
        return black + jnp.where(p, above, below) + yz_sum(black)

    def nb_black(red):
        above = jnp.concatenate([red[1:], zero_face], axis=0)
        below = jnp.concatenate([zero_face, red[:-1]], axis=0)
        return red + jnp.where(p, below, above) + yz_sum(red)

    def rim(e, i):
        lo, hi = (rows_of(xh, e, k, i) if e == 0 else xh[e, k, i] for k in range(2))
        ylo, yhi = yh[e, 0, i], yh[e, 1, i]
        mid = jnp.zeros((kp - 2, cy, cz), F32)

        def faces(k0, k1, half):
            x_part = jnp.concatenate([k0[None], mid, k1[None]], axis=0)
            low = ylo[half * kp:(half + 1) * kp][:, None, :]
            high = yhi[half * kp:(half + 1) * kp][:, None, :]
            return x_part + jnp.where(first_y, low, 0.0) + jnp.where(last_y, high, 0.0)

        red = faces(jnp.where(p, 0.0, lo), jnp.where(p, hi, 0.0), 1)
        black = faces(jnp.where(p, lo, 0.0), jnp.where(p, 0.0, hi), 0)
        return red, black

    def put_y(e, i, red, black):
        ys[e, 0, i] = jnp.concatenate([red[:, cy - 1, :], black[:, cy - 1, :]], axis=0)
        ys[e, 1, i] = jnp.concatenate([red[:, 0, :], black[:, 0, :]], axis=0)

    def put_x(e, i, red, black):
        xs[e - 1, 0, i] = jnp.where(p, red[kp - 1], black[kp - 1])
        xs[e - 1, 1, i] = jnp.where(p, black[0], red[0])

    pair_of = ions // GROUPS

    def copy(e, k, g):
        own = pl.ds(g * pair_of, pair_of)
        if k >= 2:
            src, dst = ys.at[e, k - 2, own], yh.at[e, k - 2, own]
        else:
            dst = xh.at[e, k, own]
            if e == 0:
                src = state_ref.at[own, cx - 1] if k == 0 else state_ref.at[own, 0]
            else:
                src = xs.at[e - 1, k, own]
        return pltpu.make_async_remote_copy(
            src_ref=src, dst_ref=dst, send_sem=send_sem.at[e, k, g], recv_sem=recv_sem.at[e, k, g],
            device_id=to[k], device_id_type=MESH,
        )

    def cond_copy(k):
        if k >= 2:
            src, dst = ysc.at[k - 2], yhc.at[k - 2]
        else:
            src, dst = cond_ref.at[cx - 1 if k == 0 else 0], xhc.at[k]
        return pltpu.make_async_remote_copy(
            src_ref=src, dst_ref=dst, send_sem=csend.at[k], recv_sem=crecv.at[k],
            device_id=to[k], device_id_type=MESH,
        )

    def send(e, g):
        for k in range(4):
            @pl.when(has[k])
            def _():
                copy(e, k, g).start()

    def receive(e, g):
        for k in range(4):
            @pl.when(gets[k])
            def _():
                copy(e, k, g).wait_recv()

    for k in range(4):
        @pl.when(jnp.logical_not(gets[k]))
        def _():
            for e in range(3):
                if k >= 2:
                    yh[e, k - 2] = jnp.zeros(yh.shape[2:], F32)
                else:
                    xh[e, k] = jnp.zeros(xh.shape[2:], F32)
            if k >= 2:
                yhc[k - 2] = jnp.zeros(yhc.shape[1:], F32)
            else:
                xhc[k] = jnp.zeros(xhc.shape[1:], F32)

    def pack_state(i, _):
        put_y(0, i, *split(state_ref, i))
        return 0

    loads[0].wait()
    lax.fori_loop(0, ions, pack_state, 0)
    pl.semaphore_wait(barrier, greeted)
    for g in range(GROUPS):
        send(0, g)
    expected = meet(0)

    loads[1].wait()
    condp[0], condp[1] = split(cond_ref)
    ysc[0] = jnp.concatenate([condp[0, :, cy - 1, :], condp[1, :, cy - 1, :]], axis=0)
    ysc[1] = jnp.concatenate([condp[0, :, 0, :], condp[1, :, 0, :]], axis=0)
    for load in loads[2:]:
        load.wait()
    coverp[0], coverp[1] = (v.astype(F32) for v in split(cover_ref))

    eighth = lane % COARSEN

    def pack(fields):
        total = None
        for j, v in enumerate(fields):
            pieces = []
            for b in range(0, v.shape[0], cy):
                u = sum(v[b + k * SUB:b + (k + 1) * SUB] for k in range(nv))
                pieces += [jnp.sum(u[r:r + spread_of], axis=0, keepdims=True)
                           for r in range(0, SUB, spread_of)]
            v = jnp.concatenate(pieces, axis=0)
            turned = [v if l == j else pltpu.roll(v, (j - l) % cz, 1) for l in range(COARSEN)]
            while len(turned) > 1:
                turned = [u + t for u, t in zip(turned[::2], turned[1::2])]
            here = eighth[:v.shape[0]] == j
            total = turned[0] if total is None else jnp.where(here, turned[0], total)
        return total

    def local_terms(i, _):
        spread, strength = spread_ref[i], strength_ref[i]
        st = split(state_ref, i)
        src = split(source_ref, i)
        near = (nb_red(st[1]), nb_black(st[0]))
        mass_sum = jnp.zeros((cy, cz), F32)
        for h in range(2):
            coef = spread * condp[h]
            inv = 1.0 / (1.0 + st[h])
            bound = coverp[h] * strength * inv
            mass = INV_STEP + bound * inv
            dg = mass + 6.0 * coef
            diag[h, i] = dg
            c[h, i] = coef / dg
            a[h, i] = (src[h] - (coef * (6.0 * st[h] - near[h]) + bound * st[h])) / dg
            mass_sum += jnp.sum(mass, axis=0)
        mx[i] = mass_sum
        return 0

    lax.fori_loop(0, ions, local_terms, 0)
    cond_sum = jnp.sum(condp[0] + condp[1], axis=0)
    sums = pack([mx[i] for i in range(ions)] + [spread_ref[i] * cond_sum for i in range(ions)])
    low_slot = eighth[:rows] < ions
    coarse_off = pltpu.roll(sums, cz - ions, 1) / COARSEN
    coarse_inv = 1.0 / jnp.where(low_slot, sums + 6.0 * coarse_off, 1.0)
    ops[w, s] = jnp.where(low_slot, coarse_off * coarse_inv, pltpu.roll(coarse_inv, ions, 1))

    mine = colour_ref[0, 0].astype(F32)

    def sweeps(mask, right, ids):
        coefs = [(c[0, i], c[1, i]) for i in ids]
        red = [mask * ar for ar, _ in right]
        ab = [mask * v for _, v in right]
        ar = list(red)
        black = [v + cc[1] * nb_black(r) for v, cc, r in zip(ab, coefs, red)]
        for _ in range(SWEEPS - 1):
            red = [v + cc[0] * nb_red(u) for v, cc, u in zip(ar, coefs, black)]
            black = [v + cc[1] * nb_black(r) for v, cc, r in zip(ab, coefs, red)]
        return red, black

    def phase_zero(ids):
        for i in ids:
            near = rim(0, i)
            for h in range(2):
                a[h, i] = a[h, i] + c[h, i] * near[h]
        reds, blacks = sweeps(1.0 - mine, [(a[0, i], a[1, i]) for i in ids], ids)
        for i, red, black in zip(ids, reds, blacks):
            d[0, i], d[1, i] = red, black
            put_y(1, i, red, black)
            put_x(1, i, red, black)

    met_by(0, expected)
    expected = meet(1)
    for g in range(GROUPS):
        receive(0, g)
        phase_zero(range(g * pair_of, (g + 1) * pair_of))
        send(1, g)
    met_by(1, expected)
    expected = meet(2)
    for k in range(4):
        @pl.when(has[k])
        def _():
            cond_copy(k).start()
    def phase_one(ids):
        right = []
        for i in ids:
            near = rim(1, i)
            right.append((a[0, i] + c[0, i] * near[0], a[1, i] + c[1, i] * near[1]))
        reds, blacks = sweeps(mine, right, ids)
        for i, red, black in zip(ids, reds, blacks):
            red, black = red + d[0, i], black + d[1, i]
            d[0, i], d[1, i] = red, black
            put_y(2, i, red, black)
            put_x(2, i, red, black)
            fine = diag[0, i] * (a[0, i] + c[0, i] * nb_red(black) - red)
            rhs[0, i] = fine
            still = -mine * (spread_ref[i] * condp[1] * rim(1, i)[1])
            rhs[1, i] = still
            fx[i] = jnp.sum(fine + still, axis=0)

    for g in range(GROUPS):
        receive(1, g)
        if g == GROUPS - 1:
            met_by(2, expected)
            ops_along(1, n_span)
        phase_one(range(g * pair_of, (g + 1) * pair_of))
        send(2, g)

    for k in range(4):
        @pl.when(gets[k])
        def _():
            cond_copy(k).wait_recv()

    def across(k, i):
        face = ys[2, k, i]
        other = jnp.concatenate([face[kp:], face[:kp]], axis=0)
        return spread_ref[i] * jnp.sum(yhc[1 - k] * other, axis=0, keepdims=True)

    def column(i):
        spread = spread_ref[i]
        y_part = jnp.where(first_y, across(1, i), jnp.where(last_y, across(0, i), 0.0))
        return (jnp.concatenate([fx[i], spread * (rows_of(xhc, 0) * xs[1, 1, i])], axis=0),
                jnp.concatenate([spread * (rows_of(xhc, 1) * xs[1, 0, i]), y_part], axis=0))

    columns = [column(i) for i in range(ions)]
    gath[me] = pack([u for u, _ in columns] + [v for _, v in columns])
    to_all(gath, gsend, grecv)
    ops_column(orecv.at[0])
    for k in range(1, n_width):
        ops_across(k).start()

    wide = n_width * rows
    half = n_span // 2

    crow = lax.broadcasted_iota(jnp.int32, (wide, cz), 0)
    slot_low = lax.broadcasted_iota(jnp.int32, (wide, cz), 1) % COARSEN < ions

    def wide_of(v):
        return jnp.concatenate([v[:, k] for k in range(n_width)], axis=1)

    def down(v):
        return pltpu.roll(v, cz - ions, 2)

    def up(v):
        return pltpu.roll(v, ions, 2)

    def fold(low_part, high_part):
        return jnp.where(slot_low, low_part, high_part)

    plane = jnp.zeros((1, wide, cz), F32)
    for k in range(1, n_width):
        ops_across(k).wait_recv()
    o = jnp.concatenate([ops[k] for k in range(n_width)], axis=1)
    aj[...] = fold(down(o[:half]), o[half:])
    cj[...] = fold(o[:half], up(o[half:]))
    def face_terms(i, _):
        near = rim(2, i)
        for h in range(2):
            rhs[h, i] += spread_ref[i] * condp[h] * near[h]
        return 0

    for g in range(GROUPS):
        receive(2, g)
    lax.fori_loop(0, ions, face_terms, 0)
    all_of(gath, grecv)
    g = gath[...].reshape(n_span, n_width, 2 * rows, cz)
    plus, minus = wide_of(g[:, :, :rows]), wide_of(g[:, :, rows:])
    y_sum = jnp.where(crow % rows == 0, pltpu.roll(minus, 1, 1), 0.0)
    y_sum = jnp.where(crow % rows == rows - 1, pltpu.roll(minus, wide - 1, 1), y_sum)
    crhs = fold(plus[:half], up(plus[half:]))
    crhs += fold(jnp.concatenate([plane, down(plus[:half - 1])], axis=0), plus[half - 1:-1])
    crhs += fold(minus[1:half + 1], jnp.concatenate([up(minus[half + 1:]), plane], axis=0))
    crhs += fold(down(y_sum[:half]), y_sum[half:])
    aj[...] = crhs * aj[...]
    crow = lax.broadcasted_iota(jnp.int32, (wide, cz), 0)
    clane = lax.broadcasted_iota(jnp.int32, (wide, cz), 1)

    y_plus = jnp.where(crow == wide - 1, 0.0, cj[...])
    y_minus = jnp.where(crow == 0, 0.0, cj[...])
    z_plus = jnp.where(clane >= cz - COARSEN, 0.0, cj[...])
    z_minus = jnp.where(clane < COARSEN, 0.0, cj[...])

    def jacobi(_, e):
        above = jnp.where(slot_low, up_one(e[:1], -1), 0.0)
        below = jnp.where(slot_low, 0.0, up_one(e[half - 1:], 1))
        near = jnp.concatenate([e[1:], above], axis=0) + jnp.concatenate([below, e[:-1]], axis=0)
        total = aj[...] + cj[...] * near
        total += y_plus * pltpu.roll(e, wide - 1, 1) + y_minus * pltpu.roll(e, 1, 1)
        return total + (z_plus * pltpu.roll(e, cz - COARSEN, 2) + z_minus * pltpu.roll(e, COARSEN, 2))

    def up_one(v, sign):
        return pltpu.roll(v, ions if sign > 0 else cz - ions, 2)

    e = lax.fori_loop(0, COARSE_ITERS - 1, jacobi, aj[...], unroll=UNROLL_J)
    ej[0] = plane[0]
    ej[n_span + 1] = plane[0]
    ej[1:half + 1] = e
    ej[half + 1:n_span + 1] = down(e)
    before, here, after = ej[s], ej[s + 1], ej[s + 2]

    def own_rows(v):
        out = v[:rows]
        for k in range(1, n_width):
            out = jnp.where(w == k, v[k * rows:(k + 1) * rows], out)
        return out

    y_low = jnp.zeros((1, cz), F32)
    y_high = jnp.zeros((1, cz), F32)
    for k in range(n_width):
        if k > 0:
            y_low = jnp.where(w == k, here[k * rows - 1:k * rows], y_low)
        if k < n_width - 1:
            y_high = jnp.where(w == k, here[(k + 1) * rows:(k + 1) * rows + 1], y_high)
    packed = jnp.concatenate(
        [own_rows(here), own_rows(before), own_rows(after), y_low, y_high,
         jnp.zeros((16 - 3 * rows - 2, cz), F32)], axis=0)
    for i in range(ions):
        v = jnp.where(eighth[:16] == i, packed, 0.0)
        turned = [v if l == i else pltpu.roll(v, (l - i) % cz, 1) for l in range(COARSEN)]
        while len(turned) > 1:
            turned = [u + t for u, t in zip(turned[::2], turned[1::2])]
        sp[i] = turned[0]

    def tall(v):
        return jnp.concatenate(
            [jnp.broadcast_to(v[j:j + 1], (spread_of, cz)) for j in range(rows)] * nv, axis=0)

    sums = []
    for i in range(ions):
        v = sp[i]
        lift = tall(v[:rows])
        lo, hi = tall(v[rows:2 * rows]), tall(v[2 * rows:3 * rows])
        base = yz_sum(lift) + lift
        base += jnp.where(first_y, v[3 * rows:3 * rows + 1], 0.0)
        base += jnp.where(last_y, v[3 * rows + 1:3 * rows + 2], 0.0)
        numer = jnp.zeros((cy, cz), F32)
        denom = jnp.zeros((cy, cz), F32)
        for h in range(2):
            for k in range(kp):
                side = lift
                low_side = p if h else jnp.logical_not(p)
                high_side = jnp.logical_not(p) if h else p
                if k == 0:
                    side = jnp.where(low_side, lo, side)
                if k == kp - 1:
                    side = jnp.where(high_side, hi, side)
                im = diag[h, i, k] * lift - spread_ref[i] * condp[h, k] * (base + side)
                image[h, i, k] = im
                numer += rhs[h, i, k] * im
                denom += im * im
        sums.append((jnp.sum(numer, axis=0, keepdims=True), jnp.sum(denom, axis=0, keepdims=True)))
    moments = jnp.concatenate([n for n, _ in sums] + [m for _, m in sums], axis=0)
    moments = jnp.sum(moments, axis=1, keepdims=True)
    share = cz // ions
    prow = lax.broadcasted_iota(jnp.int32, (ions, cz), 0)
    mine_of = prow == lax.broadcasted_iota(jnp.int32, (ions, cz), 1) // share
    part[me] = jnp.concatenate(
        [jnp.sum(jnp.where(mine_of, v, 0.0), axis=0, keepdims=True)
         for v in (moments[:ions], moments[ions:])], axis=0)
    to_all(part, psend, precv)

    def put(ref, i, x, value, add=None):
        for v in range(nv):
            at = (i, x, pl.ds(v, SUB, stride=nv), slice(None))
            piece = value[v * SUB:(v + 1) * SUB]
            ref[at] = piece if add is None else add[at] + piece

    def to_rows(i, _):
        for k in range(kp):
            for out, red, black, add in (
                    (up_ref, d[0, i, k], d[1, i, k], state_ref),
                    (res_ref, rhs[0, i, k], rhs[1, i, k], None),
                    (source_ref, image[0, i, k], image[1, i, k], None)):
                put(out, i, 2 * k, jnp.where(p, black, red), add)
                put(out, i, 2 * k + 1, jnp.where(p, red, black), add)
        return 0

    lax.fori_loop(0, ions, to_rows, 0)
    all_of(part, precv)
    whole = jnp.sum(part[...], axis=0)
    weight = whole[:1] / (whole[1:] + EPSILON)
    for i in range(ions):
        wv[i:i + 1] = jnp.broadcast_to(weight[:, i * share:i * share + 1], (1, cz))

    for i in range(ions):
        wt = wv[i:i + 1]
        lifted = wt * jnp.concatenate(
            [jnp.broadcast_to(sp[i, j:j + 1], (COARSEN, cz)) for j in range(rows)], axis=0)
        up_ref[i] = up_ref[i] + lifted
        res_ref[i] = res_ref[i] - wt * source_ref[i]

    for e in range(3):
        for k in range(4):
            @pl.when(has[k])
            def _():
                for g in range(GROUPS):
                    copy(e, k, g).wait_send()
    for k in range(4):
        @pl.when(has[k])
        def _():
            cond_copy(k).wait_send()
    ops_column(osend.at[0])
    for k in range(1, n_width):
        ops_across(k).wait_send()
    all_of(gath, gsend)
    all_of(part, psend)


def drain(up_ref, res_ref, up_out, res_out, sem):
    copies = [pltpu.make_async_copy(up_ref, up_out, sem.at[0]),
              pltpu.make_async_copy(res_ref, res_out, sem.at[1])]
    for one in copies:
        one.start()
    for one in copies:
        one.wait()


def on_device(n_span, n_width, state, source, conductance, rebar_cover, colour, diffusivity, binding):
    ions, cx, cy, cz = state.shape
    kp = cx // 2
    rows = cy // COARSEN
    half = pltpu.VMEM((2, ions, kp, cy, cz), F32)
    pair = pltpu.VMEM((2, kp, cy, cz), F32)
    vmem = pl.BlockSpec(memory_space=pltpu.VMEM)
    dma = pltpu.SemaphoreType.DMA
    anywhere = pl.BlockSpec(memory_space=pl.ANY)
    hbm = pl.BlockSpec(memory_space=pltpu.HBM)
    face_x = pltpu.VMEM((3, 2, ions, cy, cz), F32)
    face_y = pltpu.VMEM((3, 2, ions, 2 * kp, cz), F32)
    everyone = n_span * n_width
    up, res = pl.pallas_call(
        functools.partial(kernel, n_span, n_width, ions, cx, cy, cz),
        out_shape=(pltpu.VMEM(state.shape, F32),) * 2,
        in_specs=[pl.BlockSpec(memory_space=pltpu.HBM)] * 7,
        out_specs=(vmem, vmem),
        scratch_shapes=[
            pltpu.SMEM((1, 1), jnp.int32), pltpu.SMEM((ions,), F32), pltpu.SMEM((ions,), F32),
            pltpu.VMEM(state.shape, F32), pltpu.VMEM(state.shape, F32),
            pltpu.VMEM(conductance.shape, F32), pltpu.VMEM(conductance.shape, jnp.int32),
            pltpu.VMEM((2, 2, ions, cy, cz), F32), face_x, face_y, face_y,
            pltpu.VMEM((2, 2 * kp, cz), F32),
            pltpu.VMEM((2, cy, cz), F32),
            pltpu.VMEM((2, 2 * kp, cz), F32),
            pltpu.VMEM((n_width, n_span, rows, cz), F32),
            pltpu.VMEM((everyone, 2 * rows, cz), F32),
            pltpu.VMEM((everyone, 2, cz), F32),
            pair, pair, half, half, half, half, half, half,
            pltpu.VMEM((ions, cy, cz), F32),
            pltpu.VMEM((ions, cy, cz), F32),
            pltpu.VMEM((n_span // 2, n_width * rows, cz), F32),
            pltpu.VMEM((n_span // 2, n_width * rows, cz), F32),
            pltpu.VMEM((n_span + 2, n_width * rows, cz), F32),
            pltpu.VMEM((ions, 16, cz), F32),
            pltpu.VMEM((ions, cz), F32),
            dma((3, 4, GROUPS)), dma((3, 4, GROUPS)), dma((4,)), dma((4,)),
            dma((n_width,)), dma((n_width,)), dma, dma, dma, dma, dma((7,)), pltpu.SemaphoreType.REGULAR((3,)),
        ],
        compiler_params=pltpu.CompilerParams(
            collective_id=0, has_side_effects=True, vmem_limit_bytes=60 * 1024 * 1024
        ),
    )(state, source, conductance, rebar_cover, colour, diffusivity, binding)
    return pl.pallas_call(
        drain,
        out_shape=(jax.ShapeDtypeStruct(state.shape, F32),) * 2,
        in_specs=[anywhere] * 2,
        out_specs=(hbm, hbm),
        scratch_shapes=[dma((2,))],
        compiler_params=pltpu.CompilerParams(vmem_limit_bytes=1024 * 1024),
    )(up, res)


def solution(mesh):
    in_specs = (
        P(None, "span", "width", None),
        P(None, "span", "width", None),
        P("span", "width", None),
        P("span", "width", None),
        P("span", "width"),
        P(),
        P(),
    )
    out_specs = (P(None, "span", "width", None), P(None, "span", "width", None))
    return jax.shard_map(
        functools.partial(on_device, mesh.shape["span"], mesh.shape["width"]),
        mesh=mesh, in_specs=in_specs, out_specs=out_specs, check_vma=False,
    )
```

```python
import functools

import jax
import jax.numpy as jnp
from jax import lax
from jax.experimental import pallas as pl
from jax.experimental.pallas import tpu as pltpu
from jax.sharding import PartitionSpec as P

COARSEN = 8
SUB = 8
SWEEPS = 4
COARSE_ITERS = 20
INV_STEP = 0.05
EPSILON = 1e-06
MESH = pl.DeviceIdType.MESH
GROUPS = 2
UNROLL_J = 19
F32 = jnp.float32


def kernel(
    n_span, n_width, ions, cx, cy, cz,
    state_hbm, source_hbm, cond_hbm, cover_hbm, colour_hbm, spread_hbm, strength_hbm,
    up_ref, res_ref,
    colour_ref, spread_ref, strength_ref, state_ref, source_ref, cond_ref, cover_ref, xs, xh, ys, yh, ysc, xhc, yhc, ops, gath, part, condp, coverp, rhs, diag, c, a, d, image,
    mx, fx, aj, cj, ej, sp, wv,
    send_sem, recv_sem, csend, crecv, osend, orecv, gsend, grecv, psend, precv, in_sem, met,
):
    s = lax.axis_index("span")
    w = lax.axis_index("width")
    kp = cx // 2
    rows = cy // COARSEN
    nv = cy // SUB
    spread_of = SUB // rows
    slot = lax.broadcasted_iota(jnp.int32, (cy, cz), 0)
    row = slot % SUB * nv + slot // SUB
    lane = lax.broadcasted_iota(jnp.int32, (cy, cz), 1)
    p = (row + lane) % 2 == 1
    first_y, last_y = row == 0, row == cy - 1
    first_z, last_z = lane == 0, lane == cz - 1

    loads = [
        pltpu.make_async_copy(src, dst, in_sem.at[k])
        for k, (src, dst) in enumerate((
            (state_hbm, state_ref), (cond_hbm, cond_ref),
            (cover_hbm, cover_ref), (source_hbm, source_ref),
            (colour_hbm, colour_ref), (spread_hbm, spread_ref), (strength_hbm, strength_ref)))
    ]
    for load in loads:
        load.start()

    barrier = pltpu.get_barrier_semaphore()

    has = (s < n_span - 1, s > 0, w < n_width - 1, w > 0)
    gets = (s > 0, s < n_span - 1, w > 0, w < n_width - 1)
    to = ((s + 1, w), (s - 1, w), (s, w + 1), (s, w - 1))

    def flip(v, bit):
        return v + bit - 2 * bit * (v // bit % 2)

    def signal(sem, moves):
        count = 0
        for ok, t, v in moves:
            @pl.when(ok)
            def _():
                pl.semaphore_signal(sem, inc=1, device_id=(t, v), device_id_type=MESH)
            count = count + ok.astype(jnp.int32)
        return count

    quad = 4
    planes = n_span // quad
    everyone = n_span * n_width
    me = s * n_width + w
    partners = [lax.rem(w + k, n_width) for k in range(1, n_width)]
    staged = n_width == 2 and 2 <= planes <= 4
    if staged:
        z = s // quad

        def shifted(by):
            return (z + by >= 0) & (z + by < planes), s + by * quad

        def pairs(*moves):
            return [shifted(by) + (v,) for by, v in moves]

        always = s >= 0
        greet = [(always, s, 1 - w), (always, flip(s, 1), w), (always, flip(s, 2), w)]
        greet += pairs((1, w), (-1, w))
        greet += [((s % 2 == 1) & (s < n_span - 1), s + 1, w), ((s % 2 == 0) & (s > 0), s - 1, w)]
        rounds = [
            [(always, s, 1 - w), (always, flip(s, 1), w)],
            [(always, flip(s, 2), w)] + pairs((1, w), (-1, w)),
            [(always, flip(s, 2), w)] + pairs((2, w), (-2, w), (2, 1 - w), (-2, 1 - w)),
        ]
        greeted = signal(barrier, greet)
    else:
        rounds = [[], [], []]
        greeted = everyone - 1

        @pl.loop(1, everyone)
        def _(off):
            other = lax.rem(me + off, everyone)
            pl.semaphore_signal(
                barrier, inc=1, device_id=(other // n_width, other % n_width), device_id_type=MESH)

    def meet(k):
        return signal(met.at[k], rounds[k]) if rounds[k] else 0

    def met_by(k, count):
        if rounds[k]:
            pl.semaphore_wait(met.at[k], count)

    def bits_of(v, count):
        return [((v // b % 2) * b, b - (v // b % 2) * b) for b in (1 << k for k in range(count))]

    def far(off):
        at = off // n_width
        return at // quad + at % quad // 2 + at % 2

    span_bits, width_bits = (n_span - 1).bit_length(), (n_width - 1).bit_length()
    listed = everyone == 1 << (span_bits + width_bits) and everyone <= 64
    span_of, width_of = bits_of(s, span_bits), bits_of(w, width_bits)

    def to_all(buf, ssem, rsem):
        def send_to(t, v):
            pltpu.make_async_remote_copy(
                src_ref=buf.at[me], dst_ref=buf.at[me], send_sem=ssem, recv_sem=rsem,
                device_id=(t, v), device_id_type=MESH,
            ).start()

        if listed:
            for off in sorted(range(1, everyone), key=far, reverse=True):
                at_s, at_w = off // n_width, off % n_width
                send_to(sum(pair[at_s >> k & 1] for k, pair in enumerate(span_of)),
                        sum(pair[at_w >> k & 1] for k, pair in enumerate(width_of)))
        else:
            @pl.loop(1, everyone)
            def _(off):
                other = lax.rem(me + off, everyone)
                send_to(other // n_width, other % n_width)

    def ops_along(first, last):
        for off in sorted(range(first, last), key=lambda k: far(k * n_width), reverse=True):
            t = sum(pair[off >> k & 1] for k, pair in enumerate(span_of)) if listed else lax.rem(s + off, n_span)
            pltpu.make_async_remote_copy(
                src_ref=ops.at[w, s], dst_ref=ops.at[w, s], send_sem=osend.at[0], recv_sem=orecv.at[0],
                device_id=(t, w), device_id_type=MESH,
            ).start()

    def ops_across(k):
        return pltpu.make_async_remote_copy(
            src_ref=ops.at[w], dst_ref=ops.at[w], send_sem=osend.at[k], recv_sem=orecv.at[k],
            device_id=(s, partners[k - 1]), device_id_type=MESH,
        )

    def ops_column(sem):
        others = ops.at[w, pl.ds(0, n_span - 1)]
        pltpu.make_async_copy(others, others, sem).wait()

    def all_of(buf, sem):
        others = buf.at[pl.ds(0, everyone - 1)]
        pltpu.make_async_copy(others, others, sem).wait()

    def rows_of(ref, *at):
        return jnp.concatenate(
            [ref[at + (pl.ds(v, SUB, stride=nv), slice(None))] for v in range(nv)], axis=-2)

    def split(ref, *at):
        pairs = rows_of(ref, *at, slice(None)).reshape(kp, 2, cy, cz)
        even, odd = pairs[:, 0], pairs[:, 1]
        return jnp.where(p, odd, even), jnp.where(p, even, odd)

    def y_up(v):
        edge = jnp.where(last_y[cy - SUB:], 0.0, pltpu.roll(v[..., :SUB, :], SUB - 1, v.ndim - 2))
        return jnp.concatenate([v[..., SUB:, :], edge], axis=-2)

    def y_down(v):
        edge = jnp.where(first_y[:SUB], 0.0, pltpu.roll(v[..., cy - SUB:, :], 1, v.ndim - 2))
        return jnp.concatenate([edge, v[..., :cy - SUB, :]], axis=-2)

    def yz_sum(v):
        out = y_up(v) + y_down(v)
        out += jnp.where(last_z, 0.0, pltpu.roll(v, cz - 1, v.ndim - 1))
        out += jnp.where(first_z, 0.0, pltpu.roll(v, 1, v.ndim - 1))
        return out

    zero_face = jnp.zeros((1, cy, cz), F32)

    def nb_red(black):
        above = jnp.concatenate([black[1:], zero_face], axis=0)
        below = jnp.concatenate([zero_face, black[:-1]], axis=0)
        return black + jnp.where(p, above, below) + yz_sum(black)

    def nb_black(red):
        above = jnp.concatenate([red[1:], zero_face], axis=0)
        below = jnp.concatenate([zero_face, red[:-1]], axis=0)
        return red + jnp.where(p, below, above) + yz_sum(red)

    def rim(e, i):
        lo, hi = (rows_of(xh, e, k, i) if e == 0 else xh[e, k, i] for k in range(2))
        ylo, yhi = yh[e, 0, i], yh[e, 1, i]
        mid = jnp.zeros((kp - 2, cy, cz), F32)

        def faces(k0, k1, half):
            x_part = jnp.concatenate([k0[None], mid, k1[None]], axis=0)
            low = ylo[half * kp:(half + 1) * kp][:, None, :]
            high = yhi[half * kp:(half + 1) * kp][:, None, :]
            return x_part + jnp.where(first_y, low, 0.0) + jnp.where(last_y, high, 0.0)

        red = faces(jnp.where(p, 0.0, lo), jnp.where(p, hi, 0.0), 1)
        black = faces(jnp.where(p, lo, 0.0), jnp.where(p, 0.0, hi), 0)
        return red, black

    def put_y(e, i, red, black):
        ys[e, 0, i] = jnp.concatenate([red[:, cy - 1, :], black[:, cy - 1, :]], axis=0)
        ys[e, 1, i] = jnp.concatenate([red[:, 0, :], black[:, 0, :]], axis=0)

    def put_x(e, i, red, black):
        xs[e - 1, 0, i] = jnp.where(p, red[kp - 1], black[kp - 1])
        xs[e - 1, 1, i] = jnp.where(p, black[0], red[0])

    pair_of = ions // GROUPS

    def copy(e, k, g):
        own = pl.ds(g * pair_of, pair_of)
        if k >= 2:
            src, dst = ys.at[e, k - 2, own], yh.at[e, k - 2, own]
        else:
            dst = xh.at[e, k, own]
            if e == 0:
                src = state_ref.at[own, cx - 1] if k == 0 else state_ref.at[own, 0]
            else:
                src = xs.at[e - 1, k, own]
        return pltpu.make_async_remote_copy(
            src_ref=src, dst_ref=dst, send_sem=send_sem.at[e, k, g], recv_sem=recv_sem.at[e, k, g],
            device_id=to[k], device_id_type=MESH,
        )

    def cond_copy(k):
        if k >= 2:
            src, dst = ysc.at[k - 2], yhc.at[k - 2]
        else:
            src, dst = cond_ref.at[cx - 1 if k == 0 else 0], xhc.at[k]
        return pltpu.make_async_remote_copy(
            src_ref=src, dst_ref=dst, send_sem=csend.at[k], recv_sem=crecv.at[k],
            device_id=to[k], device_id_type=MESH,
        )

    def send(e, g):
        for k in range(4):
            @pl.when(has[k])
            def _():
                copy(e, k, g).start()

    def receive(e, g):
        for k in range(4):
            @pl.when(gets[k])
            def _():
                copy(e, k, g).wait_recv()

    for k in range(4):
        @pl.when(jnp.logical_not(gets[k]))
        def _():
            for e in range(3):
                if k >= 2:
                    yh[e, k - 2] = jnp.zeros(yh.shape[2:], F32)
                else:
                    xh[e, k] = jnp.zeros(xh.shape[2:], F32)
            if k >= 2:
                yhc[k - 2] = jnp.zeros(yhc.shape[1:], F32)
            else:
                xhc[k] = jnp.zeros(xhc.shape[1:], F32)

    def pack_state(i, _):
        put_y(0, i, *split(state_ref, i))
        return 0

    loads[0].wait()
    lax.fori_loop(0, ions, pack_state, 0)
    pl.semaphore_wait(barrier, greeted)
    for g in range(GROUPS):
        send(0, g)
    expected = meet(0)

    loads[1].wait()
    condp[0], condp[1] = split(cond_ref)
    ysc[0] = jnp.concatenate([condp[0, :, cy - 1, :], condp[1, :, cy - 1, :]], axis=0)
    ysc[1] = jnp.concatenate([condp[0, :, 0, :], condp[1, :, 0, :]], axis=0)
    for load in loads[2:]:
        load.wait()
    coverp[0], coverp[1] = (v.astype(F32) for v in split(cover_ref))

    eighth = lane % COARSEN

    def pack(fields):
        total = None
        for j, v in enumerate(fields):
            pieces = []
            for b in range(0, v.shape[0], cy):
                u = sum(v[b + k * SUB:b + (k + 1) * SUB] for k in range(nv))
                pieces += [jnp.sum(u[r:r + spread_of], axis=0, keepdims=True)
                           for r in range(0, SUB, spread_of)]
            v = jnp.concatenate(pieces, axis=0)
            turned = [v if l == j else pltpu.roll(v, (j - l) % cz, 1) for l in range(COARSEN)]
            while len(turned) > 1:
                turned = [u + t for u, t in zip(turned[::2], turned[1::2])]
            here = eighth[:v.shape[0]] == j
            total = turned[0] if total is None else jnp.where(here, turned[0], total)
        return total

    def local_terms(i, _):
        spread, strength = spread_ref[i], strength_ref[i]
        st = split(state_ref, i)
        src = split(source_ref, i)
        near = (nb_red(st[1]), nb_black(st[0]))
        mass_sum = jnp.zeros((cy, cz), F32)
        for h in range(2):
            coef = spread * condp[h]
            inv = 1.0 / (1.0 + st[h])
            bound = coverp[h] * strength * inv
            mass = INV_STEP + bound * inv
            dg = mass + 6.0 * coef
            diag[h, i] = dg
            c[h, i] = coef / dg
            a[h, i] = (src[h] - (coef * (6.0 * st[h] - near[h]) + bound * st[h])) / dg
            mass_sum += jnp.sum(mass, axis=0)
        mx[i] = mass_sum
        return 0

    lax.fori_loop(0, ions, local_terms, 0)
    cond_sum = jnp.sum(condp[0] + condp[1], axis=0)
    sums = pack([mx[i] for i in range(ions)] + [spread_ref[i] * cond_sum for i in range(ions)])
    low_slot = eighth[:rows] < ions
    coarse_off = pltpu.roll(sums, cz - ions, 1) / COARSEN
    coarse_inv = 1.0 / jnp.where(low_slot, sums + 6.0 * coarse_off, 1.0)
    ops[w, s] = jnp.where(low_slot, coarse_off * coarse_inv, pltpu.roll(coarse_inv, ions, 1))

    mine = colour_ref[0, 0].astype(F32)

    def sweeps(mask, right, ids):
        coefs = [(c[0, i], c[1, i]) for i in ids]
        red = [mask * ar for ar, _ in right]
        ab = [mask * v for _, v in right]
        ar = list(red)
        black = [v + cc[1] * nb_black(r) for v, cc, r in zip(ab, coefs, red)]
        for _ in range(SWEEPS - 1):
            red = [v + cc[0] * nb_red(u) for v, cc, u in zip(ar, coefs, black)]
            black = [v + cc[1] * nb_black(r) for v, cc, r in zip(ab, coefs, red)]
        return red, black

    def phase_zero(ids):
        for i in ids:
            near = rim(0, i)
            for h in range(2):
                a[h, i] = a[h, i] + c[h, i] * near[h]
        reds, blacks = sweeps(1.0 - mine, [(a[0, i], a[1, i]) for i in ids], ids)
        for i, red, black in zip(ids, reds, blacks):
            d[0, i], d[1, i] = red, black
            put_y(1, i, red, black)
            put_x(1, i, red, black)

    met_by(0, expected)
    expected = meet(1)
    for g in range(GROUPS):
        receive(0, g)
        phase_zero(range(g * pair_of, (g + 1) * pair_of))
        send(1, g)
    met_by(1, expected)
    expected = meet(2)
    for k in range(4):
        @pl.when(has[k])
        def _():
            cond_copy(k).start()
    def phase_one(ids):
        right = []
        for i in ids:
            near = rim(1, i)
            right.append((a[0, i] + c[0, i] * near[0], a[1, i] + c[1, i] * near[1]))
        reds, blacks = sweeps(mine, right, ids)
        for i, red, black in zip(ids, reds, blacks):
            red, black = red + d[0, i], black + d[1, i]
            d[0, i], d[1, i] = red, black
            put_y(2, i, red, black)
            put_x(2, i, red, black)
            fine = diag[0, i] * (a[0, i] + c[0, i] * nb_red(black) - red)
            rhs[0, i] = fine
            still = -mine * (spread_ref[i] * condp[1] * rim(1, i)[1])
            rhs[1, i] = still
            fx[i] = jnp.sum(fine + still, axis=0)

    for g in range(GROUPS):
        receive(1, g)
        if g == GROUPS - 1:
            met_by(2, expected)
            ops_along(1, n_span)
        phase_one(range(g * pair_of, (g + 1) * pair_of))

    for k in range(4):
        @pl.when(gets[k])
        def _():
            cond_copy(k).wait_recv()

    def across(k, i):
        face = ys[2, k, i]
        other = jnp.concatenate([face[kp:], face[:kp]], axis=0)
        return spread_ref[i] * jnp.sum(yhc[1 - k] * other, axis=0, keepdims=True)

    def column(i):
        spread = spread_ref[i]
        y_part = jnp.where(first_y, across(1, i), jnp.where(last_y, across(0, i), 0.0))
        return (jnp.concatenate([fx[i], spread * (rows_of(xhc, 0) * xs[1, 1, i])], axis=0),
                jnp.concatenate([spread * (rows_of(xhc, 1) * xs[1, 0, i]), y_part], axis=0))

    columns = [column(i) for i in range(ions)]
    gath[me] = pack([u for u, _ in columns] + [v for _, v in columns])
    to_all(gath, gsend, grecv)
    for g in range(GROUPS):
        send(2, g)
    ops_column(orecv.at[0])
    for k in range(1, n_width):
        ops_across(k).start()

    wide = n_width * rows
    half = n_span // 2

    crow = lax.broadcasted_iota(jnp.int32, (wide, cz), 0)
    slot_low = lax.broadcasted_iota(jnp.int32, (wide, cz), 1) % COARSEN < ions

    def wide_of(v):
        return jnp.concatenate([v[:, k] for k in range(n_width)], axis=1)

    def down(v):
        return pltpu.roll(v, cz - ions, 2)

    def up(v):
        return pltpu.roll(v, ions, 2)

    def fold(low_part, high_part):
        return jnp.where(slot_low, low_part, high_part)

    plane = jnp.zeros((1, wide, cz), F32)
    for k in range(1, n_width):
        ops_across(k).wait_recv()
    o = jnp.concatenate([ops[k] for k in range(n_width)], axis=1)
    aj[...] = fold(down(o[:half]), o[half:])
    cj[...] = fold(o[:half], up(o[half:]))
    all_of(gath, grecv)
    g = gath[...].reshape(n_span, n_width, 2 * rows, cz)
    plus, minus = wide_of(g[:, :, :rows]), wide_of(g[:, :, rows:])
    y_sum = jnp.where(crow % rows == 0, pltpu.roll(minus, 1, 1), 0.0)
    y_sum = jnp.where(crow % rows == rows - 1, pltpu.roll(minus, wide - 1, 1), y_sum)
    crhs = fold(plus[:half], up(plus[half:]))
    crhs += fold(jnp.concatenate([plane, down(plus[:half - 1])], axis=0), plus[half - 1:-1])
    crhs += fold(minus[1:half + 1], jnp.concatenate([up(minus[half + 1:]), plane], axis=0))
    crhs += fold(down(y_sum[:half]), y_sum[half:])
    aj[...] = crhs * aj[...]
    crow = lax.broadcasted_iota(jnp.int32, (wide, cz), 0)
    clane = lax.broadcasted_iota(jnp.int32, (wide, cz), 1)

    y_plus = jnp.where(crow == wide - 1, 0.0, cj[...])
    y_minus = jnp.where(crow == 0, 0.0, cj[...])
    z_plus = jnp.where(clane >= cz - COARSEN, 0.0, cj[...])
    z_minus = jnp.where(clane < COARSEN, 0.0, cj[...])

    def jacobi(_, e):
        above = jnp.where(slot_low, up_one(e[:1], -1), 0.0)
        below = jnp.where(slot_low, 0.0, up_one(e[half - 1:], 1))
        near = jnp.concatenate([e[1:], above], axis=0) + jnp.concatenate([below, e[:-1]], axis=0)
        total = aj[...] + cj[...] * near
        total += y_plus * pltpu.roll(e, wide - 1, 1) + y_minus * pltpu.roll(e, 1, 1)
        return total + (z_plus * pltpu.roll(e, cz - COARSEN, 2) + z_minus * pltpu.roll(e, COARSEN, 2))

    def up_one(v, sign):
        return pltpu.roll(v, ions if sign > 0 else cz - ions, 2)

    e = lax.fori_loop(0, COARSE_ITERS - 1, jacobi, aj[...], unroll=UNROLL_J)
    ej[0] = plane[0]
    ej[n_span + 1] = plane[0]
    ej[1:half + 1] = e
    ej[half + 1:n_span + 1] = down(e)
    def face_terms(i, _):
        near = rim(2, i)
        for h in range(2):
            rhs[h, i] += spread_ref[i] * condp[h] * near[h]
        return 0

    for g in range(GROUPS):
        receive(2, g)
    lax.fori_loop(0, ions, face_terms, 0)
    before, here, after = ej[s], ej[s + 1], ej[s + 2]

    def own_rows(v):
        out = v[:rows]
        for k in range(1, n_width):
            out = jnp.where(w == k, v[k * rows:(k + 1) * rows], out)
        return out

    y_low = jnp.zeros((1, cz), F32)
    y_high = jnp.zeros((1, cz), F32)
    for k in range(n_width):
        if k > 0:
            y_low = jnp.where(w == k, here[k * rows - 1:k * rows], y_low)
        if k < n_width - 1:
            y_high = jnp.where(w == k, here[(k + 1) * rows:(k + 1) * rows + 1], y_high)
    packed = jnp.concatenate(
        [own_rows(here), own_rows(before), own_rows(after), y_low, y_high,
         jnp.zeros((16 - 3 * rows - 2, cz), F32)], axis=0)
    for i in range(ions):
        v = jnp.where(eighth[:16] == i, packed, 0.0)
        turned = [v if l == i else pltpu.roll(v, (l - i) % cz, 1) for l in range(COARSEN)]
        while len(turned) > 1:
            turned = [u + t for u, t in zip(turned[::2], turned[1::2])]
        sp[i] = turned[0]

    def tall(v):
        return jnp.concatenate(
            [jnp.broadcast_to(v[j:j + 1], (spread_of, cz)) for j in range(rows)] * nv, axis=0)

    sums = []
    for i in range(ions):
        v = sp[i]
        lift = tall(v[:rows])
        lo, hi = tall(v[rows:2 * rows]), tall(v[2 * rows:3 * rows])
        base = yz_sum(lift) + lift
        base += jnp.where(first_y, v[3 * rows:3 * rows + 1], 0.0)
        base += jnp.where(last_y, v[3 * rows + 1:3 * rows + 2], 0.0)
        numer = jnp.zeros((cy, cz), F32)
        denom = jnp.zeros((cy, cz), F32)
        for h in range(2):
            for k in range(kp):
                side = lift
                low_side = p if h else jnp.logical_not(p)
                high_side = jnp.logical_not(p) if h else p
                if k == 0:
                    side = jnp.where(low_side, lo, side)
                if k == kp - 1:
                    side = jnp.where(high_side, hi, side)
                im = diag[h, i, k] * lift - spread_ref[i] * condp[h, k] * (base + side)
                image[h, i, k] = im
                numer += rhs[h, i, k] * im
                denom += im * im
        sums.append((jnp.sum(numer, axis=0, keepdims=True), jnp.sum(denom, axis=0, keepdims=True)))
    moments = jnp.concatenate([n for n, _ in sums] + [m for _, m in sums], axis=0)
    moments = jnp.sum(moments, axis=1, keepdims=True)
    share = cz // ions
    prow = lax.broadcasted_iota(jnp.int32, (ions, cz), 0)
    mine_of = prow == lax.broadcasted_iota(jnp.int32, (ions, cz), 1) // share
    part[me] = jnp.concatenate(
        [jnp.sum(jnp.where(mine_of, v, 0.0), axis=0, keepdims=True)
         for v in (moments[:ions], moments[ions:])], axis=0)
    to_all(part, psend, precv)

    def put(ref, i, x, value, add=None):
        for v in range(nv):
            at = (i, x, pl.ds(v, SUB, stride=nv), slice(None))
            piece = value[v * SUB:(v + 1) * SUB]
            ref[at] = piece if add is None else add[at] + piece

    def to_rows(i, _):
        for k in range(kp):
            for out, red, black, add in (
                    (up_ref, d[0, i, k], d[1, i, k], state_ref),
                    (res_ref, rhs[0, i, k], rhs[1, i, k], None),
                    (source_ref, image[0, i, k], image[1, i, k], None)):
                put(out, i, 2 * k, jnp.where(p, black, red), add)
                put(out, i, 2 * k + 1, jnp.where(p, red, black), add)
        return 0

    lax.fori_loop(0, ions, to_rows, 0)
    all_of(part, precv)
    whole = jnp.sum(part[...], axis=0)
    weight = whole[:1] / (whole[1:] + EPSILON)
    for i in range(ions):
        wv[i:i + 1] = jnp.broadcast_to(weight[:, i * share:i * share + 1], (1, cz))

    for i in range(ions):
        wt = wv[i:i + 1]
        lifted = wt * jnp.concatenate(
            [jnp.broadcast_to(sp[i, j:j + 1], (COARSEN, cz)) for j in range(rows)], axis=0)
        up_ref[i] = up_ref[i] + lifted
        res_ref[i] = res_ref[i] - wt * source_ref[i]

    for e in range(3):
        for k in range(4):
            @pl.when(has[k])
            def _():
                for g in range(GROUPS):
                    copy(e, k, g).wait_send()
    for k in range(4):
        @pl.when(has[k])
        def _():
            cond_copy(k).wait_send()
    ops_column(osend.at[0])
    for k in range(1, n_width):
        ops_across(k).wait_send()
    all_of(gath, gsend)
    all_of(part, psend)


def drain(up_ref, res_ref, up_out, res_out, sem):
    copies = [pltpu.make_async_copy(up_ref, up_out, sem.at[0]),
              pltpu.make_async_copy(res_ref, res_out, sem.at[1])]
    for one in copies:
        one.start()
    for one in copies:
        one.wait()


def on_device(n_span, n_width, state, source, conductance, rebar_cover, colour, diffusivity, binding):
    ions, cx, cy, cz = state.shape
    kp = cx // 2
    rows = cy // COARSEN
    half = pltpu.VMEM((2, ions, kp, cy, cz), F32)
    pair = pltpu.VMEM((2, kp, cy, cz), F32)
    vmem = pl.BlockSpec(memory_space=pltpu.VMEM)
    dma = pltpu.SemaphoreType.DMA
    anywhere = pl.BlockSpec(memory_space=pl.ANY)
    hbm = pl.BlockSpec(memory_space=pltpu.HBM)
    face_x = pltpu.VMEM((3, 2, ions, cy, cz), F32)
    face_y = pltpu.VMEM((3, 2, ions, 2 * kp, cz), F32)
    everyone = n_span * n_width
    up, res = pl.pallas_call(
        functools.partial(kernel, n_span, n_width, ions, cx, cy, cz),
        out_shape=(pltpu.VMEM(state.shape, F32),) * 2,
        in_specs=[pl.BlockSpec(memory_space=pltpu.HBM)] * 7,
        out_specs=(vmem, vmem),
        scratch_shapes=[
            pltpu.SMEM((1, 1), jnp.int32), pltpu.SMEM((ions,), F32), pltpu.SMEM((ions,), F32),
            pltpu.VMEM(state.shape, F32), pltpu.VMEM(state.shape, F32),
            pltpu.VMEM(conductance.shape, F32), pltpu.VMEM(conductance.shape, jnp.int32),
            pltpu.VMEM((2, 2, ions, cy, cz), F32), face_x, face_y, face_y,
            pltpu.VMEM((2, 2 * kp, cz), F32),
            pltpu.VMEM((2, cy, cz), F32),
            pltpu.VMEM((2, 2 * kp, cz), F32),
            pltpu.VMEM((n_width, n_span, rows, cz), F32),
            pltpu.VMEM((everyone, 2 * rows, cz), F32),
            pltpu.VMEM((everyone, 2, cz), F32),
            pair, pair, half, half, half, half, half, half,
            pltpu.VMEM((ions, cy, cz), F32),
            pltpu.VMEM((ions, cy, cz), F32),
            pltpu.VMEM((n_span // 2, n_width * rows, cz), F32),
            pltpu.VMEM((n_span // 2, n_width * rows, cz), F32),
            pltpu.VMEM((n_span + 2, n_width * rows, cz), F32),
            pltpu.VMEM((ions, 16, cz), F32),
            pltpu.VMEM((ions, cz), F32),
            dma((3, 4, GROUPS)), dma((3, 4, GROUPS)), dma((4,)), dma((4,)),
            dma((n_width,)), dma((n_width,)), dma, dma, dma, dma, dma((7,)), pltpu.SemaphoreType.REGULAR((3,)),
        ],
        compiler_params=pltpu.CompilerParams(
            collective_id=0, has_side_effects=True, vmem_limit_bytes=60 * 1024 * 1024
        ),
    )(state, source, conductance, rebar_cover, colour, diffusivity, binding)
    return pl.pallas_call(
        drain,
        out_shape=(jax.ShapeDtypeStruct(state.shape, F32),) * 2,
        in_specs=[anywhere] * 2,
        out_specs=(hbm, hbm),
        scratch_shapes=[dma((2,))],
        compiler_params=pltpu.CompilerParams(vmem_limit_bytes=1024 * 1024),
    )(up, res)


def solution(mesh):
    in_specs = (
        P(None, "span", "width", None),
        P(None, "span", "width", None),
        P("span", "width", None),
        P("span", "width", None),
        P("span", "width"),
        P(),
        P(),
    )
    out_specs = (P(None, "span", "width", None), P(None, "span", "width", None))
    return jax.shard_map(
        functools.partial(on_device, mesh.shape["span"], mesh.shape["width"]),
        mesh=mesh, in_specs=in_specs, out_specs=out_specs, check_vma=False,
    )
```

```python
import functools

import jax
import jax.numpy as jnp
from jax import lax
from jax.experimental import pallas as pl
from jax.experimental.pallas import tpu as pltpu
from jax.sharding import PartitionSpec as P

COARSEN = 8
SUB = 8
SWEEPS = 4
COARSE_ITERS = 20
INV_STEP = 0.05
EPSILON = 1e-06
MESH = pl.DeviceIdType.MESH
GROUPS = 2
UNROLL_J = 19
F32 = jnp.float32


def kernel(
    n_span, n_width, ions, cx, cy, cz,
    state_hbm, source_hbm, cond_hbm, cover_hbm, colour_hbm, spread_hbm, strength_hbm,
    up_ref, res_ref,
    colour_ref, spread_ref, strength_ref, state_ref, source_ref, cond_ref, cover_ref, xs, xh, ys, yh, ysc, xhc, yhc, ops, gath, part, condp, coverp, rhs, diag, c, a, d, image,
    mx, fx, aj, cj, ej, sp, wv,
    send_sem, recv_sem, csend, crecv, osend, orecv, gsend, grecv, psend, precv, in_sem, met,
):
    s = lax.axis_index("span")
    w = lax.axis_index("width")
    kp = cx // 2
    rows = cy // COARSEN
    nv = cy // SUB
    spread_of = SUB // rows
    slot = lax.broadcasted_iota(jnp.int32, (cy, cz), 0)
    row = slot % SUB * nv + slot // SUB
    lane = lax.broadcasted_iota(jnp.int32, (cy, cz), 1)
    p = (row + lane) % 2 == 1
    first_y, last_y = row == 0, row == cy - 1
    first_z, last_z = lane == 0, lane == cz - 1

    loads = [
        pltpu.make_async_copy(src, dst, in_sem.at[k])
        for k, (src, dst) in enumerate((
            (state_hbm, state_ref), (cond_hbm, cond_ref),
            (cover_hbm, cover_ref), (source_hbm, source_ref),
            (colour_hbm, colour_ref), (spread_hbm, spread_ref), (strength_hbm, strength_ref)))
    ]
    for load in loads:
        load.start()

    barrier = pltpu.get_barrier_semaphore()

    has = (s < n_span - 1, s > 0, w < n_width - 1, w > 0)
    gets = (s > 0, s < n_span - 1, w > 0, w < n_width - 1)
    to = ((s + 1, w), (s - 1, w), (s, w + 1), (s, w - 1))

    def flip(v, bit):
        return v + bit - 2 * bit * (v // bit % 2)

    def signal(sem, moves):
        count = 0
        for ok, t, v in moves:
            @pl.when(ok)
            def _():
                pl.semaphore_signal(sem, inc=1, device_id=(t, v), device_id_type=MESH)
            count = count + ok.astype(jnp.int32)
        return count

    quad = 4
    planes = n_span // quad
    everyone = n_span * n_width
    me = s * n_width + w
    partners = [lax.rem(w + k, n_width) for k in range(1, n_width)]
    staged = n_width == 2 and 2 <= planes <= 4
    if staged:
        z = s // quad

        def shifted(by):
            return (z + by >= 0) & (z + by < planes), s + by * quad

        def pairs(*moves):
            return [shifted(by) + (v,) for by, v in moves]

        always = s >= 0
        greet = [(always, s, 1 - w), (always, flip(s, 1), w), (always, flip(s, 2), w)]
        greet += pairs((1, w), (-1, w))
        greet += [((s % 2 == 1) & (s < n_span - 1), s + 1, w), ((s % 2 == 0) & (s > 0), s - 1, w)]
        rounds = [
            [(always, s, 1 - w), (always, flip(s, 1), w)],
            [(always, flip(s, 2), w)] + pairs((1, w), (-1, w)),
            [(always, flip(s, 2), w)] + pairs((2, w), (-2, w), (2, 1 - w), (-2, 1 - w)),
        ]
        greeted = signal(barrier, greet)
    else:
        rounds = [[], [], []]
        greeted = everyone - 1

        @pl.loop(1, everyone)
        def _(off):
            other = lax.rem(me + off, everyone)
            pl.semaphore_signal(
                barrier, inc=1, device_id=(other // n_width, other % n_width), device_id_type=MESH)

    def meet(k):
        return signal(met.at[k], rounds[k]) if rounds[k] else 0

    def met_by(k, count):
        if rounds[k]:
            pl.semaphore_wait(met.at[k], count)

    def bits_of(v, count):
        return [((v // b % 2) * b, b - (v // b % 2) * b) for b in (1 << k for k in range(count))]

    def far(off):
        at = off // n_width
        return at // quad + at % quad // 2 + at % 2

    span_bits, width_bits = (n_span - 1).bit_length(), (n_width - 1).bit_length()
    listed = everyone == 1 << (span_bits + width_bits) and everyone <= 64
    span_of, width_of = bits_of(s, span_bits), bits_of(w, width_bits)

    def to_all(buf, ssem, rsem):
        def send_to(t, v):
            pltpu.make_async_remote_copy(
                src_ref=buf.at[me], dst_ref=buf.at[me], send_sem=ssem, recv_sem=rsem,
                device_id=(t, v), device_id_type=MESH,
            ).start()

        if listed:
            for off in sorted(range(1, everyone), key=far, reverse=True):
                at_s, at_w = off // n_width, off % n_width
                send_to(sum(pair[at_s >> k & 1] for k, pair in enumerate(span_of)),
                        sum(pair[at_w >> k & 1] for k, pair in enumerate(width_of)))
        else:
            @pl.loop(1, everyone)
            def _(off):
                other = lax.rem(me + off, everyone)
                send_to(other // n_width, other % n_width)

    def ops_along(first, last):
        for off in sorted(range(first, last), key=lambda k: far(k * n_width), reverse=True):
            t = sum(pair[off >> k & 1] for k, pair in enumerate(span_of)) if listed else lax.rem(s + off, n_span)
            pltpu.make_async_remote_copy(
                src_ref=ops.at[w, s], dst_ref=ops.at[w, s], send_sem=osend.at[0], recv_sem=orecv.at[0],
                device_id=(t, w), device_id_type=MESH,
            ).start()

    def ops_across(k):
        return pltpu.make_async_remote_copy(
            src_ref=ops.at[w], dst_ref=ops.at[w], send_sem=osend.at[k], recv_sem=orecv.at[k],
            device_id=(s, partners[k - 1]), device_id_type=MESH,
        )

    def ops_column(sem):
        others = ops.at[w, pl.ds(0, n_span - 1)]
        pltpu.make_async_copy(others, others, sem).wait()

    def all_of(buf, sem):
        others = buf.at[pl.ds(0, everyone - 1)]
        pltpu.make_async_copy(others, others, sem).wait()

    def rows_of(ref, *at):
        return jnp.concatenate(
            [ref[at + (pl.ds(v, SUB, stride=nv), slice(None))] for v in range(nv)], axis=-2)

    def split(ref, *at):
        pairs = rows_of(ref, *at, slice(None)).reshape(kp, 2, cy, cz)
        even, odd = pairs[:, 0], pairs[:, 1]
        return jnp.where(p, odd, even), jnp.where(p, even, odd)

    def y_up(v):
        edge = jnp.where(last_y[cy - SUB:], 0.0, pltpu.roll(v[..., :SUB, :], SUB - 1, v.ndim - 2))
        return jnp.concatenate([v[..., SUB:, :], edge], axis=-2)

    def y_down(v):
        edge = jnp.where(first_y[:SUB], 0.0, pltpu.roll(v[..., cy - SUB:, :], 1, v.ndim - 2))
        return jnp.concatenate([edge, v[..., :cy - SUB, :]], axis=-2)

    def z_sum(v):
        return (jnp.where(last_z, 0.0, pltpu.roll(v, cz - 1, v.ndim - 1))
                + jnp.where(first_z, 0.0, pltpu.roll(v, 1, v.ndim - 1)))

    def yz_sum(v):
        return (y_up(v) + y_down(v)) + z_sum(v)

    zero_face = jnp.zeros((1, cy, cz), F32)

    def nb_red(black):
        above = jnp.concatenate([black[1:], zero_face], axis=0)
        below = jnp.concatenate([zero_face, black[:-1]], axis=0)
        return (black + jnp.where(p, above, below) + (y_up(black) + y_down(black))) + z_sum(black)

    def nb_black(red):
        above = jnp.concatenate([red[1:], zero_face], axis=0)
        below = jnp.concatenate([zero_face, red[:-1]], axis=0)
        return (red + jnp.where(p, below, above) + (y_up(red) + y_down(red))) + z_sum(red)

    def rim(e, i):
        lo, hi = (rows_of(xh, e, k, i) if e == 0 else xh[e, k, i] for k in range(2))
        ylo, yhi = yh[e, 0, i], yh[e, 1, i]
        mid = jnp.zeros((kp - 2, cy, cz), F32)

        def faces(k0, k1, half):
            x_part = jnp.concatenate([k0[None], mid, k1[None]], axis=0)
            low = ylo[half * kp:(half + 1) * kp][:, None, :]
            high = yhi[half * kp:(half + 1) * kp][:, None, :]
            return x_part + jnp.where(first_y, low, 0.0) + jnp.where(last_y, high, 0.0)

        red = faces(jnp.where(p, 0.0, lo), jnp.where(p, hi, 0.0), 1)
        black = faces(jnp.where(p, lo, 0.0), jnp.where(p, 0.0, hi), 0)
        return red, black

    def put_y(e, i, red, black):
        ys[e, 0, i] = jnp.concatenate([red[:, cy - 1, :], black[:, cy - 1, :]], axis=0)
        ys[e, 1, i] = jnp.concatenate([red[:, 0, :], black[:, 0, :]], axis=0)

    def put_x(e, i, red, black):
        xs[e - 1, 0, i] = jnp.where(p, red[kp - 1], black[kp - 1])
        xs[e - 1, 1, i] = jnp.where(p, black[0], red[0])

    pair_of = ions // GROUPS

    def copy(e, k, g):
        own = pl.ds(g * pair_of, pair_of)
        if k >= 2:
            src, dst = ys.at[e, k - 2, own], yh.at[e, k - 2, own]
        else:
            dst = xh.at[e, k, own]
            if e == 0:
                src = state_ref.at[own, cx - 1] if k == 0 else state_ref.at[own, 0]
            else:
                src = xs.at[e - 1, k, own]
        return pltpu.make_async_remote_copy(
            src_ref=src, dst_ref=dst, send_sem=send_sem.at[e, k, g], recv_sem=recv_sem.at[e, k, g],
            device_id=to[k], device_id_type=MESH,
        )

    def cond_copy(k):
        if k >= 2:
            src, dst = ysc.at[k - 2], yhc.at[k - 2]
        else:
            src, dst = cond_ref.at[cx - 1 if k == 0 else 0], xhc.at[k]
        return pltpu.make_async_remote_copy(
            src_ref=src, dst_ref=dst, send_sem=csend.at[k], recv_sem=crecv.at[k],
            device_id=to[k], device_id_type=MESH,
        )

    def send(e, g):
        for k in range(4):
            @pl.when(has[k])
            def _():
                copy(e, k, g).start()

    def receive(e, g):
        for k in range(4):
            @pl.when(gets[k])
            def _():
                copy(e, k, g).wait_recv()

    for k in range(4):
        @pl.when(jnp.logical_not(gets[k]))
        def _():
            for e in range(3):
                if k >= 2:
                    yh[e, k - 2] = jnp.zeros(yh.shape[2:], F32)
                else:
                    xh[e, k] = jnp.zeros(xh.shape[2:], F32)
            if k >= 2:
                yhc[k - 2] = jnp.zeros(yhc.shape[1:], F32)
            else:
                xhc[k] = jnp.zeros(xhc.shape[1:], F32)

    def pack_state(i, _):
        put_y(0, i, *split(state_ref, i))
        return 0

    loads[0].wait()
    lax.fori_loop(0, ions, pack_state, 0)
    pl.semaphore_wait(barrier, greeted)
    for g in range(GROUPS):
        send(0, g)
    expected = meet(0)

    loads[1].wait()
    condp[0], condp[1] = split(cond_ref)
    ysc[0] = jnp.concatenate([condp[0, :, cy - 1, :], condp[1, :, cy - 1, :]], axis=0)
    ysc[1] = jnp.concatenate([condp[0, :, 0, :], condp[1, :, 0, :]], axis=0)
    for load in loads[2:]:
        load.wait()
    coverp[0], coverp[1] = (v.astype(F32) for v in split(cover_ref))

    eighth = lane % COARSEN

    def pack(fields):
        total = None
        for j, v in enumerate(fields):
            pieces = []
            for b in range(0, v.shape[0], cy):
                u = sum(v[b + k * SUB:b + (k + 1) * SUB] for k in range(nv))
                pieces += [jnp.sum(u[r:r + spread_of], axis=0, keepdims=True)
                           for r in range(0, SUB, spread_of)]
            v = jnp.concatenate(pieces, axis=0)
            turned = [v if l == j else pltpu.roll(v, (j - l) % cz, 1) for l in range(COARSEN)]
            while len(turned) > 1:
                turned = [u + t for u, t in zip(turned[::2], turned[1::2])]
            here = eighth[:v.shape[0]] == j
            total = turned[0] if total is None else jnp.where(here, turned[0], total)
        return total

    def local_terms(i, _):
        spread, strength = spread_ref[i], strength_ref[i]
        st = split(state_ref, i)
        src = split(source_ref, i)
        near = (nb_red(st[1]), nb_black(st[0]))
        mass_sum = jnp.zeros((cy, cz), F32)
        for h in range(2):
            coef = spread * condp[h]
            inv = 1.0 / (1.0 + st[h])
            bound = coverp[h] * strength * inv
            mass = INV_STEP + bound * inv
            dg = mass + 6.0 * coef
            diag[h, i] = dg
            c[h, i] = coef / dg
            a[h, i] = (src[h] - (coef * (6.0 * st[h] - near[h]) + bound * st[h])) / dg
            mass_sum += jnp.sum(mass, axis=0)
        mx[i] = mass_sum
        return 0

    lax.fori_loop(0, ions, local_terms, 0)
    cond_sum = jnp.sum(condp[0] + condp[1], axis=0)
    sums = pack([mx[i] for i in range(ions)] + [spread_ref[i] * cond_sum for i in range(ions)])
    low_slot = eighth[:rows] < ions
    coarse_off = pltpu.roll(sums, cz - ions, 1) / COARSEN
    coarse_inv = 1.0 / jnp.where(low_slot, sums + 6.0 * coarse_off, 1.0)
    ops[w, s] = jnp.where(low_slot, coarse_off * coarse_inv, pltpu.roll(coarse_inv, ions, 1))

    mine = colour_ref[0, 0].astype(F32)

    def sweeps(mask, right, ids):
        coefs = [(c[0, i], c[1, i]) for i in ids]
        red = [mask * ar for ar, _ in right]
        ab = [mask * v for _, v in right]
        ar = list(red)
        black = [v + cc[1] * nb_black(r) for v, cc, r in zip(ab, coefs, red)]
        for _ in range(SWEEPS - 1):
            red = [v + cc[0] * nb_red(u) for v, cc, u in zip(ar, coefs, black)]
            black = [v + cc[1] * nb_black(r) for v, cc, r in zip(ab, coefs, red)]
        return red, black

    def phase_zero(ids):
        for i in ids:
            near = rim(0, i)
            for h in range(2):
                a[h, i] = a[h, i] + c[h, i] * near[h]
        reds, blacks = sweeps(1.0 - mine, [(a[0, i], a[1, i]) for i in ids], ids)
        for i, red, black in zip(ids, reds, blacks):
            d[0, i], d[1, i] = red, black
            put_y(1, i, red, black)
            put_x(1, i, red, black)

    met_by(0, expected)
    expected = meet(1)
    for g in range(GROUPS):
        receive(0, g)
        phase_zero(range(g * pair_of, (g + 1) * pair_of))
        send(1, g)
    met_by(1, expected)
    expected = meet(2)
    for k in range(4):
        @pl.when(has[k])
        def _():
            cond_copy(k).start()
    def phase_one(ids):
        right = []
        for i in ids:
            near = rim(1, i)
            right.append((a[0, i] + c[0, i] * near[0], a[1, i] + c[1, i] * near[1]))
        reds, blacks = sweeps(mine, right, ids)
        for i, red, black in zip(ids, reds, blacks):
            red, black = red + d[0, i], black + d[1, i]
            d[0, i], d[1, i] = red, black
            put_y(2, i, red, black)
            put_x(2, i, red, black)
            fine = diag[0, i] * (a[0, i] + c[0, i] * nb_red(black) - red)
            rhs[0, i] = fine
            still = -mine * (spread_ref[i] * condp[1] * rim(1, i)[1])
            rhs[1, i] = still
            fx[i] = jnp.sum(fine + still, axis=0)

    for g in range(GROUPS):
        receive(1, g)
        if g == GROUPS - 1:
            met_by(2, expected)
            ops_along(1, n_span)
        phase_one(range(g * pair_of, (g + 1) * pair_of))

    for k in range(4):
        @pl.when(gets[k])
        def _():
            cond_copy(k).wait_recv()

    def across(k, i):
        face = ys[2, k, i]
        other = jnp.concatenate([face[kp:], face[:kp]], axis=0)
        return spread_ref[i] * jnp.sum(yhc[1 - k] * other, axis=0, keepdims=True)

    def column(i):
        spread = spread_ref[i]
        y_part = jnp.where(first_y, across(1, i), jnp.where(last_y, across(0, i), 0.0))
        return (jnp.concatenate([fx[i], spread * (rows_of(xhc, 0) * xs[1, 1, i])], axis=0),
                jnp.concatenate([spread * (rows_of(xhc, 1) * xs[1, 0, i]), y_part], axis=0))

    columns = [column(i) for i in range(ions)]
    gath[me] = pack([u for u, _ in columns] + [v for _, v in columns])
    to_all(gath, gsend, grecv)
    for g in range(GROUPS):
        send(2, g)
    ops_column(orecv.at[0])
    for k in range(1, n_width):
        ops_across(k).start()

    wide = n_width * rows
    half = n_span // 2

    crow = lax.broadcasted_iota(jnp.int32, (wide, cz), 0)
    slot_low = lax.broadcasted_iota(jnp.int32, (wide, cz), 1) % COARSEN < ions

    def wide_of(v):
        return jnp.concatenate([v[:, k] for k in range(n_width)], axis=1)

    def down(v):
        return pltpu.roll(v, cz - ions, 2)

    def up(v):
        return pltpu.roll(v, ions, 2)

    def fold(low_part, high_part):
        return jnp.where(slot_low, low_part, high_part)

    plane = jnp.zeros((1, wide, cz), F32)
    for k in range(1, n_width):
        ops_across(k).wait_recv()
    o = jnp.concatenate([ops[k] for k in range(n_width)], axis=1)
    aj[...] = fold(down(o[:half]), o[half:])
    cj[...] = fold(o[:half], up(o[half:]))
    all_of(gath, grecv)
    g = gath[...].reshape(n_span, n_width, 2 * rows, cz)
    plus, minus = wide_of(g[:, :, :rows]), wide_of(g[:, :, rows:])
    y_sum = jnp.where(crow % rows == 0, pltpu.roll(minus, 1, 1), 0.0)
    y_sum = jnp.where(crow % rows == rows - 1, pltpu.roll(minus, wide - 1, 1), y_sum)
    crhs = fold(plus[:half], up(plus[half:]))
    crhs += fold(jnp.concatenate([plane, down(plus[:half - 1])], axis=0), plus[half - 1:-1])
    crhs += fold(minus[1:half + 1], jnp.concatenate([up(minus[half + 1:]), plane], axis=0))
    crhs += fold(down(y_sum[:half]), y_sum[half:])
    aj[...] = crhs * aj[...]
    crow = lax.broadcasted_iota(jnp.int32, (wide, cz), 0)
    clane = lax.broadcasted_iota(jnp.int32, (wide, cz), 1)

    y_plus = jnp.where(crow == wide - 1, 0.0, cj[...])
    y_minus = jnp.where(crow == 0, 0.0, cj[...])
    z_plus = jnp.where(clane >= cz - COARSEN, 0.0, cj[...])
    z_minus = jnp.where(clane < COARSEN, 0.0, cj[...])

    def jacobi(_, e):
        above = jnp.where(slot_low, up_one(e[:1], -1), 0.0)
        below = jnp.where(slot_low, 0.0, up_one(e[half - 1:], 1))
        near = jnp.concatenate([e[1:], above], axis=0) + jnp.concatenate([below, e[:-1]], axis=0)
        total = aj[...] + cj[...] * near
        total += y_plus * pltpu.roll(e, wide - 1, 1) + y_minus * pltpu.roll(e, 1, 1)
        return total + (z_plus * pltpu.roll(e, cz - COARSEN, 2) + z_minus * pltpu.roll(e, COARSEN, 2))

    def up_one(v, sign):
        return pltpu.roll(v, ions if sign > 0 else cz - ions, 2)

    e = lax.fori_loop(0, COARSE_ITERS - 1, jacobi, aj[...], unroll=UNROLL_J)
    ej[0] = plane[0]
    ej[n_span + 1] = plane[0]
    ej[1:half + 1] = e
    ej[half + 1:n_span + 1] = down(e)
    def face_terms(i, _):
        near = rim(2, i)
        for h in range(2):
            rhs[h, i] += spread_ref[i] * condp[h] * near[h]
        return 0

    for g in range(GROUPS):
        receive(2, g)
    lax.fori_loop(0, ions, face_terms, 0)
    before, here, after = ej[s], ej[s + 1], ej[s + 2]

    def own_rows(v):
        out = v[:rows]
        for k in range(1, n_width):
            out = jnp.where(w == k, v[k * rows:(k + 1) * rows], out)
        return out

    y_low = jnp.zeros((1, cz), F32)
    y_high = jnp.zeros((1, cz), F32)
    for k in range(n_width):
        if k > 0:
            y_low = jnp.where(w == k, here[k * rows - 1:k * rows], y_low)
        if k < n_width - 1:
            y_high = jnp.where(w == k, here[(k + 1) * rows:(k + 1) * rows + 1], y_high)
    packed = jnp.concatenate(
        [own_rows(here), own_rows(before), own_rows(after), y_low, y_high,
         jnp.zeros((16 - 3 * rows - 2, cz), F32)], axis=0)
    for i in range(ions):
        v = jnp.where(eighth[:16] == i, packed, 0.0)
        turned = [v if l == i else pltpu.roll(v, (l - i) % cz, 1) for l in range(COARSEN)]
        while len(turned) > 1:
            turned = [u + t for u, t in zip(turned[::2], turned[1::2])]
        sp[i] = turned[0]

    def tall(v):
        return jnp.concatenate(
            [jnp.broadcast_to(v[j:j + 1], (spread_of, cz)) for j in range(rows)] * nv, axis=0)

    sums = []
    for i in range(ions):
        v = sp[i]
        lift = tall(v[:rows])
        lo, hi = tall(v[rows:2 * rows]), tall(v[2 * rows:3 * rows])
        base = yz_sum(lift) + lift
        base += jnp.where(first_y, v[3 * rows:3 * rows + 1], 0.0)
        base += jnp.where(last_y, v[3 * rows + 1:3 * rows + 2], 0.0)
        numer = jnp.zeros((cy, cz), F32)
        denom = jnp.zeros((cy, cz), F32)
        for h in range(2):
            for k in range(kp):
                side = lift
                low_side = p if h else jnp.logical_not(p)
                high_side = jnp.logical_not(p) if h else p
                if k == 0:
                    side = jnp.where(low_side, lo, side)
                if k == kp - 1:
                    side = jnp.where(high_side, hi, side)
                im = diag[h, i, k] * lift - spread_ref[i] * condp[h, k] * (base + side)
                image[h, i, k] = im
                numer += rhs[h, i, k] * im
                denom += im * im
        sums.append((jnp.sum(numer, axis=0, keepdims=True), jnp.sum(denom, axis=0, keepdims=True)))
    moments = jnp.concatenate([n for n, _ in sums] + [m for _, m in sums], axis=0)
    moments = jnp.sum(moments, axis=1, keepdims=True)
    share = cz // ions
    prow = lax.broadcasted_iota(jnp.int32, (ions, cz), 0)
    mine_of = prow == lax.broadcasted_iota(jnp.int32, (ions, cz), 1) // share
    part[me] = jnp.concatenate(
        [jnp.sum(jnp.where(mine_of, v, 0.0), axis=0, keepdims=True)
         for v in (moments[:ions], moments[ions:])], axis=0)
    to_all(part, psend, precv)

    def put(ref, i, x, value, add=None):
        for v in range(nv):
            at = (i, x, pl.ds(v, SUB, stride=nv), slice(None))
            piece = value[v * SUB:(v + 1) * SUB]
            ref[at] = piece if add is None else add[at] + piece

    def to_rows(i, _):
        for k in range(kp):
            for out, red, black, add in (
                    (up_ref, d[0, i, k], d[1, i, k], state_ref),
                    (res_ref, rhs[0, i, k], rhs[1, i, k], None),
                    (source_ref, image[0, i, k], image[1, i, k], None)):
                put(out, i, 2 * k, jnp.where(p, black, red), add)
                put(out, i, 2 * k + 1, jnp.where(p, red, black), add)
        return 0

    lax.fori_loop(0, ions, to_rows, 0)
    for e in range(3):
        for k in range(4):
            @pl.when(has[k])
            def _():
                for g in range(GROUPS):
                    copy(e, k, g).wait_send()
    for k in range(4):
        @pl.when(has[k])
        def _():
            cond_copy(k).wait_send()
    ops_column(osend.at[0])
    for k in range(1, n_width):
        ops_across(k).wait_send()
    all_of(gath, gsend)
    all_of(part, precv)
    whole = jnp.sum(part[...], axis=0)
    weight = whole[:1] / (whole[1:] + EPSILON)
    for i in range(ions):
        wv[i:i + 1] = jnp.broadcast_to(weight[:, i * share:i * share + 1], (1, cz))

    for i in range(ions):
        wt = wv[i:i + 1]
        lifted = wt * jnp.concatenate(
            [jnp.broadcast_to(sp[i, j:j + 1], (COARSEN, cz)) for j in range(rows)], axis=0)
        up_ref[i] = up_ref[i] + lifted
        res_ref[i] = res_ref[i] - wt * source_ref[i]

    all_of(part, psend)


def drain(up_ref, res_ref, up_out, res_out, sem):
    copies = [pltpu.make_async_copy(up_ref, up_out, sem.at[0]),
              pltpu.make_async_copy(res_ref, res_out, sem.at[1])]
    for one in copies:
        one.start()
    for one in copies:
        one.wait()


def on_device(n_span, n_width, state, source, conductance, rebar_cover, colour, diffusivity, binding):
    ions, cx, cy, cz = state.shape
    kp = cx // 2
    rows = cy // COARSEN
    half = pltpu.VMEM((2, ions, kp, cy, cz), F32)
    pair = pltpu.VMEM((2, kp, cy, cz), F32)
    vmem = pl.BlockSpec(memory_space=pltpu.VMEM)
    dma = pltpu.SemaphoreType.DMA
    anywhere = pl.BlockSpec(memory_space=pl.ANY)
    hbm = pl.BlockSpec(memory_space=pltpu.HBM)
    face_x = pltpu.VMEM((3, 2, ions, cy, cz), F32)
    face_y = pltpu.VMEM((3, 2, ions, 2 * kp, cz), F32)
    everyone = n_span * n_width
    up, res = pl.pallas_call(
        functools.partial(kernel, n_span, n_width, ions, cx, cy, cz),
        out_shape=(pltpu.VMEM(state.shape, F32),) * 2,
        in_specs=[pl.BlockSpec(memory_space=pltpu.HBM)] * 7,
        out_specs=(vmem, vmem),
        scratch_shapes=[
            pltpu.SMEM((1, 1), jnp.int32), pltpu.SMEM((ions,), F32), pltpu.SMEM((ions,), F32),
            pltpu.VMEM(state.shape, F32), pltpu.VMEM(state.shape, F32),
            pltpu.VMEM(conductance.shape, F32), pltpu.VMEM(conductance.shape, jnp.int32),
            pltpu.VMEM((2, 2, ions, cy, cz), F32), face_x, face_y, face_y,
            pltpu.VMEM((2, 2 * kp, cz), F32),
            pltpu.VMEM((2, cy, cz), F32),
            pltpu.VMEM((2, 2 * kp, cz), F32),
            pltpu.VMEM((n_width, n_span, rows, cz), F32),
            pltpu.VMEM((everyone, 2 * rows, cz), F32),
            pltpu.VMEM((everyone, 2, cz), F32),
            pair, pair, half, half, half, half, half, half,
            pltpu.VMEM((ions, cy, cz), F32),
            pltpu.VMEM((ions, cy, cz), F32),
            pltpu.VMEM((n_span // 2, n_width * rows, cz), F32),
            pltpu.VMEM((n_span // 2, n_width * rows, cz), F32),
            pltpu.VMEM((n_span + 2, n_width * rows, cz), F32),
            pltpu.VMEM((ions, 16, cz), F32),
            pltpu.VMEM((ions, cz), F32),
            dma((3, 4, GROUPS)), dma((3, 4, GROUPS)), dma((4,)), dma((4,)),
            dma((n_width,)), dma((n_width,)), dma, dma, dma, dma, dma((7,)), pltpu.SemaphoreType.REGULAR((3,)),
        ],
        compiler_params=pltpu.CompilerParams(
            collective_id=0, has_side_effects=True, vmem_limit_bytes=60 * 1024 * 1024
        ),
    )(state, source, conductance, rebar_cover, colour, diffusivity, binding)
    return pl.pallas_call(
        drain,
        out_shape=(jax.ShapeDtypeStruct(state.shape, F32),) * 2,
        in_specs=[anywhere] * 2,
        out_specs=(hbm, hbm),
        scratch_shapes=[dma((2,))],
        compiler_params=pltpu.CompilerParams(vmem_limit_bytes=1024 * 1024),
    )(up, res)


def solution(mesh):
    in_specs = (
        P(None, "span", "width", None),
        P(None, "span", "width", None),
        P("span", "width", None),
        P("span", "width", None),
        P("span", "width"),
        P(),
        P(),
    )
    out_specs = (P(None, "span", "width", None), P(None, "span", "width", None))
    return jax.shard_map(
        functools.partial(on_device, mesh.shape["span"], mesh.shape["width"]),
        mesh=mesh, in_specs=in_specs, out_specs=out_specs, check_vma=False,
    )
```
